32 devices in a mesh: parts: 2 (over y), train: 8 (over z, core), layer: 2 (over x), query: 1.
Axes of the slice: x: 2, y: 2, z: 4, core: 2. Of those that a mesh axis runs over, the one named last changes fastest.
Arguments:
- train_grads: bfloat16 [4096, 4, 4096], P(('parts', 'train'), 'layer'), parts along dimension 0, may hold values from -0.046875 to 0.046875
- queries: bfloat16 [4, 1, 128, 4096], P('layer', 'query', 'train'), may hold values from -6 to 6
- left_factor: float32 [4, 64, 64], P('layer'), may hold values from -1 to 2
- right_factor: float32 [4, 64, 64], P('layer'), may hold values from -1 to 2
Outputs:
- scores: float32 [4096, 128], P(('parts', 'train', 'layer'), 'query'), parts along dimension 0
The draws below stay inside these ranges and needn't reach their ends.
There are 2 independent parts, one for each index of `parts`. The reference program is written for one: setup_inputs(seed, part) draws one part's arguments, and reference() takes and returns one part's arrays. A program takes and returns all parts, laid end to end along the dimension named above; an argument that names none is the same for every part. Nothing has to cross between parts.
All inputs are finite; a program needn't handle non-finite values.
Results may differ from the reference program's by a relative error of at most 0.0029.
Values may be sent and summed in bfloat16 or wider, within the bound.
No kernel may reach another device: no remote copies, remote signals or barrier semaphores. Data moves between devices by JAX's collectives and lax.ppermute only.
A program may use at most 128 MiB of HBM per device.

```python
import jax
import jax.numpy as jnp
from jax import lax

PROJ_OUT = 64
PROJ_IN = 64
PROJ = 4096
NTRAIN = 2048
LAYERS = 4
QSETS = 1
QH = 128


def factor_draw(key, width):
    diag_key, off_key = jax.random.split(key)
    diag_part = jax.random.uniform(diag_key, (LAYERS, width), jnp.float32, 0.6, 1.8)
    off_part = 0.06 * jnp.clip(jax.random.normal(off_key, (LAYERS, width, width), jnp.float32), -3.0, 3.0)
    eye = jnp.eye(width, dtype=jnp.float32)
    return off_part * (1.0 - eye) + diag_part[:, :, None] * eye


def draw_left_factor(key, part):
    key = jax.random.fold_in(key, 11)
    return factor_draw(key, PROJ_OUT)


def draw_right_factor(key, part):
    key = jax.random.fold_in(key, 23)
    return factor_draw(key, PROJ_IN)


def block_levels(own_key, dims, cuts, least, high):
    def one(axis_at, shards_of):
        heights = jax.random.uniform(jax.random.fold_in(jax.random.fold_in(own_key, 6), axis_at), (shards_of,), jnp.float32, least / len(cuts), high / len(cuts))
        return jnp.repeat(jnp.exp(heights), dims[axis_at] // shards_of).reshape((-1,) + (1,) * (len(dims) - axis_at - 1))

    level = one(*cuts[0])
    for cut in cuts[1:]:
        level = level * one(*cut)
    return level


def noise(rng, dims, scale, limit, cuts=(), kind=jnp.bfloat16):
    entries = scale * jax.random.normal(rng, dims, jnp.float32)
    if cuts:
        entries = entries * block_levels(rng, dims, cuts, -0.22, 0.18)
    return jnp.clip(entries, -limit, limit).astype(kind)


def setup_inputs(seed: int = 0, part: int = 0) -> dict:
    arg_keys = jax.random.split(jax.random.key(seed), 5)
    part_splits = jax.random.split(jax.random.fold_in(arg_keys[4], part), 5)
    train_grads = noise(part_splits[0], (NTRAIN, LAYERS, PROJ), (LAYERS * PROJ) ** -0.5, 0.046875, ((0, 8), (1, 2)))
    queries = noise(arg_keys[1], (LAYERS, QSETS, QH, PROJ), 1.0, 6.0, ((0, 2), (2, 8)))
    left_factor = draw_left_factor(jax.random.fold_in(arg_keys[4], 71), part)
    right_factor = draw_right_factor(jax.random.fold_in(arg_keys[4], 71), part)
    return dict(train_grads=train_grads, queries=queries, left_factor=left_factor, right_factor=right_factor)


def reference(train_grads, queries, left_factor, right_factor):
    layers = queries.shape[0]
    rows_out = left_factor.shape[1]
    rows_in = right_factor.shape[1]
    flat_queries = queries.reshape(layers, -1, queries.shape[3])
    total = jnp.zeros((train_grads.shape[0], flat_queries.shape[1]), jnp.float32)
    for layer_id in range(layers):
        grid = flat_queries[layer_id].astype(jnp.float32).reshape(-1, rows_out, rows_in)
        left_part = jnp.einsum("ab,nbc->nac", left_factor[layer_id], grid, precision=lax.Precision.HIGHEST)
        both = jnp.einsum("nac,cd->nad", left_part, right_factor[layer_id], precision=lax.Precision.HIGHEST)
        ready = both.reshape(grid.shape[0], -1).astype(jnp.bfloat16)
        total = total + jnp.dot(train_grads[:, layer_id, :], ready.T, preferred_element_type=jnp.float32)
    return total
```

```python
import jax
import jax.numpy as jnp
from jax import lax
from jax.sharding import PartitionSpec as P


def swap_parts(value, parts):
    return lax.ppermute(value, "parts", [(p, (p + 1) % parts) for p in range(parts)])


def gather_blocks(own, parts, pair, columns):
    train = pair * columns

    def along_columns(value, step):
        return lax.ppermute(
            value,
            "train",
            [(k, (k // pair - step) % columns * pair + k % pair) for k in range(train)],
        )

    def along_pair(value):
        return lax.ppermute(value, "train", [(k, k ^ 1) for k in range(train)])

    me = lax.axis_index("parts")
    mine = lax.dynamic_index_in_dim(own, me, 0, keepdims=False)
    got = [along_columns(mine, step) for step in range(1, columns)]
    blocks = [own]
    for piece in got:
        other = swap_parts(piece, parts)
        blocks.append(jnp.where(me == 0, jnp.stack([piece, other]), jnp.stack([other, piece])))
    ordered = []
    for block in blocks:
        ordered.append(block)
        ordered.append(along_pair(block))
    return jnp.concatenate(ordered, axis=1)


def body(shape, train_grads, queries, left_factor, right_factor):
    rows_out = left_factor.shape[1]
    rows_in = right_factor.shape[1]
    own = queries[:, 0]
    layer_count, count, width = own.shape
    grid = own.astype(jnp.float32).reshape(layer_count, count, rows_out, rows_in)
    left_part = jnp.einsum("lab,lnbc->lnac", left_factor, grid, precision=lax.Precision.HIGHEST)
    both = jnp.einsum("lnac,lcd->lnad", left_part, right_factor, precision=lax.Precision.HIGHEST)
    ready = both.reshape(layer_count, count, width).astype(jnp.bfloat16)

    train, parts, layers = shape["train"], shape["parts"], shape["layer"]
    pair = 2
    columns = train // pair
    direct = shape["query"] == 1 and train % pair == 0 and columns <= 4 and parts == layer_count == 2
    if direct:
        block = gather_blocks(ready, parts, pair, columns)
    else:
        block = lax.all_gather(ready, "train", axis=1, tiled=True)

    share = train_grads.shape[0] // layers
    here = lax.axis_index("layer")

    def terms(step):
        rows = lax.dynamic_slice_in_dim(train_grads, (here + step) % layers * share, share, 0)
        return jnp.einsum("fkm,krm->fr", rows, block, preferred_element_type=jnp.float32)

    scores = None
    for step in range(1, layers):
        sent = lax.ppermute(terms(step), "layer", [(k, (k + step) % layers) for k in range(layers)])
        scores = sent if scores is None else scores + sent
    own_terms = terms(0)
    scores = own_terms if scores is None else scores + own_terms
    if direct:
        place = lax.axis_index("train")
        scores = scores.reshape(share, columns, pair, count)
        scores = jnp.roll(scores, place // pair, axis=1)
        scores = jnp.where(place % pair == 0, scores, scores[:, :, ::-1])
        scores = scores.reshape(share, train * count)
    return scores


def solution(mesh):
    shape = dict(mesh.shape)
    return jax.shard_map(
        lambda *arrays: body(shape, *arrays),
        mesh=mesh,
        in_specs=(
            P(("parts", "train"), "layer", None),
            P("layer", "query", "train", None),
            P("layer", None, None),
            P("layer", None, None),
        ),
        out_specs=P(("parts", "train", "layer"), "query"),
        check_vma=False,
    )
```

```python
import functools

import jax
import jax.numpy as jnp
from jax import lax
from jax.experimental import pallas as pl
from jax.experimental.pallas import tpu as pltpu
from jax.sharding import PartitionSpec as P

PAIR = 2
COLUMNS = 4
LANES_LAST = (((1,), (1,)), ((), ()))


def condition(own, left_factor, right_factor):
    layer_count, count, width = own.shape
    rows_out, rows_in = left_factor.shape[1], right_factor.shape[1]
    grid = own.astype(jnp.float32).reshape(layer_count, count, rows_out, rows_in)
    left_part = jnp.einsum("lab,lnbc->lnac", left_factor, grid, precision=lax.Precision.HIGHEST)
    both = jnp.einsum("lnac,lcd->lnad", left_part, right_factor, precision=lax.Precision.HIGHEST)
    return both.reshape(layer_count, count, width).astype(jnp.bfloat16)


def along_columns(value, step):
    pairs = [
        (((k + step) % COLUMNS) * PAIR + c, k * PAIR + c)
        for k in range(COLUMNS)
        for c in range(PAIR)
    ]
    return lax.ppermute(value, "train", pairs)


def relay(value):
    pairs = [(a * PAIR + c, b * PAIR + c) for a, b in ((0, 2), (2, 3), (3, 1), (1, 0)) for c in range(PAIR)]
    return lax.ppermute(value, "train", pairs)


def other_core(value):
    return lax.ppermute(value, "train", [(k, k ^ 1) for k in range(COLUMNS * PAIR)])


def other_part(value):
    return lax.ppermute(value, "parts", [(0, 1), (1, 0)])


def score_kernel(
    train, own, own_c, s1, s1_c, s3, s3_c, y1, y1_c, y3, y3_c, r2, r2_c, d2, d2_c, sent, kept, table, terms
):
    part = lax.axis_index("parts")
    place = lax.axis_index("train")
    here = lax.axis_index("layer")
    column, core = place // PAIR, lax.rem(place, PAIR)
    count = own.shape[1]

    def put(layer, step, twin, block):
        member = lax.rem(column + step, COLUMNS) * PAIR + (1 - core if twin else core)
        table[layer, pl.ds(pl.multiple_of(member * count, count), count), :] = block

    for twin, (a, b, c, d, e, f, g) in enumerate(
        ((own, s1, s3, y1, y3, r2, d2), (own_c, s1_c, s3_c, y1_c, y3_c, r2_c, d2_c))
    ):
        put(0, 0, twin, a[0])
        put(1, 0, twin, a[1])
        put(part, 1, twin, b[...])
        put(part, 3, twin, c[...])
        put(1 - part, 1, twin, d[...])
        put(1 - part, 3, twin, e[...])
        put(part, 2, twin, f[...])
        put(1 - part, 2, twin, g[...])

    rows, layer_count, width = train.shape
    queries = table.shape[1]
    both = lax.dot_general(
        train.reshape(rows * layer_count, width)[...],
        table[...].reshape(layer_count * queries, width),
        LANES_LAST,
        preferred_element_type=jnp.float32,
    )
    for layer in range(layer_count):
        terms[layer] = both[:, layer * queries : (layer + 1) * queries]
    share = kept.shape[0]
    for out, owner in ((sent, 1 - here), (kept, here)):
        first = pl.multiple_of(owner * share * layer_count, share * layer_count)
        out[...] = sum(
            terms[layer, pl.ds(first + layer, share, stride=layer_count), :] for layer in range(layer_count)
        )


def direct(train_grads, queries, left_factor, right_factor):
    own = condition(queries[:, 0], left_factor, right_factor)
    me = lax.axis_index("parts")
    column = lax.axis_index("train") // PAIR
    mine = lax.dynamic_index_in_dim(own, me, 0, keepdims=False)
    theirs = lax.dynamic_index_in_dim(own, 1 - me, 0, keepdims=False)
    s1 = along_columns(mine, 1)
    s3 = along_columns(mine, 3)
    d2 = along_columns(theirs, 2)
    s1, s3 = lax.optimization_barrier((s1, s3))
    passed = jnp.where(column == 1, s1, jnp.where(column == 2, s3, mine))
    r2 = relay(passed)
    d2, r2 = lax.optimization_barrier((d2, r2))
    y1 = other_part(s1)
    y3 = other_part(s3)
    blocks = []
    for block in (own, s1, s3, y1, y3, r2, d2):
        blocks += [block, other_core(block)]

    rows, layer_count, width = train_grads.shape
    total = queries.shape[2] * COLUMNS * PAIR
    share = rows // 2
    spec = pl.BlockSpec(memory_space=pltpu.VMEM)
    flops = 4 * rows * layer_count * width * total
    sent, kept = pl.pallas_call(
        score_kernel,
        out_shape=[jax.ShapeDtypeStruct((share, total), jnp.float32)] * 2,
        in_specs=[spec] * (1 + len(blocks)),
        out_specs=[spec] * 2,
        scratch_shapes=[
            pltpu.VMEM((layer_count, total, width), jnp.bfloat16),
            pltpu.VMEM((layer_count, rows * layer_count, total), jnp.float32),
        ],
        compiler_params=pltpu.CompilerParams(vmem_limit_bytes=24 * 2**20),
        cost_estimate=pl.CostEstimate(flops=flops, bytes_accessed=6 * 2**20, transcendentals=0),
        name="scores",
    )(train_grads, *blocks)
    return kept + lax.ppermute(sent, "layer", [(0, 1), (1, 0)])


def general(shape, train_grads, queries, left_factor, right_factor):
    layers = shape["layer"]
    own = condition(queries[:, 0], left_factor, right_factor)
    block = lax.all_gather(own, "train", axis=1, tiled=True)
    share = train_grads.shape[0] // layers
    here = lax.axis_index("layer")

    def terms(step):
        rows = lax.dynamic_slice_in_dim(train_grads, (here + step) % layers * share, share, 0)
        return jnp.einsum("fkm,krm->fr", rows, block, preferred_element_type=jnp.float32)

    scores = terms(0)
    for step in range(1, layers):
        scores += lax.ppermute(terms(step), "layer", [(k, (k + step) % layers) for k in range(layers)])
    return scores


def body(shape, train_grads, queries, left_factor, right_factor):
    fits = (
        shape["train"] == COLUMNS * PAIR
        and shape["parts"] == shape["layer"] == 2
        and shape["query"] == 1
        and train_grads.shape[0] % 32 == 0
        and train_grads.shape[1:] == (2, 4096)
        and queries.shape[1:] == (1, 16, 4096)
    )
    if fits:
        return direct(train_grads, queries, left_factor, right_factor)
    return general(shape, train_grads, queries, left_factor, right_factor)


def solution(mesh):
    return jax.shard_map(
        functools.partial(body, dict(mesh.shape)),
        mesh=mesh,
        in_specs=(
            P(("parts", "train"), "layer", None),
            P("layer", "query", "train", None),
            P("layer", None, None),
            P("layer", None, None),
        ),
        out_specs=P(("parts", "train", "layer"), "query"),
        check_vma=False,
    )
```

```python
import functools

import jax
import jax.numpy as jnp
from jax import lax
from jax.experimental import pallas as pl
from jax.experimental.pallas import tpu as pltpu
from jax.sharding import PartitionSpec as P

PAIR = 2
COLUMNS = 4
LANES_LAST = (((1,), (1,)), ((), ()))


def condition(own, left_factor, right_factor):
    layer_count, count, width = own.shape
    rows_out, rows_in = left_factor.shape[1], right_factor.shape[1]
    grid = own.astype(jnp.float32).reshape(layer_count, count, rows_out, rows_in)
    left_part = jnp.einsum("lab,lnbc->lnac", left_factor, grid, precision=lax.Precision.HIGHEST)
    both = jnp.einsum("lnac,lcd->lnad", left_part, right_factor, precision=lax.Precision.HIGHEST)
    return both.reshape(layer_count, count, width).astype(jnp.bfloat16)


def along_columns(value, step):
    pairs = [
        (((k + step) % COLUMNS) * PAIR + c, k * PAIR + c)
        for k in range(COLUMNS)
        for c in range(PAIR)
    ]
    return lax.ppermute(value, "train", pairs)


def other_core(value):
    return lax.ppermute(value, "train", [(k, k ^ 1) for k in range(COLUMNS * PAIR)])


def other_part(value):
    return lax.ppermute(value, "parts", [(0, 1), (1, 0)])


def copy_kernel(source, target, done):
    copy = pltpu.make_async_copy(source, target, done)
    copy.start()
    copy.wait()


def copy_near(value):
    return pl.pallas_call(
        copy_kernel,
        out_shape=jax.ShapeDtypeStruct(value.shape, value.dtype),
        in_specs=[pl.BlockSpec(memory_space=pltpu.HBM)],
        out_specs=pl.BlockSpec(memory_space=pltpu.VMEM),
        scratch_shapes=[pltpu.SemaphoreType.DMA],
        compiler_params=pltpu.CompilerParams(vmem_limit_bytes=6 * 2**20),
        cost_estimate=pl.CostEstimate(flops=0, bytes_accessed=2 * value.size * 2, transcendentals=0),
        name="near",
    )(value)


def score_kernel(
    train, own, own_c, s2, s2_c, s1, s1_c, s3, s3_c, y2, y2_c, y1, y1_c, y3, y3_c, sent, kept, table, terms
):
    part = lax.axis_index("parts")
    place = lax.axis_index("train")
    here = lax.axis_index("layer")
    column, core = place // PAIR, lax.rem(place, PAIR)
    count = own.shape[1]

    def put(layer, step, twin, block):
        member = lax.rem(column + step, COLUMNS) * PAIR + (1 - core if twin else core)
        table[layer, pl.ds(pl.multiple_of(member * count, count), count), :] = block

    for twin, (both, here_steps, there_steps) in enumerate(
        ((own, (s1, s2, s3), (y1, y2, y3)), (own_c, (s1_c, s2_c, s3_c), (y1_c, y2_c, y3_c)))
    ):
        put(0, 0, twin, both[0])
        put(1, 0, twin, both[1])
        for step in range(1, COLUMNS):
            put(part, step, twin, here_steps[step - 1][...])
            put(1 - part, step, twin, there_steps[step - 1][...])

    rows, layer_count, width = train.shape
    queries = table.shape[1]
    both = lax.dot_general(
        train.reshape(rows * layer_count, width)[...],
        table[...].reshape(layer_count * queries, width),
        LANES_LAST,
        preferred_element_type=jnp.float32,
    )
    for layer in range(layer_count):
        terms[layer] = both[:, layer * queries : (layer + 1) * queries]
    share = kept.shape[0]
    for out, owner in ((sent, 1 - here), (kept, here)):
        first = pl.multiple_of(owner * share * layer_count, share * layer_count)
        out[...] = sum(
            terms[layer, pl.ds(first + layer, share, stride=layer_count), :] for layer in range(layer_count)
        )


def direct(train_grads, queries, left_factor, right_factor):
    own = condition(queries[:, 0], left_factor, right_factor)
    mine = lax.dynamic_index_in_dim(own, lax.axis_index("parts"), 0, keepdims=False)
    near = copy_near(train_grads)
    s2 = along_columns(mine, 2)
    s1 = along_columns(mine, 1)
    s3 = along_columns(mine, 3)
    y2 = other_part(s2)
    y1 = other_part(s1)
    y3 = other_part(s3)
    blocks = []
    for block in (own, s2, s1, s3, y2, y1, y3):
        blocks += [block, other_core(block)]

    rows, layer_count, width = train_grads.shape
    total = queries.shape[2] * COLUMNS * PAIR
    share = rows // 2
    spec = pl.BlockSpec(memory_space=pltpu.VMEM)
    flops = 4 * rows * layer_count * width * total
    sent, kept = pl.pallas_call(
        score_kernel,
        out_shape=[jax.ShapeDtypeStruct((share, total), jnp.float32)] * 2,
        in_specs=[spec] * (1 + len(blocks)),
        out_specs=[spec] * 2,
        scratch_shapes=[
            pltpu.VMEM((layer_count, total, width), jnp.bfloat16),
            pltpu.VMEM((layer_count, rows * layer_count, total), jnp.float32),
        ],
        compiler_params=pltpu.CompilerParams(vmem_limit_bytes=24 * 2**20),
        cost_estimate=pl.CostEstimate(flops=flops, bytes_accessed=6 * 2**20, transcendentals=0),
        name="scores",
    )(near, *blocks)
    return kept + lax.ppermute(sent, "layer", [(0, 1), (1, 0)])


def general(shape, train_grads, queries, left_factor, right_factor):
    layers = shape["layer"]
    own = condition(queries[:, 0], left_factor, right_factor)
    block = lax.all_gather(own, "train", axis=1, tiled=True)
    share = train_grads.shape[0] // layers
    here = lax.axis_index("layer")

    def terms(step):
        rows = lax.dynamic_slice_in_dim(train_grads, (here + step) % layers * share, share, 0)
        return jnp.einsum("fkm,krm->fr", rows, block, preferred_element_type=jnp.float32)

    scores = terms(0)
    for step in range(1, layers):
        scores += lax.ppermute(terms(step), "layer", [(k, (k + step) % layers) for k in range(layers)])
    return scores


def body(shape, train_grads, queries, left_factor, right_factor):
    fits = (
        shape["train"] == COLUMNS * PAIR
        and shape["parts"] == shape["layer"] == 2
        and shape["query"] == 1
        and train_grads.shape[0] % 32 == 0
        and train_grads.shape[1:] == (2, 4096)
        and queries.shape[1:] == (1, 16, 4096)
    )
    if fits:
        return direct(train_grads, queries, left_factor, right_factor)
    return general(shape, train_grads, queries, left_factor, right_factor)


def solution(mesh):
    return jax.shard_map(
        functools.partial(body, dict(mesh.shape)),
        mesh=mesh,
        in_specs=(
            P(("parts", "train"), "layer", None),
            P("layer", "query", "train", None),
            P("layer", None, None),
            P("layer", None, None),
        ),
        out_specs=P(("parts", "train", "layer"), "query"),
        check_vma=False,
    )
```

```python
import functools

import jax
import jax.numpy as jnp
from jax import lax
from jax.experimental import pallas as pl
from jax.experimental.pallas import tpu as pltpu
from jax.sharding import PartitionSpec as P

LANES = 128
PAIR = 2
COLUMNS = 4
LANES_LAST = (((1,), (1,)), ((), ()))


def split(value, parts):
    pieces = []
    for _ in range(parts):
        piece = value.astype(jnp.bfloat16)
        pieces.append(piece)
        value = value - piece.astype(jnp.float32)
    return pieces


def condition(own, left_factor, right_factor):
    layer_count, count, width = own.shape
    rows_out, rows_in = left_factor.shape[1], right_factor.shape[1]
    grid = own.astype(jnp.float32).reshape(layer_count, count, rows_out, rows_in)
    left_part = jnp.einsum("lab,lnbc->lnac", left_factor, grid, precision=lax.Precision.HIGHEST)
    both = jnp.einsum("lnac,lcd->lnad", left_part, right_factor, precision=lax.Precision.HIGHEST)
    return both.reshape(layer_count, count, width).astype(jnp.bfloat16)


def condition_block(block, left, right, put, spread, stacked, placed):
    count, width = block.shape
    inner = right.shape[0]
    pairs = width // LANES
    first_half = lax.broadcasted_iota(jnp.int32, (pairs, LANES), 1) < inner

    empty = jnp.zeros((inner, LANES), jnp.float32)
    twice = jnp.concatenate([right, right], axis=1)
    weight = jnp.concatenate(
        [jnp.concatenate([twice, empty], axis=1), jnp.concatenate([empty, twice], axis=1)], axis=0
    )
    high, middle, low = split(weight, 3)
    rows = jnp.concatenate([block[:, k * LANES : (k + 1) * LANES] for k in range(pairs)], axis=0)
    right_part = jnp.dot(
        jnp.concatenate([rows, rows], axis=1),
        jnp.concatenate([high, middle], axis=0),
        preferred_element_type=jnp.float32,
    ) + jnp.dot(rows, low, preferred_element_type=jnp.float32)
    spread[0] = right_part[:, :LANES]
    spread[1] = right_part[:, LANES:]

    for q in range(0, count, 2):
        for j in range(2):
            even = spread[j, pl.ds(q, pairs, stride=count), :]
            odd = spread[j, pl.ds(q + 1, pairs, stride=count), :]
            stacked[q // 2, pl.ds(j, pairs, stride=2), :] = jnp.where(first_half, even, odd)

    left_high, left_low = split(left, 2)
    moved = jnp.concatenate([stacked[k] for k in range(count // 2)], axis=1)
    moved_high, moved_low = split(moved, 2)
    done = jnp.dot(
        jnp.concatenate([left_high, left_high, left_low], axis=1),
        jnp.concatenate([moved_high, moved_low, moved_high], axis=0),
        preferred_element_type=jnp.float32,
    )
    for k in range(count // 2):
        stacked[k] = done[:, k * LANES : (k + 1) * LANES]

    for q in range(0, count, 2):
        upper = stacked[q // 2, pl.ds(0, pairs, stride=2), :]
        lower = stacked[q // 2, pl.ds(1, pairs, stride=2), :]
        placed[pl.ds(q, pairs, stride=count), :] = jnp.where(first_half, upper, pltpu.roll(lower, inner, 1))
        placed[pl.ds(q + 1, pairs, stride=count), :] = jnp.where(
            first_half, pltpu.roll(upper, inner, 1), lower
        )
    for k in range(pairs):
        put(k, placed[k * count : (k + 1) * count, :].astype(jnp.bfloat16))


def condition_scratch(layers, count, width):
    pairs = width // LANES
    return [
        pltpu.VMEM((layers, 2, pairs * count, LANES), jnp.float32),
        pltpu.VMEM((layers, count // 2, 2 * pairs, LANES), jnp.float32),
        pltpu.VMEM((layers, pairs * count, LANES), jnp.float32),
    ]


def condition_kernel(queries, left, right, own, mine, block_in, left_in, right_in, spread, stacked, placed, arrived):
    layers = queries.shape[0]
    copies = []
    for k, (source, target) in enumerate(((left, left_in), (right, right_in), (queries.at[:, 0], block_in))):
        copies.append(pltpu.make_async_copy(source, target, arrived.at[k]))
        copies[-1].start()
    for copy in copies:
        copy.wait()
    for layer in range(layers):

        def put(k, tile):
            own[layer, :, k * LANES : (k + 1) * LANES] = tile

        condition_block(
            block_in[layer],
            left_in[layer],
            right_in[layer],
            put,
            spread.at[layer],
            stacked.at[layer],
            placed.at[layer],
        )
    mine[...] = own[lax.axis_index("parts")]


def condition_near(queries, left_factor, right_factor):
    layers, _, count, width = queries.shape
    spec = pl.BlockSpec(memory_space=pltpu.VMEM)
    far = pl.BlockSpec(memory_space=pltpu.HBM)
    return pl.pallas_call(
        condition_kernel,
        out_shape=[
            jax.ShapeDtypeStruct((layers, count, width), jnp.bfloat16),
            jax.ShapeDtypeStruct((count, width), jnp.bfloat16),
        ],
        in_specs=[far] * 3,
        out_specs=[spec] * 2,
        scratch_shapes=[
            pltpu.VMEM((layers, count, width), jnp.bfloat16),
            pltpu.VMEM(left_factor.shape, jnp.float32),
            pltpu.VMEM(right_factor.shape, jnp.float32),
            *condition_scratch(layers, count, width),
            pltpu.SemaphoreType.DMA((3,)),
        ],
        compiler_params=pltpu.CompilerParams(vmem_limit_bytes=8 * 2**20),
        cost_estimate=pl.CostEstimate(flops=2**28, bytes_accessed=2**20, transcendentals=0),
        name="condition",
    )(*(pltpu.with_memory_space_constraint(x, pltpu.HBM) for x in (queries, left_factor, right_factor)))


def along_columns(value, step):
    pairs = [
        (((k + step) % COLUMNS) * PAIR + c, k * PAIR + c)
        for k in range(COLUMNS)
        for c in range(PAIR)
    ]
    return lax.ppermute(value, "train", pairs)


def other_core(value):
    return lax.ppermute(value, "train", [(k, k ^ 1) for k in range(COLUMNS * PAIR)])


def other_part(value):
    return lax.ppermute(value, "parts", [(0, 1), (1, 0)])


def copy_kernel(source, target, done):
    copy = pltpu.make_async_copy(source, target, done)
    copy.start()
    copy.wait()


def copy_near(value):
    return pl.pallas_call(
        copy_kernel,
        out_shape=jax.ShapeDtypeStruct(value.shape, value.dtype),
        in_specs=[pl.BlockSpec(memory_space=pltpu.HBM)],
        out_specs=pl.BlockSpec(memory_space=pltpu.VMEM),
        scratch_shapes=[pltpu.SemaphoreType.DMA],
        compiler_params=pltpu.CompilerParams(vmem_limit_bytes=6 * 2**20),
        cost_estimate=pl.CostEstimate(flops=0, bytes_accessed=2 * value.size * 2, transcendentals=0),
        name="near",
    )(pltpu.with_memory_space_constraint(value, pltpu.HBM))


def score_kernel(
    train, own, own_c, s2, s2_c, s1, s1_c, s3, s3_c, y2, y2_c, y1, y1_c, y3, y3_c, sent, kept, table, terms
):
    part = lax.axis_index("parts")
    place = lax.axis_index("train")
    here = lax.axis_index("layer")
    column, core = place // PAIR, lax.rem(place, PAIR)
    count = own.shape[1]

    def put(layer, step, twin, block):
        member = lax.rem(column + step, COLUMNS) * PAIR + (1 - core if twin else core)
        table[layer, pl.ds(pl.multiple_of(member * count, count), count), :] = block

    for twin, (both, here_steps, there_steps) in enumerate(
        ((own, (s1, s2, s3), (y1, y2, y3)), (own_c, (s1_c, s2_c, s3_c), (y1_c, y2_c, y3_c)))
    ):
        put(0, 0, twin, both[0])
        put(1, 0, twin, both[1])
        for step in range(1, COLUMNS):
            put(part, step, twin, here_steps[step - 1][...])
            put(1 - part, step, twin, there_steps[step - 1][...])

    rows, layer_count, width = train.shape
    queries = table.shape[1]
    both = lax.dot_general(
        train.reshape(rows * layer_count, width)[...],
        table[...].reshape(layer_count * queries, width),
        LANES_LAST,
        preferred_element_type=jnp.float32,
    )
    for layer in range(layer_count):
        terms[layer] = both[:, layer * queries : (layer + 1) * queries]
    share = kept.shape[0]
    for out, owner in ((sent, 1 - here), (kept, here)):
        first = pl.multiple_of(owner * share * layer_count, share * layer_count)
        out[...] = sum(
            terms[layer, pl.ds(first + layer, share, stride=layer_count), :] for layer in range(layer_count)
        )


def direct(train_grads, queries, left_factor, right_factor):
    own, mine = condition_near(queries, left_factor, right_factor)
    near = copy_near(train_grads)
    s2 = along_columns(mine, 2)
    s1 = along_columns(mine, 1)
    s3 = along_columns(mine, 3)
    y2 = other_part(s2)
    y1 = other_part(s1)
    y3 = other_part(s3)
    y1, near = lax.optimization_barrier((y1, near))
    blocks = []
    for block in (own, s2, s1, s3, y2, y1, y3):
        blocks += [block, other_core(block)]

    rows, layer_count, width = train_grads.shape
    total = queries.shape[2] * COLUMNS * PAIR
    share = rows // 2
    spec = pl.BlockSpec(memory_space=pltpu.VMEM)
    flops = 4 * rows * layer_count * width * total
    sent, kept = pl.pallas_call(
        score_kernel,
        out_shape=[jax.ShapeDtypeStruct((share, total), jnp.float32)] * 2,
        in_specs=[spec] * (1 + len(blocks)),
        out_specs=[spec] * 2,
        scratch_shapes=[
            pltpu.VMEM((layer_count, total, width), jnp.bfloat16),
            pltpu.VMEM((layer_count, rows * layer_count, total), jnp.float32),
        ],
        compiler_params=pltpu.CompilerParams(vmem_limit_bytes=24 * 2**20),
        cost_estimate=pl.CostEstimate(flops=flops, bytes_accessed=6 * 2**20, transcendentals=0),
        name="scores",
    )(near, *blocks)
    return kept + lax.ppermute(sent, "layer", [(0, 1), (1, 0)])


def general(shape, train_grads, queries, left_factor, right_factor):
    layers = shape["layer"]
    own = condition(queries[:, 0], left_factor, right_factor)
    block = lax.all_gather(own, "train", axis=1, tiled=True)
    share = train_grads.shape[0] // layers
    here = lax.axis_index("layer")

    def terms(step):
        rows = lax.dynamic_slice_in_dim(train_grads, (here + step) % layers * share, share, 0)
        return jnp.einsum("fkm,krm->fr", rows, block, preferred_element_type=jnp.float32)

    scores = terms(0)
    for step in range(1, layers):
        scores += lax.ppermute(terms(step), "layer", [(k, (k + step) % layers) for k in range(layers)])
    return scores


def body(shape, train_grads, queries, left_factor, right_factor):
    fits = (
        shape["train"] == COLUMNS * PAIR
        and shape["parts"] == shape["layer"] == 2
        and shape["query"] == 1
        and train_grads.shape[0] % 32 == 0
        and train_grads.shape[1:] == (2, 4096)
        and queries.shape[1:] == (1, 16, 4096)
        and left_factor.shape[1:] == right_factor.shape[1:] == (64, 64)
    )
    if fits:
        return direct(train_grads, queries, left_factor, right_factor)
    return general(shape, train_grads, queries, left_factor, right_factor)


def solution(mesh):
    return jax.shard_map(
        functools.partial(body, dict(mesh.shape)),
        mesh=mesh,
        in_specs=(
            P(("parts", "train"), "layer", None),
            P("layer", "query", "train", None),
            P("layer", None, None),
            P("layer", None, None),
        ),
        out_specs=P(("parts", "train", "layer"), "query"),
        check_vma=False,
    )
```

```python
import functools

import jax
import jax.numpy as jnp
from jax import lax
from jax.experimental import pallas as pl
from jax.experimental.pallas import tpu as pltpu
from jax.sharding import PartitionSpec as P

LANES = 128
PAIR = 2
COLUMNS = 4
LANES_LAST = (((1,), (1,)), ((), ()))


def split(value, parts):
    pieces = []
    for _ in range(parts):
        piece = value.astype(jnp.bfloat16)
        pieces.append(piece)
        value = value - piece.astype(jnp.float32)
    return pieces


def condition(own, left_factor, right_factor):
    layer_count, count, width = own.shape
    rows_out, rows_in = left_factor.shape[1], right_factor.shape[1]
    grid = own.astype(jnp.float32).reshape(layer_count, count, rows_out, rows_in)
    left_part = jnp.einsum("lab,lnbc->lnac", left_factor, grid, precision=lax.Precision.HIGHEST)
    both = jnp.einsum("lnac,lcd->lnad", left_part, right_factor, precision=lax.Precision.HIGHEST)
    return both.reshape(layer_count, count, width).astype(jnp.bfloat16)


def condition_block(block, left, right, put, spread, stacked, placed):
    count, width = block.shape
    inner = right.shape[0]
    pairs = width // LANES
    first_half = lax.broadcasted_iota(jnp.int32, (pairs, LANES), 1) < inner

    empty = jnp.zeros((inner, LANES), jnp.float32)
    twice = jnp.concatenate([right, right], axis=1)
    weight = jnp.concatenate(
        [jnp.concatenate([twice, empty], axis=1), jnp.concatenate([empty, twice], axis=1)], axis=0
    )
    high, middle, low = split(weight, 3)
    rows = jnp.concatenate([block[:, k * LANES : (k + 1) * LANES] for k in range(pairs)], axis=0)
    right_part = jnp.dot(
        jnp.concatenate([rows, rows], axis=1),
        jnp.concatenate([high, middle], axis=0),
        preferred_element_type=jnp.float32,
    ) + jnp.dot(rows, low, preferred_element_type=jnp.float32)
    spread[0] = right_part[:, :LANES]
    spread[1] = right_part[:, LANES:]

    for q in range(0, count, 2):
        for j in range(2):
            even = spread[j, pl.ds(q, pairs, stride=count), :]
            odd = spread[j, pl.ds(q + 1, pairs, stride=count), :]
            stacked[q // 2, pl.ds(j, pairs, stride=2), :] = jnp.where(first_half, even, odd)

    left_high, left_low = split(left, 2)
    moved = jnp.concatenate([stacked[k] for k in range(count // 2)], axis=1)
    moved_high, moved_low = split(moved, 2)
    done = jnp.dot(
        jnp.concatenate([left_high, left_high, left_low], axis=1),
        jnp.concatenate([moved_high, moved_low, moved_high], axis=0),
        preferred_element_type=jnp.float32,
    )
    for k in range(count // 2):
        stacked[k] = done[:, k * LANES : (k + 1) * LANES]

    for q in range(0, count, 2):
        upper = stacked[q // 2, pl.ds(0, pairs, stride=2), :]
        lower = stacked[q // 2, pl.ds(1, pairs, stride=2), :]
        placed[pl.ds(q, pairs, stride=count), :] = jnp.where(first_half, upper, pltpu.roll(lower, inner, 1))
        placed[pl.ds(q + 1, pairs, stride=count), :] = jnp.where(
            first_half, pltpu.roll(upper, inner, 1), lower
        )
    for k in range(pairs):
        put(k, placed[k * count : (k + 1) * count, :].astype(jnp.bfloat16))


def condition_kernel(other, queries, left, right, out, block_in, left_in, right_in, spread, stacked, placed, arrived):
    part = lax.axis_index("parts")
    layer = 1 - part if other else part
    copies = [
        pltpu.make_async_copy(source, target, arrived.at[k])
        for k, (source, target) in enumerate(
            ((queries.at[layer, 0], block_in), (right.at[layer], right_in), (left.at[layer], left_in))
        )
    ]
    for copy in copies:
        copy.start()
    for copy in copies:
        copy.wait()

    def put(k, tile):
        out[:, k * LANES : (k + 1) * LANES] = tile

    condition_block(block_in[...], left_in[...], right_in[...], put, spread, stacked, placed)


def condition_layer(other, queries, left_factor, right_factor):
    _, _, count, width = queries.shape
    pairs = width // LANES
    far = pl.BlockSpec(memory_space=pltpu.HBM)
    return pl.pallas_call(
        functools.partial(condition_kernel, other),
        out_shape=jax.ShapeDtypeStruct((count, width), jnp.bfloat16),
        in_specs=[far] * 3,
        out_specs=pl.BlockSpec(memory_space=pltpu.VMEM),
        scratch_shapes=[
            pltpu.VMEM((count, width), jnp.bfloat16),
            pltpu.VMEM(left_factor.shape[1:], jnp.float32),
            pltpu.VMEM(right_factor.shape[1:], jnp.float32),
            pltpu.VMEM((2, pairs * count, LANES), jnp.float32),
            pltpu.VMEM((count // 2, 2 * pairs, LANES), jnp.float32),
            pltpu.VMEM((pairs * count, LANES), jnp.float32),
            pltpu.SemaphoreType.DMA((3,)),
        ],
        compiler_params=pltpu.CompilerParams(vmem_limit_bytes=8 * 2**20),
        cost_estimate=pl.CostEstimate(flops=2**27, bytes_accessed=2**19, transcendentals=0),
        name="condition_other" if other else "condition_mine",
    )(*(pltpu.with_memory_space_constraint(x, pltpu.HBM) for x in (queries, left_factor, right_factor)))


def along_columns(value, step):
    pairs = [
        (((k + step) % COLUMNS) * PAIR + c, k * PAIR + c)
        for k in range(COLUMNS)
        for c in range(PAIR)
    ]
    return lax.ppermute(value, "train", pairs)


def other_core(value):
    return lax.ppermute(value, "train", [(k, k ^ 1) for k in range(COLUMNS * PAIR)])


def other_part(value):
    return lax.ppermute(value, "parts", [(0, 1), (1, 0)])


def copy_kernel(source, target, done):
    copy = pltpu.make_async_copy(source, target, done)
    copy.start()
    copy.wait()


def copy_near(value):
    return pl.pallas_call(
        copy_kernel,
        out_shape=jax.ShapeDtypeStruct(value.shape, value.dtype),
        in_specs=[pl.BlockSpec(memory_space=pltpu.HBM)],
        out_specs=pl.BlockSpec(memory_space=pltpu.VMEM),
        scratch_shapes=[pltpu.SemaphoreType.DMA],
        compiler_params=pltpu.CompilerParams(vmem_limit_bytes=6 * 2**20),
        cost_estimate=pl.CostEstimate(flops=0, bytes_accessed=2 * value.size * 2, transcendentals=0),
        name="near",
    )(pltpu.with_memory_space_constraint(value, pltpu.HBM))


def place():
    member = lax.axis_index("train")
    return member // PAIR, lax.rem(member, PAIR)


def both_products(train, table):
    rows, layer_count, width = train.shape
    return lax.dot_general(
        train.reshape(rows * layer_count, width)[...],
        table[...].reshape(table.shape[0] * table.shape[1], width),
        LANES_LAST,
        preferred_element_type=jnp.float32,
    )


def early_kernel(train, *refs):
    blocks, (sent, kept, table, terms) = refs[:-4], refs[-4:]
    part, here = lax.axis_index("parts"), lax.axis_index("layer")
    column, core = place()
    count, width = blocks[0].shape
    layer_count, queries = table.shape[:2]
    share = kept.shape[0]

    def put(layer, step, twin, block):
        member = lax.rem(column + step, COLUMNS) * PAIR + (1 - core if twin else core)
        table[layer, pl.ds(pl.multiple_of(member * count, count), count), :] = block

    nothing = jnp.zeros((count, width), jnp.bfloat16)
    for twin in range(PAIR):
        for k, step in enumerate((0, 1, 3)):
            put(part, step, twin, blocks[4 * k + twin][...])
            put(1 - part, step, twin, blocks[4 * k + 2 + twin][...])
        for layer in range(layer_count):
            put(layer, 2, twin, nothing)

    both = both_products(train, table)
    for layer in range(layer_count):
        terms[layer] = both[:, layer * queries : (layer + 1) * queries]
    for out, owner in ((sent, 1 - here), (kept, here)):
        first = pl.multiple_of(owner * share * layer_count, share * layer_count)
        out[...] = sum(
            terms[layer, pl.ds(first + layer, share, stride=layer_count), :] for layer in range(layer_count)
        )


def late_kernel(train, s2, s2_c, y2, y2_c, sent, kept, table, terms):
    part, here = lax.axis_index("parts"), lax.axis_index("layer")
    _, core = place()
    count = s2.shape[0]
    layer_count = table.shape[0]
    late, share = kept.shape

    for layer, block, twin in ((part, s2, core), (part, s2_c, 1 - core), (1 - part, y2, core), (1 - part, y2_c, 1 - core)):
        table[layer, pl.ds(pl.multiple_of(twin * count, count), count), :] = block[...]
    both = both_products(train, table)
    terms[:, : layer_count * late] = both
    for out, owner in ((sent, 1 - here), (kept, here)):
        first = pl.multiple_of(owner * share * layer_count, share * layer_count)
        total = terms[pl.ds(first, share, stride=layer_count), :]
        for layer in range(1, layer_count):
            more = terms[pl.ds(first + layer, share, stride=layer_count), :]
            total = total + pltpu.roll(more, LANES - layer * late, 1)
        out[...] = jnp.transpose(total)[:late]


def sum_kernel(kept, received, late_kept, late_received, scores, late):
    column, _ = place()
    count = late_kept.shape[0]
    late[...] = jnp.zeros_like(late)
    first = pl.multiple_of(lax.rem(column + 2, COLUMNS) * count, count)
    late[pl.ds(first, count), :] = late_kept[...] + late_received[...]
    scores[...] = kept[...] + received[...] + jnp.transpose(late[...])


def local_call(kernel, name, out_shape, scratch_shapes, flops, moved, *operands):
    spec = pl.BlockSpec(memory_space=pltpu.VMEM)
    return pl.pallas_call(
        kernel,
        out_shape=out_shape,
        in_specs=[spec] * len(operands),
        out_specs=jax.tree.map(lambda _: spec, out_shape),
        scratch_shapes=scratch_shapes,
        compiler_params=pltpu.CompilerParams(vmem_limit_bytes=24 * 2**20),
        cost_estimate=pl.CostEstimate(flops=flops, bytes_accessed=moved, transcendentals=0),
        name=name,
    )(*operands)


def direct(train_grads, queries, left_factor, right_factor):
    rows, layer_count, width = train_grads.shape
    count = queries.shape[2]
    total = count * COLUMNS * PAIR
    late = count * PAIR
    share = rows // 2

    mine = condition_layer(False, queries, left_factor, right_factor)
    other = condition_layer(True, queries, left_factor, right_factor)
    near = copy_near(train_grads)
    s2 = along_columns(mine, 2)
    s1 = along_columns(mine, 1)
    s3 = along_columns(mine, 3)
    s1, other = lax.optimization_barrier((s1, other))
    y1 = other_part(s1)
    s3, near = lax.optimization_barrier((s3, near))
    y3 = other_part(s3)
    y2 = other_part(s2)

    blocks = []
    for block in (mine, other, s1, y1, s3, y3):
        blocks += [block, other_core(block)]
    f32 = functools.partial(jax.ShapeDtypeStruct, dtype=jnp.float32)
    sent, kept = local_call(
        early_kernel,
        "early_scores",
        [f32((share, total))] * 2,
        [
            pltpu.VMEM((layer_count, total, width), jnp.bfloat16),
            pltpu.VMEM((layer_count, rows * layer_count, total), jnp.float32),
        ],
        4 * rows * layer_count * width * total,
        6 * 2**20,
        near,
        *blocks,
    )
    y2, sent = lax.optimization_barrier((y2, sent))
    received = lax.ppermute(sent, "layer", [(0, 1), (1, 0)])
    late_sent, late_kept = local_call(
        late_kernel,
        "late_scores",
        [f32((late, share))] * 2,
        [
            pltpu.VMEM((layer_count, late, width), jnp.bfloat16),
            pltpu.VMEM((rows * layer_count, LANES), jnp.float32),
        ],
        4 * rows * layer_count * width * late,
        5 * 2**20,
        near,
        s2,
        other_core(s2),
        y2,
        other_core(y2),
    )
    late_received = lax.ppermute(late_sent, "layer", [(0, 1), (1, 0)])
    return local_call(
        sum_kernel,
        "sum_scores",
        f32((share, total)),
        [pltpu.VMEM((total, share), jnp.float32)],
        3 * share * total,
        2**18,
        kept,
        received,
        late_kept,
        late_received,
    )


def general(shape, train_grads, queries, left_factor, right_factor):
    layers = shape["layer"]
    own = condition(queries[:, 0], left_factor, right_factor)
    block = lax.all_gather(own, "train", axis=1, tiled=True)
    share = train_grads.shape[0] // layers
    here = lax.axis_index("layer")

    def terms(step):
        rows = lax.dynamic_slice_in_dim(train_grads, (here + step) % layers * share, share, 0)
        return jnp.einsum("fkm,krm->fr", rows, block, preferred_element_type=jnp.float32)

    scores = terms(0)
    for step in range(1, layers):
        scores += lax.ppermute(terms(step), "layer", [(k, (k + step) % layers) for k in range(layers)])
    return scores


def body(shape, train_grads, queries, left_factor, right_factor):
    fits = (
        shape["train"] == COLUMNS * PAIR
        and shape["parts"] == shape["layer"] == 2
        and shape["query"] == 1
        and train_grads.shape[0] == 2 * LANES
        and train_grads.shape[1:] == (2, 4096)
        and queries.shape[1:] == (1, 16, 4096)
        and left_factor.shape[1:] == right_factor.shape[1:] == (64, 64)
    )
    if fits:
        return direct(train_grads, queries, left_factor, right_factor)
    return general(shape, train_grads, queries, left_factor, right_factor)


def solution(mesh):
    return jax.shard_map(
        functools.partial(body, dict(mesh.shape)),
        mesh=mesh,
        in_specs=(
            P(("parts", "train"), "layer", None),
            P("layer", "query", "train", None),
            P("layer", None, None),
            P("layer", None, None),
        ),
        out_specs=P(("parts", "train", "layer"), "query"),
        check_vma=False,
    )
```

```python
import functools

import jax
import jax.numpy as jnp
from jax import lax
from jax.experimental import pallas as pl
from jax.experimental.pallas import tpu as pltpu
from jax.sharding import PartitionSpec as P

LANES = 128
PAIR = 2
COLUMNS = 4
LANES_LAST = (((1,), (1,)), ((), ()))


def split(value, parts):
    pieces = []
    for _ in range(parts):
        piece = value.astype(jnp.bfloat16)
        pieces.append(piece)
        value = value - piece.astype(jnp.float32)
    return pieces


def condition(own, left_factor, right_factor):
    layer_count, count, width = own.shape
    rows_out, rows_in = left_factor.shape[1], right_factor.shape[1]
    grid = own.astype(jnp.float32).reshape(layer_count, count, rows_out, rows_in)
    left_part = jnp.einsum("lab,lnbc->lnac", left_factor, grid, precision=lax.Precision.HIGHEST)
    both = jnp.einsum("lnac,lcd->lnad", left_part, right_factor, precision=lax.Precision.HIGHEST)
    return both.reshape(layer_count, count, width).astype(jnp.bfloat16)


def condition_block(block, left, right, put, spread, stacked, placed):
    count, width = block.shape
    inner = right.shape[0]
    pairs = width // LANES
    first_half = lax.broadcasted_iota(jnp.int32, (pairs, LANES), 1) < inner

    empty = jnp.zeros((inner, LANES), jnp.float32)
    twice = jnp.concatenate([right, right], axis=1)
    weight = jnp.concatenate(
        [jnp.concatenate([twice, empty], axis=1), jnp.concatenate([empty, twice], axis=1)], axis=0
    )
    high, middle, low = split(weight, 3)
    rows = jnp.concatenate([block[:, k * LANES : (k + 1) * LANES] for k in range(pairs)], axis=0)
    right_part = jnp.dot(
        jnp.concatenate([rows, rows], axis=1),
        jnp.concatenate([high, middle], axis=0),
        preferred_element_type=jnp.float32,
    ) + jnp.dot(rows, low, preferred_element_type=jnp.float32)
    spread[0] = right_part[:, :LANES]
    spread[1] = right_part[:, LANES:]

    for q in range(0, count, 2):
        for j in range(2):
            even = spread[j, pl.ds(q, pairs, stride=count), :]
            odd = spread[j, pl.ds(q + 1, pairs, stride=count), :]
            stacked[q // 2, pl.ds(j, pairs, stride=2), :] = jnp.where(first_half, even, odd)

    left_high, left_low = split(left, 2)
    moved = jnp.concatenate([stacked[k] for k in range(count // 2)], axis=1)
    moved_high, moved_low = split(moved, 2)
    done = jnp.dot(
        jnp.concatenate([left_high, left_high, left_low], axis=1),
        jnp.concatenate([moved_high, moved_low, moved_high], axis=0),
        preferred_element_type=jnp.float32,
    )
    for k in range(count // 2):
        stacked[k] = done[:, k * LANES : (k + 1) * LANES]

    for q in range(0, count, 2):
        upper = stacked[q // 2, pl.ds(0, pairs, stride=2), :]
        lower = stacked[q // 2, pl.ds(1, pairs, stride=2), :]
        placed[pl.ds(q, pairs, stride=count), :] = jnp.where(first_half, upper, pltpu.roll(lower, inner, 1))
        placed[pl.ds(q + 1, pairs, stride=count), :] = jnp.where(
            first_half, pltpu.roll(upper, inner, 1), lower
        )
    for k in range(pairs):
        put(k, placed[k * count : (k + 1) * count, :].astype(jnp.bfloat16))


def condition_kernel(other, queries, left, right, out, block_in, left_in, right_in, spread, stacked, placed, arrived):
    part = lax.axis_index("parts")
    layer = 1 - part if other else part
    copies = [
        pltpu.make_async_copy(source, target, arrived.at[k])
        for k, (source, target) in enumerate(
            ((queries.at[layer, 0], block_in), (right.at[layer], right_in), (left.at[layer], left_in))
        )
    ]
    for copy in copies:
        copy.start()
    for copy in copies:
        copy.wait()

    def put(k, tile):
        out[:, k * LANES : (k + 1) * LANES] = tile

    condition_block(block_in[...], left_in[...], right_in[...], put, spread, stacked, placed)


def condition_layer(other, queries, left_factor, right_factor):
    _, _, count, width = queries.shape
    pairs = width // LANES
    far = pl.BlockSpec(memory_space=pltpu.HBM)
    return pl.pallas_call(
        functools.partial(condition_kernel, other),
        out_shape=jax.ShapeDtypeStruct((count, width), jnp.bfloat16),
        in_specs=[far] * 3,
        out_specs=pl.BlockSpec(memory_space=pltpu.VMEM),
        scratch_shapes=[
            pltpu.VMEM((count, width), jnp.bfloat16),
            pltpu.VMEM(left_factor.shape[1:], jnp.float32),
            pltpu.VMEM(right_factor.shape[1:], jnp.float32),
            pltpu.VMEM((2, pairs * count, LANES), jnp.float32),
            pltpu.VMEM((count // 2, 2 * pairs, LANES), jnp.float32),
            pltpu.VMEM((pairs * count, LANES), jnp.float32),
            pltpu.SemaphoreType.DMA((3,)),
        ],
        compiler_params=pltpu.CompilerParams(vmem_limit_bytes=8 * 2**20),
        cost_estimate=pl.CostEstimate(flops=2**27, bytes_accessed=2**19, transcendentals=0),
        name="condition_other" if other else "condition_mine",
    )(*(pltpu.with_memory_space_constraint(x, pltpu.HBM) for x in (queries, left_factor, right_factor)))


def along_columns(value, step):
    pairs = [
        (((k + step) % COLUMNS) * PAIR + c, k * PAIR + c)
        for k in range(COLUMNS)
        for c in range(PAIR)
    ]
    return lax.ppermute(value, "train", pairs)


def other_core(value):
    return lax.ppermute(value, "train", [(k, k ^ 1) for k in range(COLUMNS * PAIR)])


def other_part(value):
    return lax.ppermute(value, "parts", [(0, 1), (1, 0)])


def copy_kernel(source, target, done):
    copy = pltpu.make_async_copy(source, target, done)
    copy.start()
    copy.wait()


def copy_near(value):
    return pl.pallas_call(
        copy_kernel,
        out_shape=jax.ShapeDtypeStruct(value.shape, value.dtype),
        in_specs=[pl.BlockSpec(memory_space=pltpu.HBM)],
        out_specs=pl.BlockSpec(memory_space=pltpu.VMEM),
        scratch_shapes=[pltpu.SemaphoreType.DMA],
        compiler_params=pltpu.CompilerParams(vmem_limit_bytes=6 * 2**20),
        cost_estimate=pl.CostEstimate(flops=0, bytes_accessed=2 * value.size * 2, transcendentals=0),
        name="near",
    )(pltpu.with_memory_space_constraint(value, pltpu.HBM))


def place():
    member = lax.axis_index("train")
    return member // PAIR, lax.rem(member, PAIR)


def row_scores(train, table, owner, terms, scores):
    share = scores.shape[0]
    rows, layer_count, width = train.shape
    queries = table.shape[1]
    first = pl.multiple_of(owner * share * layer_count, share * layer_count)
    both = lax.dot_general(
        train.reshape(rows * layer_count, width)[pl.ds(first, share * layer_count), :],
        table[...].reshape(layer_count * queries, width),
        LANES_LAST,
        preferred_element_type=jnp.float32,
    )
    for layer in range(layer_count):
        terms[layer] = both[:, layer * queries : (layer + 1) * queries]
    scores[...] = sum(terms[layer, pl.ds(layer, share, stride=layer_count), :] for layer in range(layer_count))


def sent_kernel(train, *refs):
    blocks, (scores, table, terms) = refs[:-3], refs[-3:]
    part = lax.axis_index("parts")
    column, core = place()
    count = blocks[0].shape[0]

    def put(layer, step, twin, block):
        member = lax.rem(column + step, COLUMNS) * PAIR + (1 - core if twin else core)
        table[layer, pl.ds(pl.multiple_of(member * count, count), count), :] = block

    for twin in range(PAIR):
        for k, (layer, step) in enumerate(
            ((part, 0), (1 - part, 0), (part, 2), (part, 1), (part, 3), (1 - part, 2), (1 - part, 1), (1 - part, 3))
        ):
            put(layer, step, twin, blocks[PAIR * k + twin][...])
    row_scores(train, table, 1 - lax.axis_index("layer"), terms, scores)


def kept_kernel(train, table, scores, terms):
    row_scores(train, table, lax.axis_index("layer"), terms, scores)


def local_call(kernel, name, out_shape, scratch_shapes, *operands):
    spec = pl.BlockSpec(memory_space=pltpu.VMEM)
    return pl.pallas_call(
        kernel,
        out_shape=out_shape,
        in_specs=[spec] * len(operands),
        out_specs=jax.tree.map(lambda _: spec, out_shape),
        scratch_shapes=scratch_shapes,
        compiler_params=pltpu.CompilerParams(vmem_limit_bytes=24 * 2**20),
        cost_estimate=pl.CostEstimate(flops=2**29, bytes_accessed=2**22, transcendentals=0),
        name=name,
    )(*operands)


def direct(train_grads, queries, left_factor, right_factor):
    rows, layer_count, width = train_grads.shape
    count = queries.shape[2]
    total = count * COLUMNS * PAIR
    share = rows // 2

    mine = condition_layer(False, queries, left_factor, right_factor)
    other = condition_layer(True, queries, left_factor, right_factor)
    near = copy_near(train_grads)
    s2 = along_columns(mine, 2)
    s1 = along_columns(mine, 1)
    s3 = along_columns(mine, 3)
    s1, other = lax.optimization_barrier((s1, other))
    s3, near = lax.optimization_barrier((s3, near))
    y1 = other_part(s1)
    y3 = other_part(s3)
    s2, y1, y3 = lax.optimization_barrier((s2, y1, y3))
    y2 = other_part(s2)

    blocks = []
    for block in (mine, other, s2, s1, s3, y2, y1, y3):
        blocks += [block, other_core(block)]
    f32 = functools.partial(jax.ShapeDtypeStruct, dtype=jnp.float32)
    terms = [pltpu.VMEM((layer_count, share * layer_count, total), jnp.float32)]
    sent, table = local_call(
        sent_kernel,
        "scores_sent",
        [f32((share, total)), jax.ShapeDtypeStruct((layer_count, total, width), jnp.bfloat16)],
        terms,
        near,
        *blocks,
    )
    received = lax.ppermute(sent, "layer", [(0, 1), (1, 0)])
    kept = local_call(kept_kernel, "scores_kept", f32((share, total)), terms, near, table)
    return kept + received


def general(shape, train_grads, queries, left_factor, right_factor):
    layers = shape["layer"]
    own = condition(queries[:, 0], left_factor, right_factor)
    block = lax.all_gather(own, "train", axis=1, tiled=True)
    share = train_grads.shape[0] // layers
    here = lax.axis_index("layer")

    def terms(step):
        rows = lax.dynamic_slice_in_dim(train_grads, (here + step) % layers * share, share, 0)
        return jnp.einsum("fkm,krm->fr", rows, block, preferred_element_type=jnp.float32)

    scores = terms(0)
    for step in range(1, layers):
        scores += lax.ppermute(terms(step), "layer", [(k, (k + step) % layers) for k in range(layers)])
    return scores


def body(shape, train_grads, queries, left_factor, right_factor):
    fits = (
        shape["train"] == COLUMNS * PAIR
        and shape["parts"] == shape["layer"] == 2
        and shape["query"] == 1
        and train_grads.shape[0] == 2 * LANES
        and train_grads.shape[1:] == (2, 4096)
        and queries.shape[1:] == (1, 16, 4096)
        and left_factor.shape[1:] == right_factor.shape[1:] == (64, 64)
    )
    if fits:
        return direct(train_grads, queries, left_factor, right_factor)
    return general(shape, train_grads, queries, left_factor, right_factor)


def solution(mesh):
    return jax.shard_map(
        functools.partial(body, dict(mesh.shape)),
        mesh=mesh,
        in_specs=(
            P(("parts", "train"), "layer", None),
            P("layer", "query", "train", None),
            P("layer", None, None),
            P("layer", None, None),
        ),
        out_specs=P(("parts", "train", "layer"), "query"),
        check_vma=False,
    )
```

```python
import functools

import jax
import jax.numpy as jnp
from jax import lax
from jax.experimental import pallas as pl
from jax.experimental.pallas import tpu as pltpu
from jax.sharding import PartitionSpec as P

LANES = 128
PAIR = 2
COLUMNS = 4
LANES_LAST = (((1,), (1,)), ((), ()))


def split(value, parts):
    pieces = []
    for _ in range(parts):
        piece = value.astype(jnp.bfloat16)
        pieces.append(piece)
        value = value - piece.astype(jnp.float32)
    return pieces


def condition(own, left_factor, right_factor):
    layer_count, count, width = own.shape
    rows_out, rows_in = left_factor.shape[1], right_factor.shape[1]
    grid = own.astype(jnp.float32).reshape(layer_count, count, rows_out, rows_in)
    left_part = jnp.einsum("lab,lnbc->lnac", left_factor, grid, precision=lax.Precision.HIGHEST)
    both = jnp.einsum("lnac,lcd->lnad", left_part, right_factor, precision=lax.Precision.HIGHEST)
    return both.reshape(layer_count, count, width).astype(jnp.bfloat16)


def condition_block(block, left, right, put, spread, stacked, placed):
    count, width = block.shape
    inner = right.shape[0]
    pairs = width // LANES
    first_half = lax.broadcasted_iota(jnp.int32, (pairs, LANES), 1) < inner

    empty = jnp.zeros((inner, LANES), jnp.float32)
    twice = jnp.concatenate([right, right], axis=1)
    weight = jnp.concatenate(
        [jnp.concatenate([twice, empty], axis=1), jnp.concatenate([empty, twice], axis=1)], axis=0
    )
    high, middle, low = split(weight, 3)
    rows = jnp.concatenate([block[:, k * LANES : (k + 1) * LANES] for k in range(pairs)], axis=0)
    right_part = jnp.dot(
        jnp.concatenate([rows, rows], axis=1),
        jnp.concatenate([high, middle], axis=0),
        preferred_element_type=jnp.float32,
    ) + jnp.dot(rows, low, preferred_element_type=jnp.float32)
    spread[0] = right_part[:, :LANES]
    spread[1] = right_part[:, LANES:]

    for q in range(0, count, 2):
        for j in range(2):
            even = spread[j, pl.ds(q, pairs, stride=count), :]
            odd = spread[j, pl.ds(q + 1, pairs, stride=count), :]
            stacked[q // 2, pl.ds(j, pairs, stride=2), :] = jnp.where(first_half, even, odd)

    left_high, left_low = split(left, 2)
    moved = jnp.concatenate([stacked[k] for k in range(count // 2)], axis=1)
    moved_high, moved_low = split(moved, 2)
    done = jnp.dot(
        jnp.concatenate([left_high, left_high, left_low], axis=1),
        jnp.concatenate([moved_high, moved_low, moved_high], axis=0),
        preferred_element_type=jnp.float32,
    )
    for k in range(count // 2):
        stacked[k] = done[:, k * LANES : (k + 1) * LANES]

    for q in range(0, count, 2):
        upper = stacked[q // 2, pl.ds(0, pairs, stride=2), :]
        lower = stacked[q // 2, pl.ds(1, pairs, stride=2), :]
        placed[pl.ds(q, pairs, stride=count), :] = jnp.where(first_half, upper, pltpu.roll(lower, inner, 1))
        placed[pl.ds(q + 1, pairs, stride=count), :] = jnp.where(
            first_half, pltpu.roll(upper, inner, 1), lower
        )
    for k in range(pairs):
        put(k, placed[k * count : (k + 1) * count, :].astype(jnp.bfloat16))


def condition_kernel(other, queries, left, right, out, block_in, left_in, right_in, spread, stacked, placed, arrived):
    part = lax.axis_index("parts")
    layer = 1 - part if other else part
    copies = [
        pltpu.make_async_copy(source, target, arrived.at[k])
        for k, (source, target) in enumerate(
            ((queries.at[layer, 0], block_in), (right.at[layer], right_in), (left.at[layer], left_in))
        )
    ]
    for copy in copies:
        copy.start()
    for copy in copies:
        copy.wait()

    def put(k, tile):
        out[:, k * LANES : (k + 1) * LANES] = tile

    condition_block(block_in[...], left_in[...], right_in[...], put, spread, stacked, placed)


def condition_layer(other, queries, left_factor, right_factor):
    _, _, count, width = queries.shape
    pairs = width // LANES
    far = pl.BlockSpec(memory_space=pltpu.HBM)
    return pl.pallas_call(
        functools.partial(condition_kernel, other),
        out_shape=jax.ShapeDtypeStruct((count, width), jnp.bfloat16),
        in_specs=[far] * 3,
        out_specs=pl.BlockSpec(memory_space=pltpu.VMEM),
        scratch_shapes=[
            pltpu.VMEM((count, width), jnp.bfloat16),
            pltpu.VMEM(left_factor.shape[1:], jnp.float32),
            pltpu.VMEM(right_factor.shape[1:], jnp.float32),
            pltpu.VMEM((2, pairs * count, LANES), jnp.float32),
            pltpu.VMEM((count // 2, 2 * pairs, LANES), jnp.float32),
            pltpu.VMEM((pairs * count, LANES), jnp.float32),
            pltpu.SemaphoreType.DMA((3,)),
        ],
        compiler_params=pltpu.CompilerParams(vmem_limit_bytes=8 * 2**20),
        cost_estimate=pl.CostEstimate(flops=2**27, bytes_accessed=2**19, transcendentals=0),
        name="condition_other" if other else "condition_mine",
    )(*(pltpu.with_memory_space_constraint(x, pltpu.HBM) for x in (queries, left_factor, right_factor)))


def along_columns(value, step):
    pairs = [
        (((k + step) % COLUMNS) * PAIR + c, k * PAIR + c)
        for k in range(COLUMNS)
        for c in range(PAIR)
    ]
    return lax.ppermute(value, "train", pairs)


def other_core(value):
    return lax.ppermute(value, "train", [(k, k ^ 1) for k in range(COLUMNS * PAIR)])


def other_part(value):
    return lax.ppermute(value, "parts", [(0, 1), (1, 0)])


def copy_kernel(source, target, done):
    copy = pltpu.make_async_copy(source, target, done)
    copy.start()
    copy.wait()


def copy_near(value):
    return pl.pallas_call(
        copy_kernel,
        out_shape=jax.ShapeDtypeStruct(value.shape, value.dtype),
        in_specs=[pl.BlockSpec(memory_space=pltpu.HBM)],
        out_specs=pl.BlockSpec(memory_space=pltpu.VMEM),
        scratch_shapes=[pltpu.SemaphoreType.DMA],
        compiler_params=pltpu.CompilerParams(vmem_limit_bytes=6 * 2**20),
        cost_estimate=pl.CostEstimate(flops=0, bytes_accessed=2 * value.size * 2, transcendentals=0),
        name="near",
    )(pltpu.with_memory_space_constraint(value, pltpu.HBM))


def place():
    member = lax.axis_index("train")
    return member // PAIR, lax.rem(member, PAIR)


def row_scores(train, table, owner, terms, scores):
    share = scores.shape[0]
    rows, layer_count, width = train.shape
    queries = table.shape[1]
    first = pl.multiple_of(owner * share * layer_count, share * layer_count)
    both = lax.dot_general(
        train.reshape(rows * layer_count, width)[pl.ds(first, share * layer_count), :],
        table[...].reshape(layer_count * queries, width),
        LANES_LAST,
        preferred_element_type=jnp.float32,
    )
    for layer in range(layer_count):
        terms[layer] = both[:, layer * queries : (layer + 1) * queries]
    scores[...] = sum(terms[layer, pl.ds(layer, share, stride=layer_count), :] for layer in range(layer_count))


def sent_kernel(train, *refs):
    blocks, (scores, table, terms) = refs[:-3], refs[-3:]
    part = lax.axis_index("parts")
    column, core = place()
    count = blocks[0].shape[0]

    def put(layer, step, twin, block):
        member = lax.rem(column + step, COLUMNS) * PAIR + (1 - core if twin else core)
        table[layer, pl.ds(pl.multiple_of(member * count, count), count), :] = block

    for twin in range(PAIR):
        for k, (layer, step) in enumerate(
            ((part, 0), (1 - part, 0), (part, 2), (part, 1), (part, 3), (1 - part, 2), (1 - part, 1), (1 - part, 3))
        ):
            put(layer, step, twin, blocks[PAIR * k + twin][...])
    row_scores(train, table, 1 - lax.axis_index("layer"), terms, scores)


def kept_kernel(train, table, scores, terms):
    row_scores(train, table, lax.axis_index("layer"), terms, scores)


def local_call(kernel, name, out_shape, scratch_shapes, *operands):
    spec = pl.BlockSpec(memory_space=pltpu.VMEM)
    return pl.pallas_call(
        kernel,
        out_shape=out_shape,
        in_specs=[spec] * len(operands),
        out_specs=jax.tree.map(lambda _: spec, out_shape),
        scratch_shapes=scratch_shapes,
        compiler_params=pltpu.CompilerParams(vmem_limit_bytes=24 * 2**20),
        cost_estimate=pl.CostEstimate(flops=2**29, bytes_accessed=2**22, transcendentals=0),
        name=name,
    )(*operands)


def direct(train_grads, queries, left_factor, right_factor):
    rows, layer_count, width = train_grads.shape
    count = queries.shape[2]
    total = count * COLUMNS * PAIR
    share = rows // 2

    mine = condition_layer(False, queries, left_factor, right_factor)
    other = condition_layer(True, queries, left_factor, right_factor)
    near = copy_near(train_grads)
    mine_late, other = lax.optimization_barrier((mine, other))
    s2 = along_columns(mine_late, 2)
    s1 = along_columns(mine, 1)
    s3 = along_columns(mine, 3)
    y2 = other_part(s2)
    y1 = other_part(s1)
    y3 = other_part(s3)
    y1, y3, near = lax.optimization_barrier((y1, y3, near))

    blocks = []
    for block in (mine, other, s2, s1, s3, y2, y1, y3):
        blocks += [block, other_core(block)]
    f32 = functools.partial(jax.ShapeDtypeStruct, dtype=jnp.float32)
    terms = [pltpu.VMEM((layer_count, share * layer_count, total), jnp.float32)]
    sent, table = local_call(
        sent_kernel,
        "scores_sent",
        [f32((share, total)), jax.ShapeDtypeStruct((layer_count, total, width), jnp.bfloat16)],
        terms,
        near,
        *blocks,
    )
    received = lax.ppermute(sent, "layer", [(0, 1), (1, 0)])
    kept = local_call(kept_kernel, "scores_kept", f32((share, total)), terms, near, table)
    return kept + received


def general(shape, train_grads, queries, left_factor, right_factor):
    layers = shape["layer"]
    own = condition(queries[:, 0], left_factor, right_factor)
    block = lax.all_gather(own, "train", axis=1, tiled=True)
    share = train_grads.shape[0] // layers
    here = lax.axis_index("layer")

    def terms(step):
        rows = lax.dynamic_slice_in_dim(train_grads, (here + step) % layers * share, share, 0)
        return jnp.einsum("fkm,krm->fr", rows, block, preferred_element_type=jnp.float32)

    scores = terms(0)
    for step in range(1, layers):
        scores += lax.ppermute(terms(step), "layer", [(k, (k + step) % layers) for k in range(layers)])
    return scores


def body(shape, train_grads, queries, left_factor, right_factor):
    fits = (
        shape["train"] == COLUMNS * PAIR
        and shape["parts"] == shape["layer"] == 2
        and shape["query"] == 1
        and train_grads.shape[0] == 2 * LANES
        and train_grads.shape[1:] == (2, 4096)
        and queries.shape[1:] == (1, 16, 4096)
        and left_factor.shape[1:] == right_factor.shape[1:] == (64, 64)
    )
    if fits:
        return direct(train_grads, queries, left_factor, right_factor)
    return general(shape, train_grads, queries, left_factor, right_factor)


def solution(mesh):
    return jax.shard_map(
        functools.partial(body, dict(mesh.shape)),
        mesh=mesh,
        in_specs=(
            P(("parts", "train"), "layer", None),
            P("layer", "query", "train", None),
            P("layer", None, None),
            P("layer", None, None),
        ),
        out_specs=P(("parts", "train", "layer"), "query"),
        check_vma=False,
    )
```

```python
import functools

import jax
import jax.numpy as jnp
from jax import lax
from jax.experimental import pallas as pl
from jax.experimental.pallas import tpu as pltpu
from jax.sharding import PartitionSpec as P

LANES = 128
PAIR = 2
COLUMNS = 4
LANES_LAST = (((1,), (1,)), ((), ()))


def split(value, parts):
    pieces = []
    for _ in range(parts):
        piece = value.astype(jnp.bfloat16)
        pieces.append(piece)
        value = value - piece.astype(jnp.float32)
    return pieces


def condition(own, left_factor, right_factor):
    layer_count, count, width = own.shape
    rows_out, rows_in = left_factor.shape[1], right_factor.shape[1]
    grid = own.astype(jnp.float32).reshape(layer_count, count, rows_out, rows_in)
    left_part = jnp.einsum("lab,lnbc->lnac", left_factor, grid, precision=lax.Precision.HIGHEST)
    both = jnp.einsum("lnac,lcd->lnad", left_part, right_factor, precision=lax.Precision.HIGHEST)
    return both.reshape(layer_count, count, width).astype(jnp.bfloat16)


def condition_block(block, left, right, put, spread, stacked, placed):
    count, width = block.shape
    inner = right.shape[0]
    pairs = width // LANES
    first_half = lax.broadcasted_iota(jnp.int32, (pairs, LANES), 1) < inner

    empty = jnp.zeros((inner, LANES), jnp.float32)
    twice = jnp.concatenate([right, right], axis=1)
    weight = jnp.concatenate(
        [jnp.concatenate([twice, empty], axis=1), jnp.concatenate([empty, twice], axis=1)], axis=0
    )
    high, middle, low = split(weight, 3)
    rows = jnp.concatenate([block[:, k * LANES : (k + 1) * LANES] for k in range(pairs)], axis=0)
    right_part = jnp.dot(
        jnp.concatenate([rows, rows], axis=1),
        jnp.concatenate([high, middle], axis=0),
        preferred_element_type=jnp.float32,
    ) + jnp.dot(rows, low, preferred_element_type=jnp.float32)
    spread[0] = right_part[:, :LANES]
    spread[1] = right_part[:, LANES:]

    for q in range(0, count, 2):
        for j in range(2):
            even = spread[j, pl.ds(q, pairs, stride=count), :]
            odd = spread[j, pl.ds(q + 1, pairs, stride=count), :]
            stacked[q // 2, pl.ds(j, pairs, stride=2), :] = jnp.where(first_half, even, odd)

    left_high, left_low = split(left, 2)
    moved = jnp.concatenate([stacked[k] for k in range(count // 2)], axis=1)
    moved_high, moved_low = split(moved, 2)
    done = jnp.dot(
        jnp.concatenate([left_high, left_high, left_low], axis=1),
        jnp.concatenate([moved_high, moved_low, moved_high], axis=0),
        preferred_element_type=jnp.float32,
    )
    for k in range(count // 2):
        stacked[k] = done[:, k * LANES : (k + 1) * LANES]

    for q in range(0, count, 2):
        upper = stacked[q // 2, pl.ds(0, pairs, stride=2), :]
        lower = stacked[q // 2, pl.ds(1, pairs, stride=2), :]
        placed[pl.ds(q, pairs, stride=count), :] = jnp.where(first_half, upper, pltpu.roll(lower, inner, 1))
        placed[pl.ds(q + 1, pairs, stride=count), :] = jnp.where(
            first_half, pltpu.roll(upper, inner, 1), lower
        )
    for k in range(pairs):
        put(k, placed[k * count : (k + 1) * count, :].astype(jnp.bfloat16))


def condition_kernel(other, *refs):
    if other:
        queries, left, right, train, out, near, *scratch, near_arrived = refs
        near_copy = pltpu.make_async_copy(train, near, near_arrived)
    else:
        queries, left, right, out, *scratch = refs
    block_in, left_in, right_in, spread, stacked, placed, arrived = scratch
    part = lax.axis_index("parts")
    layer = 1 - part if other else part
    copies = [
        pltpu.make_async_copy(source, target, arrived.at[k])
        for k, (source, target) in enumerate(
            ((queries.at[layer, 0], block_in), (right.at[layer], right_in), (left.at[layer], left_in))
        )
    ]
    for copy in copies:
        copy.start()
    if other:
        near_copy.start()
    for copy in copies:
        copy.wait()

    def put(k, tile):
        out[:, k * LANES : (k + 1) * LANES] = tile

    condition_block(block_in[...], left_in[...], right_in[...], put, spread, stacked, placed)
    if other:
        near_copy.wait()


def condition_layer(other, queries, left_factor, right_factor, *train):
    _, _, count, width = queries.shape
    pairs = width // LANES
    far = pl.BlockSpec(memory_space=pltpu.HBM)
    return pl.pallas_call(
        functools.partial(condition_kernel, other),
        out_shape=[jax.ShapeDtypeStruct(shape, jnp.bfloat16) for shape in ((count, width), *(x.shape for x in train))],
        in_specs=[far] * (3 + len(train)),
        out_specs=[pl.BlockSpec(memory_space=pltpu.VMEM)] * (1 + len(train)),
        scratch_shapes=[
            pltpu.VMEM((count, width), jnp.bfloat16),
            pltpu.VMEM(left_factor.shape[1:], jnp.float32),
            pltpu.VMEM(right_factor.shape[1:], jnp.float32),
            pltpu.VMEM((2, pairs * count, LANES), jnp.float32),
            pltpu.VMEM((count // 2, 2 * pairs, LANES), jnp.float32),
            pltpu.VMEM((pairs * count, LANES), jnp.float32),
            pltpu.SemaphoreType.DMA((3,)),
            *(pltpu.SemaphoreType.DMA for _ in train),
        ],
        compiler_params=pltpu.CompilerParams(vmem_limit_bytes=12 * 2**20),
        cost_estimate=pl.CostEstimate(flops=2**27, bytes_accessed=2**19, transcendentals=0),
        name="condition_other" if other else "condition_mine",
    )(*(pltpu.with_memory_space_constraint(x, pltpu.HBM) for x in (queries, left_factor, right_factor, *train)))


def along_columns(value, step):
    pairs = [
        (((k + step) % COLUMNS) * PAIR + c, k * PAIR + c)
        for k in range(COLUMNS)
        for c in range(PAIR)
    ]
    return lax.ppermute(value, "train", pairs)


def relay(value):
    pairs = [
        (a * PAIR + c, b * PAIR + c) for a, b in ((0, 2), (2, 3), (3, 1), (1, 0)) for c in range(PAIR)
    ]
    return lax.ppermute(value, "train", pairs)


def other_core(value):
    return lax.ppermute(value, "train", [(k, k ^ 1) for k in range(COLUMNS * PAIR)])


def other_part(value):
    return lax.ppermute(value, "parts", [(0, 1), (1, 0)])


def place():
    member = lax.axis_index("train")
    return member // PAIR, lax.rem(member, PAIR)


def row_scores(train, table, owner, terms, scores):
    share = scores.shape[0]
    rows, layer_count, width = train.shape
    queries = table.shape[1]
    first = pl.multiple_of(owner * share * layer_count, share * layer_count)
    both = lax.dot_general(
        train.reshape(rows * layer_count, width)[pl.ds(first, share * layer_count), :],
        table[...].reshape(layer_count * queries, width),
        LANES_LAST,
        preferred_element_type=jnp.float32,
    )
    for layer in range(layer_count):
        terms[layer] = both[:, layer * queries : (layer + 1) * queries]
    scores[...] = sum(terms[layer, pl.ds(layer, share, stride=layer_count), :] for layer in range(layer_count))


def sent_kernel(train, *refs):
    blocks, (scores, table, terms) = refs[:-3], refs[-3:]
    part = lax.axis_index("parts")
    column, core = place()
    count = blocks[0].shape[0]

    def put(layer, step, twin, block, lane=0):
        member = lax.rem(column + step, COLUMNS) * PAIR + (1 - core if twin else core)
        table[layer, pl.ds(pl.multiple_of(member * count, count), count), lane : lane + block.shape[1]] = block

    far = table.shape[2] // 2
    for twin in range(PAIR):
        for k, (layer, step, lane) in enumerate(
            (
                (part, 0, 0),
                (1 - part, 0, 0),
                (part, 2, far),
                (part, 2, 0),
                (part, 1, 0),
                (part, 3, 0),
                (1 - part, 2, far),
                (1 - part, 2, 0),
                (1 - part, 1, 0),
                (1 - part, 3, 0),
            )
        ):
            put(layer, step, twin, blocks[PAIR * k + twin][...], lane)
    row_scores(train, table, 1 - lax.axis_index("layer"), terms, scores)


def kept_kernel(train, table, scores, terms):
    row_scores(train, table, lax.axis_index("layer"), terms, scores)


def local_call(kernel, name, out_shape, scratch_shapes, *operands):
    spec = pl.BlockSpec(memory_space=pltpu.VMEM)
    return pl.pallas_call(
        kernel,
        out_shape=out_shape,
        in_specs=[spec] * len(operands),
        out_specs=jax.tree.map(lambda _: spec, out_shape),
        scratch_shapes=scratch_shapes,
        compiler_params=pltpu.CompilerParams(vmem_limit_bytes=24 * 2**20),
        cost_estimate=pl.CostEstimate(flops=2**29, bytes_accessed=2**22, transcendentals=0),
        name=name,
    )(*operands)


def direct(train_grads, queries, left_factor, right_factor):
    rows, layer_count, width = train_grads.shape
    count = queries.shape[2]
    total = count * COLUMNS * PAIR
    share = rows // 2

    (mine,) = condition_layer(False, queries, left_factor, right_factor)
    other, near = condition_layer(True, queries, left_factor, right_factor, train_grads)
    half = width // 2
    column, _ = place()
    mine_late, other = lax.optimization_barrier((mine, other))
    s2a = along_columns(mine_late[:, :half], 2)
    s1 = along_columns(mine, 1)
    s3 = along_columns(mine, 3)
    passed = jnp.where(column == 1, s1[:, half:], jnp.where(column == 2, s3[:, half:], mine[:, half:]))
    s2b = relay(passed)
    y1 = other_part(s1)
    y3 = other_part(s3)
    s2a, s2b = lax.optimization_barrier((s2a, s2b))
    y2a = other_part(s2a)
    y2b = other_part(s2b)

    blocks = []
    for block in (mine, other, s2b, s2a, s1, s3, y2b, y2a, y1, y3):
        blocks += [block, other_core(block)]
    f32 = functools.partial(jax.ShapeDtypeStruct, dtype=jnp.float32)
    terms = [pltpu.VMEM((layer_count, share * layer_count, total), jnp.float32)]
    sent, table = local_call(
        sent_kernel,
        "scores_sent",
        [f32((share, total)), jax.ShapeDtypeStruct((layer_count, total, width), jnp.bfloat16)],
        terms,
        near,
        *blocks,
    )
    received = lax.ppermute(sent, "layer", [(0, 1), (1, 0)])
    kept = local_call(kept_kernel, "scores_kept", f32((share, total)), terms, near, table)
    return kept + received


def general(shape, train_grads, queries, left_factor, right_factor):
    layers = shape["layer"]
    own = condition(queries[:, 0], left_factor, right_factor)
    block = lax.all_gather(own, "train", axis=1, tiled=True)
    share = train_grads.shape[0] // layers
    here = lax.axis_index("layer")

    def terms(step):
        rows = lax.dynamic_slice_in_dim(train_grads, (here + step) % layers * share, share, 0)
        return jnp.einsum("fkm,krm->fr", rows, block, preferred_element_type=jnp.float32)

    scores = terms(0)
    for step in range(1, layers):
        scores += lax.ppermute(terms(step), "layer", [(k, (k + step) % layers) for k in range(layers)])
    return scores


def body(shape, train_grads, queries, left_factor, right_factor):
    fits = (
        shape["train"] == COLUMNS * PAIR
        and shape["parts"] == shape["layer"] == 2
        and shape["query"] == 1
        and train_grads.shape[0] == 2 * LANES
        and train_grads.shape[1:] == (2, 4096)
        and queries.shape[1:] == (1, 16, 4096)
        and left_factor.shape[1:] == right_factor.shape[1:] == (64, 64)
    )
    if fits:
        return direct(train_grads, queries, left_factor, right_factor)
    return general(shape, train_grads, queries, left_factor, right_factor)


def solution(mesh):
    return jax.shard_map(
        functools.partial(body, dict(mesh.shape)),
        mesh=mesh,
        in_specs=(
            P(("parts", "train"), "layer", None),
            P("layer", "query", "train", None),
            P("layer", None, None),
            P("layer", None, None),
        ),
        out_specs=P(("parts", "train", "layer"), "query"),
        check_vma=False,
    )
```

```python
import functools

import jax
import jax.numpy as jnp
from jax import lax
from jax.experimental import pallas as pl
from jax.experimental.pallas import tpu as pltpu
from jax.sharding import PartitionSpec as P

LANES = 128
PAIR = 2
COLUMNS = 4
LANES_LAST = (((1,), (1,)), ((), ()))


def split(value, parts):
    pieces = []
    for _ in range(parts):
        piece = value.astype(jnp.bfloat16)
        pieces.append(piece)
        value = value - piece.astype(jnp.float32)
    return pieces


def condition(own, left_factor, right_factor):
    layer_count, count, width = own.shape
    rows_out, rows_in = left_factor.shape[1], right_factor.shape[1]
    grid = own.astype(jnp.float32).reshape(layer_count, count, rows_out, rows_in)
    left_part = jnp.einsum("lab,lnbc->lnac", left_factor, grid, precision=lax.Precision.HIGHEST)
    both = jnp.einsum("lnac,lcd->lnad", left_part, right_factor, precision=lax.Precision.HIGHEST)
    return both.reshape(layer_count, count, width).astype(jnp.bfloat16)


def condition_block(block, left, right, put, spread, stacked, placed):
    count, width = block.shape
    inner = right.shape[0]
    pairs = width // LANES
    first_half = lax.broadcasted_iota(jnp.int32, (pairs, LANES), 1) < inner

    empty = jnp.zeros((inner, LANES), jnp.float32)
    twice = jnp.concatenate([right, right], axis=1)
    weight = jnp.concatenate(
        [jnp.concatenate([twice, empty], axis=1), jnp.concatenate([empty, twice], axis=1)], axis=0
    )
    high, middle, low = split(weight, 3)
    rows = jnp.concatenate([block[:, k * LANES : (k + 1) * LANES] for k in range(pairs)], axis=0)
    right_part = jnp.dot(
        jnp.concatenate([rows, rows], axis=1),
        jnp.concatenate([high, middle], axis=0),
        preferred_element_type=jnp.float32,
    ) + jnp.dot(rows, low, preferred_element_type=jnp.float32)
    spread[0] = right_part[:, :LANES]
    spread[1] = right_part[:, LANES:]

    for q in range(0, count, 2):
        for j in range(2):
            even = spread[j, pl.ds(q, pairs, stride=count), :]
            odd = spread[j, pl.ds(q + 1, pairs, stride=count), :]
            stacked[q // 2, pl.ds(j, pairs, stride=2), :] = jnp.where(first_half, even, odd)

    left_high, left_low = split(left, 2)
    moved = jnp.concatenate([stacked[k] for k in range(count // 2)], axis=1)
    moved_high, moved_low = split(moved, 2)
    done = jnp.dot(
        jnp.concatenate([left_high, left_high, left_low], axis=1),
        jnp.concatenate([moved_high, moved_low, moved_high], axis=0),
        preferred_element_type=jnp.float32,
    )
    for k in range(count // 2):
        stacked[k] = done[:, k * LANES : (k + 1) * LANES]

    for q in range(0, count, 2):
        upper = stacked[q // 2, pl.ds(0, pairs, stride=2), :]
        lower = stacked[q // 2, pl.ds(1, pairs, stride=2), :]
        placed[pl.ds(q, pairs, stride=count), :] = jnp.where(first_half, upper, pltpu.roll(lower, inner, 1))
        placed[pl.ds(q + 1, pairs, stride=count), :] = jnp.where(
            first_half, pltpu.roll(upper, inner, 1), lower
        )
    for k in range(pairs):
        put(k, placed[k * count : (k + 1) * count, :].astype(jnp.bfloat16))


def condition_kernel(other, queries, left, right, out, block_in, left_in, right_in, spread, stacked, placed, arrived):
    part = lax.axis_index("parts")
    layer = 1 - part if other else part
    copies = [
        pltpu.make_async_copy(source, target, arrived.at[k])
        for k, (source, target) in enumerate(
            ((queries.at[layer, 0], block_in), (right.at[layer], right_in), (left.at[layer], left_in))
        )
    ]
    for copy in copies:
        copy.start()
    for copy in copies:
        copy.wait()

    def put(k, tile):
        out[:, k * LANES : (k + 1) * LANES] = tile

    condition_block(block_in[...], left_in[...], right_in[...], put, spread, stacked, placed)


def condition_layer(other, queries, left_factor, right_factor):
    _, _, count, width = queries.shape
    pairs = width // LANES
    far = pl.BlockSpec(memory_space=pltpu.HBM)
    return pl.pallas_call(
        functools.partial(condition_kernel, other),
        out_shape=jax.ShapeDtypeStruct((count, width), jnp.bfloat16),
        in_specs=[far] * 3,
        out_specs=pl.BlockSpec(memory_space=pltpu.VMEM),
        scratch_shapes=[
            pltpu.VMEM((count, width), jnp.bfloat16),
            pltpu.VMEM(left_factor.shape[1:], jnp.float32),
            pltpu.VMEM(right_factor.shape[1:], jnp.float32),
            pltpu.VMEM((2, pairs * count, LANES), jnp.float32),
            pltpu.VMEM((count // 2, 2 * pairs, LANES), jnp.float32),
            pltpu.VMEM((pairs * count, LANES), jnp.float32),
            pltpu.SemaphoreType.DMA((3,)),
        ],
        compiler_params=pltpu.CompilerParams(vmem_limit_bytes=8 * 2**20),
        cost_estimate=pl.CostEstimate(flops=2**27, bytes_accessed=2**19, transcendentals=0),
        name="condition_other" if other else "condition_mine",
    )(*(pltpu.with_memory_space_constraint(x, pltpu.HBM) for x in (queries, left_factor, right_factor)))


def along_columns(value, step):
    pairs = [
        (((k + step) % COLUMNS) * PAIR + c, k * PAIR + c)
        for k in range(COLUMNS)
        for c in range(PAIR)
    ]
    return lax.ppermute(value, "train", pairs)


def relay(value):
    pairs = [
        (a * PAIR + c, b * PAIR + c) for a, b in ((0, 2), (2, 3), (3, 1), (1, 0)) for c in range(PAIR)
    ]
    return lax.ppermute(value, "train", pairs)


def other_core(value):
    return lax.ppermute(value, "train", [(k, k ^ 1) for k in range(COLUMNS * PAIR)])


def other_part(value):
    return lax.ppermute(value, "parts", [(0, 1), (1, 0)])


def copy_kernel(source, target, done):
    copy = pltpu.make_async_copy(source, target, done)
    copy.start()
    copy.wait()


def copy_near(value):
    return pl.pallas_call(
        copy_kernel,
        out_shape=jax.ShapeDtypeStruct(value.shape, value.dtype),
        in_specs=[pl.BlockSpec(memory_space=pltpu.HBM)],
        out_specs=pl.BlockSpec(memory_space=pltpu.VMEM),
        scratch_shapes=[pltpu.SemaphoreType.DMA],
        compiler_params=pltpu.CompilerParams(vmem_limit_bytes=6 * 2**20),
        cost_estimate=pl.CostEstimate(flops=0, bytes_accessed=2 * value.size * 2, transcendentals=0),
        name="near",
    )(pltpu.with_memory_space_constraint(value, pltpu.HBM))


def place():
    member = lax.axis_index("train")
    return member // PAIR, lax.rem(member, PAIR)


def row_scores(train, table, owner, terms, scores):
    share = scores.shape[0]
    rows, layer_count, width = train.shape
    queries = table.shape[1]
    first = pl.multiple_of(owner * share * layer_count, share * layer_count)
    both = lax.dot_general(
        train.reshape(rows * layer_count, width)[pl.ds(first, share * layer_count), :],
        table[...].reshape(layer_count * queries, width),
        LANES_LAST,
        preferred_element_type=jnp.float32,
    )
    for layer in range(layer_count):
        terms[layer] = both[:, layer * queries : (layer + 1) * queries]
    scores[...] = sum(terms[layer, pl.ds(layer, share, stride=layer_count), :] for layer in range(layer_count))


def sent_kernel(train, *refs):
    blocks, (scores, table, terms) = refs[:-3], refs[-3:]
    part = lax.axis_index("parts")
    column, core = place()
    count = blocks[0].shape[0]

    def put(layer, step, twin, block):
        member = lax.rem(column + step, COLUMNS) * PAIR + (1 - core if twin else core)
        table[layer, pl.ds(pl.multiple_of(member * count, count), count), :] = block

    for twin in range(PAIR):
        for k, (layer, step) in enumerate(
            ((part, 0), (1 - part, 0), (part, 2), (part, 1), (part, 3), (1 - part, 2), (1 - part, 1), (1 - part, 3))
        ):
            put(layer, step, twin, blocks[PAIR * k + twin][...])
    row_scores(train, table, 1 - lax.axis_index("layer"), terms, scores)


def kept_kernel(train, table, scores, terms):
    row_scores(train, table, lax.axis_index("layer"), terms, scores)


def local_call(kernel, name, out_shape, scratch_shapes, *operands):
    spec = pl.BlockSpec(memory_space=pltpu.VMEM)
    return pl.pallas_call(
        kernel,
        out_shape=out_shape,
        in_specs=[spec] * len(operands),
        out_specs=jax.tree.map(lambda _: spec, out_shape),
        scratch_shapes=scratch_shapes,
        compiler_params=pltpu.CompilerParams(vmem_limit_bytes=24 * 2**20),
        cost_estimate=pl.CostEstimate(flops=2**29, bytes_accessed=2**22, transcendentals=0),
        name=name,
    )(*operands)


def direct(train_grads, queries, left_factor, right_factor):
    rows, layer_count, width = train_grads.shape
    count = queries.shape[2]
    total = count * COLUMNS * PAIR
    share = rows // 2

    mine = condition_layer(False, queries, left_factor, right_factor)
    other = condition_layer(True, queries, left_factor, right_factor)
    near = copy_near(train_grads)
    column, _ = place()
    s1 = along_columns(mine, 1)
    s3 = along_columns(mine, 3)
    s3, other = lax.optimization_barrier((s3, other))
    s2 = relay(jnp.where(column == 1, s1, jnp.where(column == 2, s3, mine)))
    y1 = other_part(s1)
    y3 = other_part(s3)
    y2 = other_part(s2)
    y1, y3, near = lax.optimization_barrier((y1, y3, near))

    blocks = []
    for block in (mine, other, s2, s1, s3, y2, y1, y3):
        blocks += [block, other_core(block)]
    f32 = functools.partial(jax.ShapeDtypeStruct, dtype=jnp.float32)
    terms = [pltpu.VMEM((layer_count, share * layer_count, total), jnp.float32)]
    sent, table = local_call(
        sent_kernel,
        "scores_sent",
        [f32((share, total)), jax.ShapeDtypeStruct((layer_count, total, width), jnp.bfloat16)],
        terms,
        near,
        *blocks,
    )
    received = lax.ppermute(sent, "layer", [(0, 1), (1, 0)])
    kept = local_call(kept_kernel, "scores_kept", f32((share, total)), terms, near, table)
    return kept + received


def general(shape, train_grads, queries, left_factor, right_factor):
    layers = shape["layer"]
    own = condition(queries[:, 0], left_factor, right_factor)
    block = lax.all_gather(own, "train", axis=1, tiled=True)
    share = train_grads.shape[0] // layers
    here = lax.axis_index("layer")

    def terms(step):
        rows = lax.dynamic_slice_in_dim(train_grads, (here + step) % layers * share, share, 0)
        return jnp.einsum("fkm,krm->fr", rows, block, preferred_element_type=jnp.float32)

    scores = terms(0)
    for step in range(1, layers):
        scores += lax.ppermute(terms(step), "layer", [(k, (k + step) % layers) for k in range(layers)])
    return scores


def body(shape, train_grads, queries, left_factor, right_factor):
    fits = (
        shape["train"] == COLUMNS * PAIR
        and shape["parts"] == shape["layer"] == 2
        and shape["query"] == 1
        and train_grads.shape[0] == 2 * LANES
        and train_grads.shape[1:] == (2, 4096)
        and queries.shape[1:] == (1, 16, 4096)
        and left_factor.shape[1:] == right_factor.shape[1:] == (64, 64)
    )
    if fits:
        return direct(train_grads, queries, left_factor, right_factor)
    return general(shape, train_grads, queries, left_factor, right_factor)


def solution(mesh):
    return jax.shard_map(
        functools.partial(body, dict(mesh.shape)),
        mesh=mesh,
        in_specs=(
            P(("parts", "train"), "layer", None),
            P("layer", "query", "train", None),
            P("layer", None, None),
            P("layer", None, None),
        ),
        out_specs=P(("parts", "train", "layer"), "query"),
        check_vma=False,
    )
```

```python
import functools

import jax
import jax.numpy as jnp
from jax import lax
from jax.experimental import pallas as pl
from jax.experimental.pallas import tpu as pltpu
from jax.sharding import PartitionSpec as P

LANES = 128
PAIR = 2
COLUMNS = 4
LANES_LAST = (((1,), (1,)), ((), ()))


def split(value, parts):
    pieces = []
    for _ in range(parts):
        piece = value.astype(jnp.bfloat16)
        pieces.append(piece)
        value = value - piece.astype(jnp.float32)
    return pieces


def condition(own, left_factor, right_factor):
    layer_count, count, width = own.shape
    rows_out, rows_in = left_factor.shape[1], right_factor.shape[1]
    grid = own.astype(jnp.float32).reshape(layer_count, count, rows_out, rows_in)
    left_part = jnp.einsum("lab,lnbc->lnac", left_factor, grid, precision=lax.Precision.HIGHEST)
    both = jnp.einsum("lnac,lcd->lnad", left_part, right_factor, precision=lax.Precision.HIGHEST)
    return both.reshape(layer_count, count, width).astype(jnp.bfloat16)


def condition_block(block, left, right, put, spread, stacked, placed):
    count, width = block.shape
    inner = right.shape[0]
    pairs = width // LANES
    first_half = lax.broadcasted_iota(jnp.int32, (pairs, LANES), 1) < inner

    empty = jnp.zeros((inner, LANES), jnp.float32)
    twice = jnp.concatenate([right, right], axis=1)
    weight = jnp.concatenate(
        [jnp.concatenate([twice, empty], axis=1), jnp.concatenate([empty, twice], axis=1)], axis=0
    )
    high, middle, low = split(weight, 3)
    rows = jnp.concatenate([block[:, k * LANES : (k + 1) * LANES] for k in range(pairs)], axis=0)
    right_part = jnp.dot(
        jnp.concatenate([rows, rows], axis=1),
        jnp.concatenate([high, middle], axis=0),
        preferred_element_type=jnp.float32,
    ) + jnp.dot(rows, low, preferred_element_type=jnp.float32)
    spread[0] = right_part[:, :LANES]
    spread[1] = right_part[:, LANES:]

    for q in range(0, count, 2):
        for j in range(2):
            even = spread[j, pl.ds(q, pairs, stride=count), :]
            odd = spread[j, pl.ds(q + 1, pairs, stride=count), :]
            stacked[q // 2, pl.ds(j, pairs, stride=2), :] = jnp.where(first_half, even, odd)

    left_high, left_low = split(left, 2)
    moved = jnp.concatenate([stacked[k] for k in range(count // 2)], axis=1)
    moved_high, moved_low = split(moved, 2)
    done = jnp.dot(
        jnp.concatenate([left_high, left_high, left_low], axis=1),
        jnp.concatenate([moved_high, moved_low, moved_high], axis=0),
        preferred_element_type=jnp.float32,
    )
    for k in range(count // 2):
        stacked[k] = done[:, k * LANES : (k + 1) * LANES]

    for q in range(0, count, 2):
        upper = stacked[q // 2, pl.ds(0, pairs, stride=2), :]
        lower = stacked[q // 2, pl.ds(1, pairs, stride=2), :]
        placed[pl.ds(q, pairs, stride=count), :] = jnp.where(first_half, upper, pltpu.roll(lower, inner, 1))
        placed[pl.ds(q + 1, pairs, stride=count), :] = jnp.where(
            first_half, pltpu.roll(upper, inner, 1), lower
        )
    for k in range(pairs):
        put(k, placed[k * count : (k + 1) * count, :].astype(jnp.bfloat16))


def condition_kernel(other, queries, left, right, out, block_in, left_in, right_in, spread, stacked, placed, arrived):
    part = lax.axis_index("parts")
    layer = 1 - part if other else part
    copies = [
        pltpu.make_async_copy(source, target, arrived.at[k])
        for k, (source, target) in enumerate(
            ((queries.at[layer, 0], block_in), (right.at[layer], right_in), (left.at[layer], left_in))
        )
    ]
    for copy in copies:
        copy.start()
    for copy in copies:
        copy.wait()

    def put(k, tile):
        out[:, k * LANES : (k + 1) * LANES] = tile

    condition_block(block_in[...], left_in[...], right_in[...], put, spread, stacked, placed)


def condition_layer(other, queries, left_factor, right_factor):
    _, _, count, width = queries.shape
    pairs = width // LANES
    far = pl.BlockSpec(memory_space=pltpu.HBM)
    return pl.pallas_call(
        functools.partial(condition_kernel, other),
        out_shape=jax.ShapeDtypeStruct((count, width), jnp.bfloat16),
        in_specs=[far] * 3,
        out_specs=pl.BlockSpec(memory_space=pltpu.VMEM),
        scratch_shapes=[
            pltpu.VMEM((count, width), jnp.bfloat16),
            pltpu.VMEM(left_factor.shape[1:], jnp.float32),
            pltpu.VMEM(right_factor.shape[1:], jnp.float32),
            pltpu.VMEM((2, pairs * count, LANES), jnp.float32),
            pltpu.VMEM((count // 2, 2 * pairs, LANES), jnp.float32),
            pltpu.VMEM((pairs * count, LANES), jnp.float32),
            pltpu.SemaphoreType.DMA((3,)),
        ],
        compiler_params=pltpu.CompilerParams(vmem_limit_bytes=8 * 2**20),
        cost_estimate=pl.CostEstimate(flops=2**27, bytes_accessed=2**19, transcendentals=0),
        name="condition_other" if other else "condition_mine",
    )(*(pltpu.with_memory_space_constraint(x, pltpu.HBM) for x in (queries, left_factor, right_factor)))


def along_columns(value, step):
    pairs = [
        (((k + step) % COLUMNS) * PAIR + c, k * PAIR + c)
        for k in range(COLUMNS)
        for c in range(PAIR)
    ]
    return lax.ppermute(value, "train", pairs)


def relay(value):
    pairs = [
        (a * PAIR + c, b * PAIR + c) for a, b in ((0, 2), (2, 3), (3, 1), (1, 0)) for c in range(PAIR)
    ]
    return lax.ppermute(value, "train", pairs)


def other_core(value):
    return lax.ppermute(value, "train", [(k, k ^ 1) for k in range(COLUMNS * PAIR)])


def other_part(value):
    return lax.ppermute(value, "parts", [(0, 1), (1, 0)])


def copy_kernel(source, target, done):
    copy = pltpu.make_async_copy(source, target, done)
    copy.start()
    copy.wait()


def copy_near(value):
    return pl.pallas_call(
        copy_kernel,
        out_shape=jax.ShapeDtypeStruct(value.shape, value.dtype),
        in_specs=[pl.BlockSpec(memory_space=pltpu.HBM)],
        out_specs=pl.BlockSpec(memory_space=pltpu.VMEM),
        scratch_shapes=[pltpu.SemaphoreType.DMA],
        compiler_params=pltpu.CompilerParams(vmem_limit_bytes=6 * 2**20),
        cost_estimate=pl.CostEstimate(flops=0, bytes_accessed=2 * value.size * 2, transcendentals=0),
        name="near",
    )(pltpu.with_memory_space_constraint(value, pltpu.HBM))


def place():
    member = lax.axis_index("train")
    return member // PAIR, lax.rem(member, PAIR)


def row_scores(train, table, owner, terms, scores):
    share = scores.shape[0]
    rows, layer_count, width = train.shape
    queries = table.shape[1]
    first = pl.multiple_of(owner * share * layer_count, share * layer_count)
    both = lax.dot_general(
        train.reshape(rows * layer_count, width)[pl.ds(first, share * layer_count), :],
        table[...].reshape(layer_count * queries, width),
        LANES_LAST,
        preferred_element_type=jnp.float32,
    )
    for layer in range(layer_count):
        terms[layer] = both[:, layer * queries : (layer + 1) * queries]
    scores[...] = sum(terms[layer, pl.ds(layer, share, stride=layer_count), :] for layer in range(layer_count))


def sent_kernel(train, *refs):
    blocks, (scores, table, terms) = refs[:-3], refs[-3:]
    part = lax.axis_index("parts")
    column, core = place()
    count = blocks[0].shape[0]

    def put(layer, step, twin, block):
        member = lax.rem(column + step, COLUMNS) * PAIR + (1 - core if twin else core)
        table[layer, pl.ds(pl.multiple_of(member * count, count), count), :] = block

    for twin in range(PAIR):
        for k, (layer, step) in enumerate(
            ((part, 0), (1 - part, 0), (part, 2), (part, 1), (part, 3), (1 - part, 2), (1 - part, 1), (1 - part, 3))
        ):
            put(layer, step, twin, blocks[PAIR * k + twin][...])
    row_scores(train, table, 1 - lax.axis_index("layer"), terms, scores)


def kept_kernel(train, table, scores, terms):
    row_scores(train, table, lax.axis_index("layer"), terms, scores)


def local_call(kernel, name, out_shape, scratch_shapes, *operands):
    spec = pl.BlockSpec(memory_space=pltpu.VMEM)
    return pl.pallas_call(
        kernel,
        out_shape=out_shape,
        in_specs=[spec] * len(operands),
        out_specs=jax.tree.map(lambda _: spec, out_shape),
        scratch_shapes=scratch_shapes,
        compiler_params=pltpu.CompilerParams(vmem_limit_bytes=24 * 2**20),
        cost_estimate=pl.CostEstimate(flops=2**29, bytes_accessed=2**22, transcendentals=0),
        name=name,
    )(*operands)


def direct(train_grads, queries, left_factor, right_factor):
    rows, layer_count, width = train_grads.shape
    count = queries.shape[2]
    total = count * COLUMNS * PAIR
    share = rows // 2

    mine = condition_layer(False, queries, left_factor, right_factor)
    mine_c = other_core(mine)
    left_late, mine_c = lax.optimization_barrier((left_factor, mine_c))
    other = condition_layer(True, queries, left_late, right_factor)
    near = copy_near(train_grads)
    column, _ = place()
    s3 = along_columns(mine, 3)
    mine_late, other = lax.optimization_barrier((mine, other))
    s1 = along_columns(mine_late, 1)
    s2 = relay(jnp.where(column == 1, s1, jnp.where(column == 2, s3, mine)))
    y1 = other_part(s1)
    y3 = other_part(s3)
    s2, y3 = lax.optimization_barrier((s2, y3))
    y2 = other_part(s2)
    y1, near = lax.optimization_barrier((y1, near))

    blocks = [mine, mine_c]
    for block in (other, s2, s1, s3, y2, y1, y3):
        blocks += [block, other_core(block)]
    f32 = functools.partial(jax.ShapeDtypeStruct, dtype=jnp.float32)
    terms = [pltpu.VMEM((layer_count, share * layer_count, total), jnp.float32)]
    sent, table = local_call(
        sent_kernel,
        "scores_sent",
        [f32((share, total)), jax.ShapeDtypeStruct((layer_count, total, width), jnp.bfloat16)],
        terms,
        near,
        *blocks,
    )
    received = lax.ppermute(sent, "layer", [(0, 1), (1, 0)])
    kept = local_call(kept_kernel, "scores_kept", f32((share, total)), terms, near, table)
    return kept + received


def general(shape, train_grads, queries, left_factor, right_factor):
    layers = shape["layer"]
    own = condition(queries[:, 0], left_factor, right_factor)
    block = lax.all_gather(own, "train", axis=1, tiled=True)
    share = train_grads.shape[0] // layers
    here = lax.axis_index("layer")

    def terms(step):
        rows = lax.dynamic_slice_in_dim(train_grads, (here + step) % layers * share, share, 0)
        return jnp.einsum("fkm,krm->fr", rows, block, preferred_element_type=jnp.float32)

    scores = terms(0)
    for step in range(1, layers):
        scores += lax.ppermute(terms(step), "layer", [(k, (k + step) % layers) for k in range(layers)])
    return scores


def body(shape, train_grads, queries, left_factor, right_factor):
    fits = (
        shape["train"] == COLUMNS * PAIR
        and shape["parts"] == shape["layer"] == 2
        and shape["query"] == 1
        and train_grads.shape[0] == 2 * LANES
        and train_grads.shape[1:] == (2, 4096)
        and queries.shape[1:] == (1, 16, 4096)
        and left_factor.shape[1:] == right_factor.shape[1:] == (64, 64)
    )
    if fits:
        return direct(train_grads, queries, left_factor, right_factor)
    return general(shape, train_grads, queries, left_factor, right_factor)


def solution(mesh):
    return jax.shard_map(
        functools.partial(body, dict(mesh.shape)),
        mesh=mesh,
        in_specs=(
            P(("parts", "train"), "layer", None),
            P("layer", "query", "train", None),
            P("layer", None, None),
            P("layer", None, None),
        ),
        out_specs=P(("parts", "train", "layer"), "query"),
        check_vma=False,
    )
```

```python
import functools

import jax
import jax.numpy as jnp
from jax import lax
from jax.experimental import pallas as pl
from jax.experimental.pallas import tpu as pltpu
from jax.sharding import PartitionSpec as P

LANES = 128
PAIR = 2
COLUMNS = 4
LANES_LAST = (((1,), (1,)), ((), ()))


def split(value, parts):
    pieces = []
    for _ in range(parts):
        piece = value.astype(jnp.bfloat16)
        pieces.append(piece)
        value = value - piece.astype(jnp.float32)
    return pieces


def condition(own, left_factor, right_factor):
    layer_count, count, width = own.shape
    rows_out, rows_in = left_factor.shape[1], right_factor.shape[1]
    grid = own.astype(jnp.float32).reshape(layer_count, count, rows_out, rows_in)
    left_part = jnp.einsum("lab,lnbc->lnac", left_factor, grid, precision=lax.Precision.HIGHEST)
    both = jnp.einsum("lnac,lcd->lnad", left_part, right_factor, precision=lax.Precision.HIGHEST)
    return both.reshape(layer_count, count, width).astype(jnp.bfloat16)


def condition_block(block, left, right, put, spread, stacked, placed):
    count, width = block.shape
    inner = right.shape[0]
    pairs = width // LANES
    first_half = lax.broadcasted_iota(jnp.int32, (pairs, LANES), 1) < inner

    empty = jnp.zeros((inner, LANES), jnp.float32)
    twice = jnp.concatenate([right, right], axis=1)
    weight = jnp.concatenate(
        [jnp.concatenate([twice, empty], axis=1), jnp.concatenate([empty, twice], axis=1)], axis=0
    )
    high, middle, low = split(weight, 3)
    rows = jnp.concatenate([block[:, k * LANES : (k + 1) * LANES] for k in range(pairs)], axis=0)
    right_part = jnp.dot(
        jnp.concatenate([rows, rows], axis=1),
        jnp.concatenate([high, middle], axis=0),
        preferred_element_type=jnp.float32,
    ) + jnp.dot(rows, low, preferred_element_type=jnp.float32)
    spread[0] = right_part[:, :LANES]
    spread[1] = right_part[:, LANES:]

    for q in range(0, count, 2):
        for j in range(2):
            even = spread[j, pl.ds(q, pairs, stride=count), :]
            odd = spread[j, pl.ds(q + 1, pairs, stride=count), :]
            stacked[q // 2, pl.ds(j, pairs, stride=2), :] = jnp.where(first_half, even, odd)

    left_high, left_low = split(left, 2)
    moved = jnp.concatenate([stacked[k] for k in range(count // 2)], axis=1)
    moved_high, moved_low = split(moved, 2)
    done = jnp.dot(
        jnp.concatenate([left_high, left_high, left_low], axis=1),
        jnp.concatenate([moved_high, moved_low, moved_high], axis=0),
        preferred_element_type=jnp.float32,
    )
    for k in range(count // 2):
        stacked[k] = done[:, k * LANES : (k + 1) * LANES]

    for q in range(0, count, 2):
        upper = stacked[q // 2, pl.ds(0, pairs, stride=2), :]
        lower = stacked[q // 2, pl.ds(1, pairs, stride=2), :]
        placed[pl.ds(q, pairs, stride=count), :] = jnp.where(first_half, upper, pltpu.roll(lower, inner, 1))
        placed[pl.ds(q + 1, pairs, stride=count), :] = jnp.where(
            first_half, pltpu.roll(upper, inner, 1), lower
        )
    for k in range(pairs):
        put(k, placed[k * count : (k + 1) * count, :].astype(jnp.bfloat16))


def condition_kernel(other, queries, left, right, out, block_in, left_in, right_in, spread, stacked, placed, arrived):
    part = lax.axis_index("parts")
    layer = 1 - part if other else part
    copies = [
        pltpu.make_async_copy(source, target, arrived.at[k])
        for k, (source, target) in enumerate(
            ((queries.at[layer, 0], block_in), (right.at[layer], right_in), (left.at[layer], left_in))
        )
    ]
    for copy in copies:
        copy.start()
    for copy in copies:
        copy.wait()

    def put(k, tile):
        out[:, k * LANES : (k + 1) * LANES] = tile

    condition_block(block_in[...], left_in[...], right_in[...], put, spread, stacked, placed)


def condition_layer(other, queries, left_factor, right_factor):
    _, _, count, width = queries.shape
    pairs = width // LANES
    far = pl.BlockSpec(memory_space=pltpu.HBM)
    return pl.pallas_call(
        functools.partial(condition_kernel, other),
        out_shape=jax.ShapeDtypeStruct((count, width), jnp.bfloat16),
        in_specs=[far] * 3,
        out_specs=pl.BlockSpec(memory_space=pltpu.VMEM),
        scratch_shapes=[
            pltpu.VMEM((count, width), jnp.bfloat16),
            pltpu.VMEM(left_factor.shape[1:], jnp.float32),
            pltpu.VMEM(right_factor.shape[1:], jnp.float32),
            pltpu.VMEM((2, pairs * count, LANES), jnp.float32),
            pltpu.VMEM((count // 2, 2 * pairs, LANES), jnp.float32),
            pltpu.VMEM((pairs * count, LANES), jnp.float32),
            pltpu.SemaphoreType.DMA((3,)),
        ],
        compiler_params=pltpu.CompilerParams(vmem_limit_bytes=8 * 2**20),
        cost_estimate=pl.CostEstimate(flops=2**27, bytes_accessed=2**19, transcendentals=0),
        name="condition_other" if other else "condition_mine",
    )(*(pltpu.with_memory_space_constraint(x, pltpu.HBM) for x in (queries, left_factor, right_factor)))


def along_columns(value, step):
    pairs = [
        (((k + step) % COLUMNS) * PAIR + c, k * PAIR + c)
        for k in range(COLUMNS)
        for c in range(PAIR)
    ]
    return lax.ppermute(value, "train", pairs)


def relay(value):
    pairs = [
        (a * PAIR + c, b * PAIR + c) for a, b in ((0, 2), (2, 3), (3, 1), (1, 0)) for c in range(PAIR)
    ]
    return lax.ppermute(value, "train", pairs)


def other_core(value):
    return lax.ppermute(value, "train", [(k, k ^ 1) for k in range(COLUMNS * PAIR)])


def other_part(value):
    return lax.ppermute(value, "parts", [(0, 1), (1, 0)])


def copy_kernel(source, target, done):
    copy = pltpu.make_async_copy(source, target, done)
    copy.start()
    copy.wait()


def copy_near(value):
    return pl.pallas_call(
        copy_kernel,
        out_shape=jax.ShapeDtypeStruct(value.shape, value.dtype),
        in_specs=[pl.BlockSpec(memory_space=pltpu.HBM)],
        out_specs=pl.BlockSpec(memory_space=pltpu.VMEM),
        scratch_shapes=[pltpu.SemaphoreType.DMA],
        compiler_params=pltpu.CompilerParams(vmem_limit_bytes=6 * 2**20),
        cost_estimate=pl.CostEstimate(flops=0, bytes_accessed=2 * value.size * 2, transcendentals=0),
        name="near",
    )(pltpu.with_memory_space_constraint(value, pltpu.HBM))


def place():
    member = lax.axis_index("train")
    return member // PAIR, lax.rem(member, PAIR)


def row_scores(train, table, owner, terms, scores):
    share = scores.shape[0]
    rows, layer_count, width = train.shape
    queries = table.shape[1]
    first = pl.multiple_of(owner * share * layer_count, share * layer_count)
    both = lax.dot_general(
        train.reshape(rows * layer_count, width)[pl.ds(first, share * layer_count), :],
        table[...].reshape(layer_count * queries, width),
        LANES_LAST,
        preferred_element_type=jnp.float32,
    )
    for layer in range(layer_count):
        terms[layer] = both[:, layer * queries : (layer + 1) * queries]
    scores[...] = sum(terms[layer, pl.ds(layer, share, stride=layer_count), :] for layer in range(layer_count))


def sent_kernel(train, *refs):
    blocks, (scores, table, terms) = refs[:-3], refs[-3:]
    part = lax.axis_index("parts")
    column, core = place()
    count = blocks[0].shape[0]

    def put(layer, step, twin, block):
        member = lax.rem(column + step, COLUMNS) * PAIR + (1 - core if twin else core)
        table[layer, pl.ds(pl.multiple_of(member * count, count), count), :] = block

    for twin in range(PAIR):
        for k, (layer, step) in enumerate(
            ((part, 0), (1 - part, 0), (part, 2), (part, 1), (part, 3), (1 - part, 2), (1 - part, 1), (1 - part, 3))
        ):
            put(layer, step, twin, blocks[PAIR * k + twin][...])
    row_scores(train, table, 1 - lax.axis_index("layer"), terms, scores)


def kept_kernel(train, table, scores, terms):
    row_scores(train, table, lax.axis_index("layer"), terms, scores)


def local_call(kernel, name, out_shape, scratch_shapes, *operands):
    spec = pl.BlockSpec(memory_space=pltpu.VMEM)
    return pl.pallas_call(
        kernel,
        out_shape=out_shape,
        in_specs=[spec] * len(operands),
        out_specs=jax.tree.map(lambda _: spec, out_shape),
        scratch_shapes=scratch_shapes,
        compiler_params=pltpu.CompilerParams(vmem_limit_bytes=24 * 2**20),
        cost_estimate=pl.CostEstimate(flops=2**29, bytes_accessed=2**22, transcendentals=0),
        name=name,
    )(*operands)


def direct(train_grads, queries, left_factor, right_factor):
    rows, layer_count, width = train_grads.shape
    count = queries.shape[2]
    total = count * COLUMNS * PAIR
    share = rows // 2

    mine = condition_layer(False, queries, left_factor, right_factor)
    other = condition_layer(True, queries, left_factor, right_factor)
    near = copy_near(train_grads)
    column, _ = place()
    s1 = along_columns(mine, 1)
    s3 = along_columns(mine, 3)
    s1, s3, other = lax.optimization_barrier((s1, s3, other))
    s2 = relay(jnp.where(column == 1, s1, jnp.where(column == 2, s3, mine)))
    y1 = other_part(s1)
    y3 = other_part(s3)
    y2 = other_part(s2)
    y1, y3, _ = lax.optimization_barrier((y1, y3, s2))
    y2, near = lax.optimization_barrier((y2, near))

    blocks = []
    for block in (mine, other, s2, s1, s3, y2, y1, y3):
        blocks += [block, other_core(block)]
    f32 = functools.partial(jax.ShapeDtypeStruct, dtype=jnp.float32)
    terms = [pltpu.VMEM((layer_count, share * layer_count, total), jnp.float32)]
    sent, table = local_call(
        sent_kernel,
        "scores_sent",
        [f32((share, total)), jax.ShapeDtypeStruct((layer_count, total, width), jnp.bfloat16)],
        terms,
        near,
        *blocks,
    )
    received = lax.ppermute(sent, "layer", [(0, 1), (1, 0)])
    kept = local_call(kept_kernel, "scores_kept", f32((share, total)), terms, near, table)
    return kept + received


def general(shape, train_grads, queries, left_factor, right_factor):
    layers = shape["layer"]
    own = condition(queries[:, 0], left_factor, right_factor)
    block = lax.all_gather(own, "train", axis=1, tiled=True)
    share = train_grads.shape[0] // layers
    here = lax.axis_index("layer")

    def terms(step):
        rows = lax.dynamic_slice_in_dim(train_grads, (here + step) % layers * share, share, 0)
        return jnp.einsum("fkm,krm->fr", rows, block, preferred_element_type=jnp.float32)

    scores = terms(0)
    for step in range(1, layers):
        scores += lax.ppermute(terms(step), "layer", [(k, (k + step) % layers) for k in range(layers)])
    return scores


def body(shape, train_grads, queries, left_factor, right_factor):
    fits = (
        shape["train"] == COLUMNS * PAIR
        and shape["parts"] == shape["layer"] == 2
        and shape["query"] == 1
        and train_grads.shape[0] == 2 * LANES
        and train_grads.shape[1:] == (2, 4096)
        and queries.shape[1:] == (1, 16, 4096)
        and left_factor.shape[1:] == right_factor.shape[1:] == (64, 64)
    )
    if fits:
        return direct(train_grads, queries, left_factor, right_factor)
    return general(shape, train_grads, queries, left_factor, right_factor)


def solution(mesh):
    return jax.shard_map(
        functools.partial(body, dict(mesh.shape)),
        mesh=mesh,
        in_specs=(
            P(("parts", "train"), "layer", None),
            P("layer", "query", "train", None),
            P("layer", None, None),
            P("layer", None, None),
        ),
        out_specs=P(("parts", "train", "layer"), "query"),
        check_vma=False,
    )
```

```python
import functools

import jax
import jax.numpy as jnp
from jax import lax
from jax.experimental import pallas as pl
from jax.experimental.pallas import tpu as pltpu
from jax.sharding import PartitionSpec as P

LANES = 128
PAIR = 2
COLUMNS = 4
LANES_LAST = (((1,), (1,)), ((), ()))


def split(value, parts):
    pieces = []
    for _ in range(parts):
        piece = value.astype(jnp.bfloat16)
        pieces.append(piece)
        value = value - piece.astype(jnp.float32)
    return pieces


def condition(own, left_factor, right_factor):
    layer_count, count, width = own.shape
    rows_out, rows_in = left_factor.shape[1], right_factor.shape[1]
    grid = own.astype(jnp.float32).reshape(layer_count, count, rows_out, rows_in)
    left_part = jnp.einsum("lab,lnbc->lnac", left_factor, grid, precision=lax.Precision.HIGHEST)
    both = jnp.einsum("lnac,lcd->lnad", left_part, right_factor, precision=lax.Precision.HIGHEST)
    return both.reshape(layer_count, count, width).astype(jnp.bfloat16)


def condition_block(block, left, right, put, spread, stacked, placed):
    count, width = block.shape
    inner = right.shape[0]
    pairs = width // LANES
    first_half = lax.broadcasted_iota(jnp.int32, (pairs, LANES), 1) < inner

    empty = jnp.zeros((inner, LANES), jnp.float32)
    twice = jnp.concatenate([right, right], axis=1)
    weight = jnp.concatenate(
        [jnp.concatenate([twice, empty], axis=1), jnp.concatenate([empty, twice], axis=1)], axis=0
    )
    high, middle, low = split(weight, 3)
    rows = jnp.concatenate([block[:, k * LANES : (k + 1) * LANES] for k in range(pairs)], axis=0)
    right_part = jnp.dot(
        jnp.concatenate([rows, rows], axis=1),
        jnp.concatenate([high, middle], axis=0),
        preferred_element_type=jnp.float32,
    ) + jnp.dot(rows, low, preferred_element_type=jnp.float32)
    spread[0] = right_part[:, :LANES]
    spread[1] = right_part[:, LANES:]

    for q in range(0, count, 2):
        for j in range(2):
            even = spread[j, pl.ds(q, pairs, stride=count), :]
            odd = spread[j, pl.ds(q + 1, pairs, stride=count), :]
            stacked[q // 2, pl.ds(j, pairs, stride=2), :] = jnp.where(first_half, even, odd)

    left_high, left_low = split(left, 2)
    moved = jnp.concatenate([stacked[k] for k in range(count // 2)], axis=1)
    moved_high, moved_low = split(moved, 2)
    done = jnp.dot(
        jnp.concatenate([left_high, left_high, left_low], axis=1),
        jnp.concatenate([moved_high, moved_low, moved_high], axis=0),
        preferred_element_type=jnp.float32,
    )
    for k in range(count // 2):
        stacked[k] = done[:, k * LANES : (k + 1) * LANES]

    for q in range(0, count, 2):
        upper = stacked[q // 2, pl.ds(0, pairs, stride=2), :]
        lower = stacked[q // 2, pl.ds(1, pairs, stride=2), :]
        placed[pl.ds(q, pairs, stride=count), :] = jnp.where(first_half, upper, pltpu.roll(lower, inner, 1))
        placed[pl.ds(q + 1, pairs, stride=count), :] = jnp.where(
            first_half, pltpu.roll(upper, inner, 1), lower
        )
    for k in range(pairs):
        put(k, placed[k * count : (k + 1) * count, :].astype(jnp.bfloat16))


def condition_scratch(layers, count, width):
    pairs = width // LANES
    return [
        pltpu.VMEM((layers, 2, pairs * count, LANES), jnp.float32),
        pltpu.VMEM((layers, count // 2, 2 * pairs, LANES), jnp.float32),
        pltpu.VMEM((layers, pairs * count, LANES), jnp.float32),
    ]


def condition_kernel(queries, left, right, own, mine, block_in, left_in, right_in, spread, stacked, placed, arrived):
    layers = queries.shape[0]
    copies = []
    for k, (source, target) in enumerate(((left, left_in), (right, right_in), (queries.at[:, 0], block_in))):
        copies.append(pltpu.make_async_copy(source, target, arrived.at[k]))
        copies[-1].start()
    for copy in copies:
        copy.wait()
    for layer in range(layers):

        def put(k, tile):
            own[layer, :, k * LANES : (k + 1) * LANES] = tile

        condition_block(
            block_in[layer],
            left_in[layer],
            right_in[layer],
            put,
            spread.at[layer],
            stacked.at[layer],
            placed.at[layer],
        )
    mine[...] = own[lax.axis_index("parts")]


def condition_near(queries, left_factor, right_factor):
    layers, _, count, width = queries.shape
    spec = pl.BlockSpec(memory_space=pltpu.VMEM)
    far = pl.BlockSpec(memory_space=pltpu.HBM)
    return pl.pallas_call(
        condition_kernel,
        out_shape=[
            jax.ShapeDtypeStruct((layers, count, width), jnp.bfloat16),
            jax.ShapeDtypeStruct((count, width), jnp.bfloat16),
        ],
        in_specs=[far] * 3,
        out_specs=[spec] * 2,
        scratch_shapes=[
            pltpu.VMEM((layers, count, width), jnp.bfloat16),
            pltpu.VMEM(left_factor.shape, jnp.float32),
            pltpu.VMEM(right_factor.shape, jnp.float32),
            *condition_scratch(layers, count, width),
            pltpu.SemaphoreType.DMA((3,)),
        ],
        compiler_params=pltpu.CompilerParams(vmem_limit_bytes=8 * 2**20),
        cost_estimate=pl.CostEstimate(flops=2**28, bytes_accessed=2**20, transcendentals=0),
        name="condition",
    )(*(pltpu.with_memory_space_constraint(x, pltpu.HBM) for x in (queries, left_factor, right_factor)))


def along_columns(value, *steps):
    pairs = [(a * PAIR + c, b * PAIR + c) for a, b in steps for c in range(PAIR)]
    return lax.ppermute(value, "train", pairs)


def other_core(value):
    return lax.ppermute(value, "train", [(k, k ^ 1) for k in range(COLUMNS * PAIR)])


def other_part(value):
    return lax.ppermute(value, "parts", [(0, 1), (1, 0)])


def copy_kernel(source, target, done):
    copy = pltpu.make_async_copy(source, target, done)
    copy.start()
    copy.wait()


def copy_near(value):
    return pl.pallas_call(
        copy_kernel,
        out_shape=jax.ShapeDtypeStruct(value.shape, value.dtype),
        in_specs=[pl.BlockSpec(memory_space=pltpu.HBM)],
        out_specs=pl.BlockSpec(memory_space=pltpu.VMEM),
        scratch_shapes=[pltpu.SemaphoreType.DMA],
        compiler_params=pltpu.CompilerParams(vmem_limit_bytes=6 * 2**20),
        cost_estimate=pl.CostEstimate(flops=0, bytes_accessed=2**23, transcendentals=0),
        name="near",
    )(pltpu.with_memory_space_constraint(value, pltpu.HBM))


def place():
    member = lax.axis_index("train")
    return member // PAIR, lax.rem(member, PAIR)


def row_scores(train, table, owner, terms, scores):
    share = scores.shape[0]
    rows, layer_count, width = train.shape
    queries = table.shape[1]
    first = pl.multiple_of(owner * share * layer_count, share * layer_count)
    both = lax.dot_general(
        train.reshape(rows * layer_count, width)[pl.ds(first, share * layer_count), :],
        table[...].reshape(layer_count * queries, width),
        LANES_LAST,
        preferred_element_type=jnp.float32,
    )
    for layer in range(layer_count):
        terms[layer] = both[:, layer * queries : (layer + 1) * queries]
    scores[...] = sum(terms[layer, pl.ds(layer, share, stride=layer_count), :] for layer in range(layer_count))


def sent_kernel(train, *refs):
    blocks, (scores, table, terms) = refs[:-3], refs[-3:]
    part = lax.axis_index("parts")
    column, core = place()
    count = blocks[0].shape[1]

    def put(layer, step, twin, block):
        member = lax.rem(column + step, COLUMNS) * PAIR + (1 - core if twin else core)
        table[layer, pl.ds(pl.multiple_of(member * count, count), count), :] = block

    for twin in range(PAIR):
        for layer in range(table.shape[0]):
            put(layer, 0, twin, blocks[twin][layer])
        for k, (layer, step) in enumerate(
            ((part, 2), (part, 1), (part, 3), (1 - part, 2), (1 - part, 1), (1 - part, 3)), 1
        ):
            put(layer, step, twin, blocks[PAIR * k + twin][...])
    row_scores(train, table, 1 - lax.axis_index("layer"), terms, scores)


def kept_kernel(train, table, scores, terms):
    row_scores(train, table, lax.axis_index("layer"), terms, scores)


def local_call(kernel, name, out_shape, scratch_shapes, *operands):
    spec = pl.BlockSpec(memory_space=pltpu.VMEM)
    return pl.pallas_call(
        kernel,
        out_shape=out_shape,
        in_specs=[spec] * len(operands),
        out_specs=jax.tree.map(lambda _: spec, out_shape),
        scratch_shapes=scratch_shapes,
        compiler_params=pltpu.CompilerParams(vmem_limit_bytes=24 * 2**20),
        cost_estimate=pl.CostEstimate(flops=2**29, bytes_accessed=2**22, transcendentals=0),
        name=name,
    )(*operands)


def direct(train_grads, queries, left_factor, right_factor):
    rows, layer_count, width = train_grads.shape
    count = queries.shape[2]
    total = count * COLUMNS * PAIR
    share = rows // 2

    own, mine = condition_near(queries, left_factor, right_factor)
    near = copy_near(train_grads)
    column, _ = place()
    before = along_columns(mine, (0, 1), (1, 2), (2, 3))
    after = along_columns(mine, (3, 2), (2, 1), (1, 0))
    ends = along_columns(mine, (0, 3), (3, 0))
    passed = jnp.where(column == 1, after, jnp.where(column == 2, before, mine))
    s2 = along_columns(passed, (0, 2), (2, 3), (3, 1), (1, 0))
    before, after, ends, near = lax.optimization_barrier((before, after, ends, near))
    s1 = jnp.where(column == 3, ends, after)
    s3 = jnp.where(column == 0, ends, before)
    y1 = other_part(s1)
    y3 = other_part(s3)
    y2 = other_part(s2)

    blocks = []
    for block in (own, s2, s1, s3, y2, y1, y3):
        blocks += [block, other_core(block)]
    f32 = functools.partial(jax.ShapeDtypeStruct, dtype=jnp.float32)
    terms = [pltpu.VMEM((layer_count, share * layer_count, total), jnp.float32)]
    sent, table = local_call(
        sent_kernel,
        "scores_sent",
        [f32((share, total)), jax.ShapeDtypeStruct((layer_count, total, width), jnp.bfloat16)],
        terms,
        near,
        *blocks,
    )
    received = lax.ppermute(sent, "layer", [(0, 1), (1, 0)])
    kept = local_call(kept_kernel, "scores_kept", f32((share, total)), terms, near, table)
    return kept + received


def general(shape, train_grads, queries, left_factor, right_factor):
    layers = shape["layer"]
    own = condition(queries[:, 0], left_factor, right_factor)
    block = lax.all_gather(own, "train", axis=1, tiled=True)
    share = train_grads.shape[0] // layers
    here = lax.axis_index("layer")

    def terms(step):
        rows = lax.dynamic_slice_in_dim(train_grads, (here + step) % layers * share, share, 0)
        return jnp.einsum("fkm,krm->fr", rows, block, preferred_element_type=jnp.float32)

    scores = terms(0)
    for step in range(1, layers):
        scores += lax.ppermute(terms(step), "layer", [(k, (k + step) % layers) for k in range(layers)])
    return scores


def body(shape, train_grads, queries, left_factor, right_factor):
    fits = (
        shape["train"] == COLUMNS * PAIR
        and shape["parts"] == shape["layer"] == 2
        and shape["query"] == 1
        and train_grads.shape[0] == 2 * LANES
        and train_grads.shape[1:] == (2, 4096)
        and queries.shape[1:] == (1, 16, 4096)
        and left_factor.shape[1:] == right_factor.shape[1:] == (64, 64)
    )
    if fits:
        return direct(train_grads, queries, left_factor, right_factor)
    return general(shape, train_grads, queries, left_factor, right_factor)


def solution(mesh):
    return jax.shard_map(
        functools.partial(body, dict(mesh.shape)),
        mesh=mesh,
        in_specs=(
            P(("parts", "train"), "layer", None),
            P("layer", "query", "train", None),
            P("layer", None, None),
            P("layer", None, None),
        ),
        out_specs=P(("parts", "train", "layer"), "query"),
        check_vma=False,
    )
```

```python
import functools

import jax
import jax.numpy as jnp
from jax import lax
from jax.experimental import pallas as pl
from jax.experimental.pallas import tpu as pltpu
from jax.sharding import PartitionSpec as P

LANES = 128
PAIR = 2
COLUMNS = 4
LANES_LAST = (((1,), (1,)), ((), ()))


def split(value, parts):
    pieces = []
    for _ in range(parts):
        piece = value.astype(jnp.bfloat16)
        pieces.append(piece)
        value = value - piece.astype(jnp.float32)
    return pieces


def condition(own, left_factor, right_factor):
    layer_count, count, width = own.shape
    rows_out, rows_in = left_factor.shape[1], right_factor.shape[1]
    grid = own.astype(jnp.float32).reshape(layer_count, count, rows_out, rows_in)
    left_part = jnp.einsum("lab,lnbc->lnac", left_factor, grid, precision=lax.Precision.HIGHEST)
    both = jnp.einsum("lnac,lcd->lnad", left_part, right_factor, precision=lax.Precision.HIGHEST)
    return both.reshape(layer_count, count, width).astype(jnp.bfloat16)


def condition_block(block, left, right, put, spread, stacked, placed):
    count, width = block.shape
    inner = right.shape[0]
    pairs = width // LANES
    first_half = lax.broadcasted_iota(jnp.int32, (pairs, LANES), 1) < inner

    empty = jnp.zeros((inner, LANES), jnp.float32)
    twice = jnp.concatenate([right, right], axis=1)
    weight = jnp.concatenate(
        [jnp.concatenate([twice, empty], axis=1), jnp.concatenate([empty, twice], axis=1)], axis=0
    )
    high, middle, low = split(weight, 3)
    rows = jnp.concatenate([block[:, k * LANES : (k + 1) * LANES] for k in range(pairs)], axis=0)
    right_part = jnp.dot(
        jnp.concatenate([rows, rows], axis=1),
        jnp.concatenate([high, middle], axis=0),
        preferred_element_type=jnp.float32,
    ) + jnp.dot(rows, low, preferred_element_type=jnp.float32)
    spread[0] = right_part[:, :LANES]
    spread[1] = right_part[:, LANES:]

    for q in range(0, count, 2):
        for j in range(2):
            even = spread[j, pl.ds(q, pairs, stride=count), :]
            odd = spread[j, pl.ds(q + 1, pairs, stride=count), :]
            stacked[q // 2, pl.ds(j, pairs, stride=2), :] = jnp.where(first_half, even, odd)

    left_high, left_low = split(left, 2)
    moved = jnp.concatenate([stacked[k] for k in range(count // 2)], axis=1)
    moved_high, moved_low = split(moved, 2)
    done = jnp.dot(
        jnp.concatenate([left_high, left_high, left_low], axis=1),
        jnp.concatenate([moved_high, moved_low, moved_high], axis=0),
        preferred_element_type=jnp.float32,
    )
    for k in range(count // 2):
        stacked[k] = done[:, k * LANES : (k + 1) * LANES]

    for q in range(0, count, 2):
        upper = stacked[q // 2, pl.ds(0, pairs, stride=2), :]
        lower = stacked[q // 2, pl.ds(1, pairs, stride=2), :]
        placed[pl.ds(q, pairs, stride=count), :] = jnp.where(first_half, upper, pltpu.roll(lower, inner, 1))
        placed[pl.ds(q + 1, pairs, stride=count), :] = jnp.where(
            first_half, pltpu.roll(upper, inner, 1), lower
        )
    for k in range(pairs):
        put(k, placed[k * count : (k + 1) * count, :].astype(jnp.bfloat16))


def condition_kernel(other, queries, left, right, out, block_in, left_in, right_in, spread, stacked, placed, arrived):
    part = lax.axis_index("parts")
    layer = 1 - part if other else part
    copies = [
        pltpu.make_async_copy(source, target, arrived.at[k])
        for k, (source, target) in enumerate(
            ((queries.at[layer, 0], block_in), (right.at[layer], right_in), (left.at[layer], left_in))
        )
    ]
    for copy in copies:
        copy.start()
    for copy in copies:
        copy.wait()

    def put(k, tile):
        out[:, k * LANES : (k + 1) * LANES] = tile

    condition_block(block_in[...], left_in[...], right_in[...], put, spread, stacked, placed)


def condition_layer(other, queries, left_factor, right_factor):
    _, _, count, width = queries.shape
    pairs = width // LANES
    far = pl.BlockSpec(memory_space=pltpu.HBM)
    return pl.pallas_call(
        functools.partial(condition_kernel, other),
        out_shape=jax.ShapeDtypeStruct((count, width), jnp.bfloat16),
        in_specs=[far] * 3,
        out_specs=pl.BlockSpec(memory_space=pltpu.VMEM),
        scratch_shapes=[
            pltpu.VMEM((count, width), jnp.bfloat16),
            pltpu.VMEM(left_factor.shape[1:], jnp.float32),
            pltpu.VMEM(right_factor.shape[1:], jnp.float32),
            pltpu.VMEM((2, pairs * count, LANES), jnp.float32),
            pltpu.VMEM((count // 2, 2 * pairs, LANES), jnp.float32),
            pltpu.VMEM((pairs * count, LANES), jnp.float32),
            pltpu.SemaphoreType.DMA((3,)),
        ],
        compiler_params=pltpu.CompilerParams(vmem_limit_bytes=8 * 2**20),
        cost_estimate=pl.CostEstimate(flops=2**27, bytes_accessed=2**19, transcendentals=0),
        name="condition_other" if other else "condition_mine",
    )(*(pltpu.with_memory_space_constraint(x, pltpu.HBM) for x in (queries, left_factor, right_factor)))


def along_columns(value, flip):
    return lax.ppermute(value, "train", [(k, k ^ (flip * PAIR)) for k in range(COLUMNS * PAIR)])


def other_core(value):
    return lax.ppermute(value, "train", [(k, k ^ 1) for k in range(COLUMNS * PAIR)])


def other_part(value, cross=False):
    train = COLUMNS * PAIR
    pairs = [(part * train + k, (1 - part) * train + (k ^ cross)) for part in range(2) for k in range(train)]
    return lax.ppermute(value, ("parts", "train"), pairs)


def copy_kernel(source, target, done):
    copy = pltpu.make_async_copy(source, target, done)
    copy.start()
    copy.wait()


def copy_near(value):
    return pl.pallas_call(
        copy_kernel,
        out_shape=jax.ShapeDtypeStruct(value.shape, value.dtype),
        in_specs=[pl.BlockSpec(memory_space=pltpu.HBM)],
        out_specs=pl.BlockSpec(memory_space=pltpu.VMEM),
        scratch_shapes=[pltpu.SemaphoreType.DMA],
        compiler_params=pltpu.CompilerParams(vmem_limit_bytes=6 * 2**20),
        cost_estimate=pl.CostEstimate(flops=0, bytes_accessed=2 * value.size * 2, transcendentals=0),
        name="near",
    )(pltpu.with_memory_space_constraint(value, pltpu.HBM))


def place():
    member = lax.axis_index("train")
    return member // PAIR, lax.rem(member, PAIR)


def row_scores(train, table, owner, terms, scores):
    share = scores.shape[0]
    rows, layer_count, width = train.shape
    queries = table.shape[1]
    first = pl.multiple_of(owner * share * layer_count, share * layer_count)
    both = lax.dot_general(
        train.reshape(rows * layer_count, width)[pl.ds(first, share * layer_count), :],
        table[...].reshape(layer_count * queries, width),
        LANES_LAST,
        preferred_element_type=jnp.float32,
    )
    for layer in range(layer_count):
        terms[layer] = both[:, layer * queries : (layer + 1) * queries]
    scores[...] = sum(terms[layer, pl.ds(layer, share, stride=layer_count), :] for layer in range(layer_count))


def sent_kernel(train, *refs):
    blocks, (scores, table, terms) = refs[:-3], refs[-3:]
    part = lax.axis_index("parts")
    column, core = place()
    count = blocks[0].shape[0]

    def put(layer, flip, other, block):
        member = (column ^ flip) * PAIR + (core ^ other)
        table[layer, pl.ds(pl.multiple_of(member * count, count), count), :] = block

    for twin in range(PAIR):
        for k, (layer, flip, cross) in enumerate(
            (
                (part, 0, 0),
                (1 - part, 0, 0),
                (part, 2, 0),
                (part, 1, 0),
                (part, 3, 0),
                (1 - part, 2, 0),
                (1 - part, 1, 1),
                (1 - part, 3, 0),
            )
        ):
            put(layer, flip, twin ^ cross, blocks[PAIR * k + twin][...])
    row_scores(train, table, 1 - lax.axis_index("layer"), terms, scores)


def kept_kernel(train, table, scores, terms):
    row_scores(train, table, lax.axis_index("layer"), terms, scores)


def local_call(kernel, name, out_shape, scratch_shapes, *operands):
    spec = pl.BlockSpec(memory_space=pltpu.VMEM)
    return pl.pallas_call(
        kernel,
        out_shape=out_shape,
        in_specs=[spec] * len(operands),
        out_specs=jax.tree.map(lambda _: spec, out_shape),
        scratch_shapes=scratch_shapes,
        compiler_params=pltpu.CompilerParams(vmem_limit_bytes=24 * 2**20),
        cost_estimate=pl.CostEstimate(flops=2**29, bytes_accessed=2**22, transcendentals=0),
        name=name,
    )(*operands)


def direct(train_grads, queries, left_factor, right_factor):
    rows, layer_count, width = train_grads.shape
    count = queries.shape[2]
    total = count * COLUMNS * PAIR
    share = rows // 2

    mine = condition_layer(False, queries, left_factor, right_factor)
    other = condition_layer(True, queries, left_factor, right_factor)
    near = copy_near(train_grads)
    mine_late, other = lax.optimization_barrier((mine, other))
    s2 = along_columns(mine_late, 2)
    s1 = along_columns(mine, 1)
    s3 = along_columns(mine, 3)
    y1 = other_part(s1, cross=True)
    y3 = other_part(s3)
    y2 = other_part(s2)
    y1, y3, near = lax.optimization_barrier((y1, y3, near))

    blocks = []
    for block in (mine, other, s2, s1, s3, y2, y1, y3):
        blocks += [block, other_core(block)]
    f32 = functools.partial(jax.ShapeDtypeStruct, dtype=jnp.float32)
    terms = [pltpu.VMEM((layer_count, share * layer_count, total), jnp.float32)]
    sent, table = local_call(
        sent_kernel,
        "scores_sent",
        [f32((share, total)), jax.ShapeDtypeStruct((layer_count, total, width), jnp.bfloat16)],
        terms,
        near,
        *blocks,
    )
    received = lax.ppermute(sent, "layer", [(0, 1), (1, 0)])
    kept = local_call(kept_kernel, "scores_kept", f32((share, total)), terms, near, table)
    return kept + received


def general(shape, train_grads, queries, left_factor, right_factor):
    layers = shape["layer"]
    own = condition(queries[:, 0], left_factor, right_factor)
    block = lax.all_gather(own, "train", axis=1, tiled=True)
    share = train_grads.shape[0] // layers
    here = lax.axis_index("layer")

    def terms(step):
        rows = lax.dynamic_slice_in_dim(train_grads, (here + step) % layers * share, share, 0)
        return jnp.einsum("fkm,krm->fr", rows, block, preferred_element_type=jnp.float32)

    scores = terms(0)
    for step in range(1, layers):
        scores += lax.ppermute(terms(step), "layer", [(k, (k + step) % layers) for k in range(layers)])
    return scores


def body(shape, train_grads, queries, left_factor, right_factor):
    fits = (
        shape["train"] == COLUMNS * PAIR
        and shape["parts"] == shape["layer"] == 2
        and shape["query"] == 1
        and train_grads.shape[0] == 2 * LANES
        and train_grads.shape[1:] == (2, 4096)
        and queries.shape[1:] == (1, 16, 4096)
        and left_factor.shape[1:] == right_factor.shape[1:] == (64, 64)
    )
    if fits:
        return direct(train_grads, queries, left_factor, right_factor)
    return general(shape, train_grads, queries, left_factor, right_factor)


def solution(mesh):
    return jax.shard_map(
        functools.partial(body, dict(mesh.shape)),
        mesh=mesh,
        in_specs=(
            P(("parts", "train"), "layer", None),
            P("layer", "query", "train", None),
            P("layer", None, None),
            P("layer", None, None),
        ),
        out_specs=P(("parts", "train", "layer"), "query"),
        check_vma=False,
    )
```

```python
import functools

import jax
import jax.numpy as jnp
from jax import lax
from jax.experimental import pallas as pl
from jax.experimental.pallas import tpu as pltpu
from jax.sharding import PartitionSpec as P

LANES = 128
PAIR = 2
COLUMNS = 4
LANES_LAST = (((1,), (1,)), ((), ()))


def split(value, parts):
    pieces = []
    for _ in range(parts):
        piece = value.astype(jnp.bfloat16)
        pieces.append(piece)
        value = value - piece.astype(jnp.float32)
    return pieces


def condition(own, left_factor, right_factor):
    layer_count, count, width = own.shape
    rows_out, rows_in = left_factor.shape[1], right_factor.shape[1]
    grid = own.astype(jnp.float32).reshape(layer_count, count, rows_out, rows_in)
    left_part = jnp.einsum("lab,lnbc->lnac", left_factor, grid, precision=lax.Precision.HIGHEST)
    both = jnp.einsum("lnac,lcd->lnad", left_part, right_factor, precision=lax.Precision.HIGHEST)
    return both.reshape(layer_count, count, width).astype(jnp.bfloat16)


def condition_block(block, left, right, put, spread, stacked, placed):
    count, width = block.shape
    inner = right.shape[0]
    pairs = width // LANES
    first_half = lax.broadcasted_iota(jnp.int32, (pairs, LANES), 1) < inner

    empty = jnp.zeros((inner, LANES), jnp.float32)
    twice = jnp.concatenate([right, right], axis=1)
    weight = jnp.concatenate(
        [jnp.concatenate([twice, empty], axis=1), jnp.concatenate([empty, twice], axis=1)], axis=0
    )
    high, middle, low = split(weight, 3)
    rows = jnp.concatenate([block[:, k * LANES : (k + 1) * LANES] for k in range(pairs)], axis=0)
    right_part = jnp.dot(
        jnp.concatenate([rows, rows], axis=1),
        jnp.concatenate([high, middle], axis=0),
        preferred_element_type=jnp.float32,
    ) + jnp.dot(rows, low, preferred_element_type=jnp.float32)
    spread[0] = right_part[:, :LANES]
    spread[1] = right_part[:, LANES:]

    for q in range(0, count, 2):
        for j in range(2):
            even = spread[j, pl.ds(q, pairs, stride=count), :]
            odd = spread[j, pl.ds(q + 1, pairs, stride=count), :]
            stacked[q // 2, pl.ds(j, pairs, stride=2), :] = jnp.where(first_half, even, odd)

    left_high, left_low = split(left, 2)
    moved = jnp.concatenate([stacked[k] for k in range(count // 2)], axis=1)
    moved_high, moved_low = split(moved, 2)
    done = jnp.dot(
        jnp.concatenate([left_high, left_high, left_low], axis=1),
        jnp.concatenate([moved_high, moved_low, moved_high], axis=0),
        preferred_element_type=jnp.float32,
    )
    for k in range(count // 2):
        stacked[k] = done[:, k * LANES : (k + 1) * LANES]

    for q in range(0, count, 2):
        upper = stacked[q // 2, pl.ds(0, pairs, stride=2), :]
        lower = stacked[q // 2, pl.ds(1, pairs, stride=2), :]
        placed[pl.ds(q, pairs, stride=count), :] = jnp.where(first_half, upper, pltpu.roll(lower, inner, 1))
        placed[pl.ds(q + 1, pairs, stride=count), :] = jnp.where(
            first_half, pltpu.roll(upper, inner, 1), lower
        )
    for k in range(pairs):
        put(k, placed[k * count : (k + 1) * count, :].astype(jnp.bfloat16))


def condition_kernel(other, queries, left, right, out, block_in, left_in, right_in, spread, stacked, placed, arrived):
    part = lax.axis_index("parts")
    layer = 1 - part if other else part
    copies = [
        pltpu.make_async_copy(source, target, arrived.at[k])
        for k, (source, target) in enumerate(
            ((queries.at[layer, 0], block_in), (right.at[layer], right_in), (left.at[layer], left_in))
        )
    ]
    for copy in copies:
        copy.start()
    for copy in copies:
        copy.wait()

    def put(k, tile):
        out[:, k * LANES : (k + 1) * LANES] = tile

    condition_block(block_in[...], left_in[...], right_in[...], put, spread, stacked, placed)


def condition_layer(other, queries, left_factor, right_factor):
    _, _, count, width = queries.shape
    pairs = width // LANES
    far = pl.BlockSpec(memory_space=pltpu.HBM)
    return pl.pallas_call(
        functools.partial(condition_kernel, other),
        out_shape=jax.ShapeDtypeStruct((count, width), jnp.bfloat16),
        in_specs=[far] * 3,
        out_specs=pl.BlockSpec(memory_space=pltpu.VMEM),
        scratch_shapes=[
            pltpu.VMEM((count, width), jnp.bfloat16),
            pltpu.VMEM(left_factor.shape[1:], jnp.float32),
            pltpu.VMEM(right_factor.shape[1:], jnp.float32),
            pltpu.VMEM((2, pairs * count, LANES), jnp.float32),
            pltpu.VMEM((count // 2, 2 * pairs, LANES), jnp.float32),
            pltpu.VMEM((pairs * count, LANES), jnp.float32),
            pltpu.SemaphoreType.DMA((3,)),
        ],
        compiler_params=pltpu.CompilerParams(vmem_limit_bytes=8 * 2**20),
        cost_estimate=pl.CostEstimate(flops=2**27, bytes_accessed=2**19, transcendentals=0),
        name="condition_other" if other else "condition_mine",
    )(*(pltpu.with_memory_space_constraint(x, pltpu.HBM) for x in (queries, left_factor, right_factor)))


def along_columns(value, flip):
    return lax.ppermute(value, "train", [(k, k ^ (flip * PAIR)) for k in range(COLUMNS * PAIR)])


def other_core(value):
    return lax.ppermute(value, "train", [(k, k ^ 1) for k in range(COLUMNS * PAIR)])


def other_part(value, cross=False):
    train = COLUMNS * PAIR
    pairs = [(part * train + k, (1 - part) * train + (k ^ cross)) for part in range(2) for k in range(train)]
    return lax.ppermute(value, ("parts", "train"), pairs)


def copy_kernel(source, target, done):
    copy = pltpu.make_async_copy(source, target, done)
    copy.start()
    copy.wait()


def copy_near(value):
    return pl.pallas_call(
        copy_kernel,
        out_shape=jax.ShapeDtypeStruct(value.shape, value.dtype),
        in_specs=[pl.BlockSpec(memory_space=pltpu.HBM)],
        out_specs=pl.BlockSpec(memory_space=pltpu.VMEM),
        scratch_shapes=[pltpu.SemaphoreType.DMA],
        compiler_params=pltpu.CompilerParams(vmem_limit_bytes=6 * 2**20),
        cost_estimate=pl.CostEstimate(flops=0, bytes_accessed=2 * value.size * 2, transcendentals=0),
        name="near",
    )(pltpu.with_memory_space_constraint(value, pltpu.HBM))


def place():
    member = lax.axis_index("train")
    return member // PAIR, lax.rem(member, PAIR)


def row_scores(train, table, owner, terms, scores):
    share = scores.shape[0]
    rows, layer_count, width = train.shape
    queries = table.shape[1]
    first = pl.multiple_of(owner * share * layer_count, share * layer_count)
    both = lax.dot_general(
        train.reshape(rows * layer_count, width)[pl.ds(first, share * layer_count), :],
        table[...].reshape(layer_count * queries, width),
        LANES_LAST,
        preferred_element_type=jnp.float32,
    )
    for layer in range(layer_count):
        terms[layer] = both[:, layer * queries : (layer + 1) * queries]
    scores[...] = sum(terms[layer, pl.ds(layer, share, stride=layer_count), :] for layer in range(layer_count))


def sent_kernel(train, *refs):
    blocks, (scores, table, terms) = refs[:-3], refs[-3:]
    part = lax.axis_index("parts")
    column, core = place()
    count = blocks[0].shape[0]

    def put(layer, flip, other, block):
        member = (column ^ flip) * PAIR + (core ^ other)
        table[layer, pl.ds(pl.multiple_of(member * count, count), count), :] = block

    for twin in range(PAIR):
        for k, (layer, flip, cross) in enumerate(
            (
                (part, 0, 0),
                (1 - part, 0, 0),
                (part, 2, 0),
                (part, 1, 0),
                (part, 3, 0),
                (1 - part, 2, 0),
                (1 - part, 1, 1),
                (1 - part, 3, 0),
            )
        ):
            put(layer, flip, twin ^ cross, blocks[PAIR * k + twin][...])
    row_scores(train, table, 1 - lax.axis_index("layer"), terms, scores)


def kept_kernel(train, table, scores, terms):
    row_scores(train, table, lax.axis_index("layer"), terms, scores)


def local_call(kernel, name, out_shape, scratch_shapes, *operands):
    spec = pl.BlockSpec(memory_space=pltpu.VMEM)
    return pl.pallas_call(
        kernel,
        out_shape=out_shape,
        in_specs=[spec] * len(operands),
        out_specs=jax.tree.map(lambda _: spec, out_shape),
        scratch_shapes=scratch_shapes,
        compiler_params=pltpu.CompilerParams(vmem_limit_bytes=24 * 2**20),
        cost_estimate=pl.CostEstimate(flops=2**29, bytes_accessed=2**22, transcendentals=0),
        name=name,
    )(*operands)


def direct(train_grads, queries, left_factor, right_factor):
    rows, layer_count, width = train_grads.shape
    count = queries.shape[2]
    total = count * COLUMNS * PAIR
    share = rows // 2

    mine = condition_layer(False, queries, left_factor, right_factor)
    other = condition_layer(True, queries, left_factor, right_factor)
    near = copy_near(train_grads)
    s2 = along_columns(mine, 2)
    s1 = along_columns(mine, 1)
    s3 = along_columns(mine, 3)
    s1, other = lax.optimization_barrier((s1, other))
    y1 = other_part(s1, cross=True)
    y3 = other_part(s3)
    y2 = other_part(s2)
    y1, near = lax.optimization_barrier((y1, near))

    blocks = []
    for block in (mine, other, s2, s1, s3, y2, y1, y3):
        blocks += [block, other_core(block)]
    f32 = functools.partial(jax.ShapeDtypeStruct, dtype=jnp.float32)
    terms = [pltpu.VMEM((layer_count, share * layer_count, total), jnp.float32)]
    sent, table = local_call(
        sent_kernel,
        "scores_sent",
        [f32((share, total)), jax.ShapeDtypeStruct((layer_count, total, width), jnp.bfloat16)],
        terms,
        near,
        *blocks,
    )
    received = lax.ppermute(sent, "layer", [(0, 1), (1, 0)])
    kept = local_call(kept_kernel, "scores_kept", f32((share, total)), terms, near, table)
    return kept + received


def general(shape, train_grads, queries, left_factor, right_factor):
    layers = shape["layer"]
    own = condition(queries[:, 0], left_factor, right_factor)
    block = lax.all_gather(own, "train", axis=1, tiled=True)
    share = train_grads.shape[0] // layers
    here = lax.axis_index("layer")

    def terms(step):
        rows = lax.dynamic_slice_in_dim(train_grads, (here + step) % layers * share, share, 0)
        return jnp.einsum("fkm,krm->fr", rows, block, preferred_element_type=jnp.float32)

    scores = terms(0)
    for step in range(1, layers):
        scores += lax.ppermute(terms(step), "layer", [(k, (k + step) % layers) for k in range(layers)])
    return scores


def body(shape, train_grads, queries, left_factor, right_factor):
    fits = (
        shape["train"] == COLUMNS * PAIR
        and shape["parts"] == shape["layer"] == 2
        and shape["query"] == 1
        and train_grads.shape[0] == 2 * LANES
        and train_grads.shape[1:] == (2, 4096)
        and queries.shape[1:] == (1, 16, 4096)
        and left_factor.shape[1:] == right_factor.shape[1:] == (64, 64)
    )
    if fits:
        return direct(train_grads, queries, left_factor, right_factor)
    return general(shape, train_grads, queries, left_factor, right_factor)


def solution(mesh):
    return jax.shard_map(
        functools.partial(body, dict(mesh.shape)),
        mesh=mesh,
        in_specs=(
            P(("parts", "train"), "layer", None),
            P("layer", "query", "train", None),
            P("layer", None, None),
            P("layer", None, None),
        ),
        out_specs=P(("parts", "train", "layer"), "query"),
        check_vma=False,
    )
```

```python
import functools

import jax
import jax.numpy as jnp
from jax import lax
from jax.experimental import pallas as pl
from jax.experimental.pallas import tpu as pltpu
from jax.sharding import PartitionSpec as P

LANES = 128
PAIR = 2
COLUMNS = 4
LANES_LAST = (((1,), (1,)), ((), ()))


def split(value, parts):
    pieces = []
    for _ in range(parts):
        piece = value.astype(jnp.bfloat16)
        pieces.append(piece)
        value = value - piece.astype(jnp.float32)
    return pieces


def condition(own, left_factor, right_factor):
    layer_count, count, width = own.shape
    rows_out, rows_in = left_factor.shape[1], right_factor.shape[1]
    grid = own.astype(jnp.float32).reshape(layer_count, count, rows_out, rows_in)
    left_part = jnp.einsum("lab,lnbc->lnac", left_factor, grid, precision=lax.Precision.HIGHEST)
    both = jnp.einsum("lnac,lcd->lnad", left_part, right_factor, precision=lax.Precision.HIGHEST)
    return both.reshape(layer_count, count, width).astype(jnp.bfloat16)


def condition_block(block, left, right, put, spread, stacked, placed):
    count, width = block.shape
    inner = right.shape[0]
    pairs = width // LANES
    first_half = lax.broadcasted_iota(jnp.int32, (pairs, LANES), 1) < inner

    empty = jnp.zeros((inner, LANES), jnp.float32)
    twice = jnp.concatenate([right, right], axis=1)
    weight = jnp.concatenate(
        [jnp.concatenate([twice, empty], axis=1), jnp.concatenate([empty, twice], axis=1)], axis=0
    )
    high, middle, low = split(weight, 3)
    rows = jnp.concatenate([block[:, k * LANES : (k + 1) * LANES] for k in range(pairs)], axis=0)
    right_part = jnp.dot(
        jnp.concatenate([rows, rows], axis=1),
        jnp.concatenate([high, middle], axis=0),
        preferred_element_type=jnp.float32,
    ) + jnp.dot(rows, low, preferred_element_type=jnp.float32)
    spread[0] = right_part[:, :LANES]
    spread[1] = right_part[:, LANES:]

    for q in range(0, count, 2):
        for j in range(2):
            even = spread[j, pl.ds(q, pairs, stride=count), :]
            odd = spread[j, pl.ds(q + 1, pairs, stride=count), :]
            stacked[q // 2, pl.ds(j, pairs, stride=2), :] = jnp.where(first_half, even, odd)

    left_high, left_low = split(left, 2)
    moved = jnp.concatenate([stacked[k] for k in range(count // 2)], axis=1)
    moved_high, moved_low = split(moved, 2)
    done = jnp.dot(
        jnp.concatenate([left_high, left_high, left_low], axis=1),
        jnp.concatenate([moved_high, moved_low, moved_high], axis=0),
        preferred_element_type=jnp.float32,
    )
    for k in range(count // 2):
        stacked[k] = done[:, k * LANES : (k + 1) * LANES]

    for q in range(0, count, 2):
        upper = stacked[q // 2, pl.ds(0, pairs, stride=2), :]
        lower = stacked[q // 2, pl.ds(1, pairs, stride=2), :]
        placed[pl.ds(q, pairs, stride=count), :] = jnp.where(first_half, upper, pltpu.roll(lower, inner, 1))
        placed[pl.ds(q + 1, pairs, stride=count), :] = jnp.where(
            first_half, pltpu.roll(upper, inner, 1), lower
        )
    for k in range(pairs):
        put(k, placed[k * count : (k + 1) * count, :].astype(jnp.bfloat16))


def condition_kernel(other, queries, left, right, out, block_in, left_in, right_in, spread, stacked, placed, arrived):
    part = lax.axis_index("parts")
    layer = 1 - part if other else part
    copies = [
        pltpu.make_async_copy(source, target, arrived.at[k])
        for k, (source, target) in enumerate(
            ((queries.at[layer, 0], block_in), (right.at[layer], right_in), (left.at[layer], left_in))
        )
    ]
    for copy in copies:
        copy.start()
    for copy in copies:
        copy.wait()

    def put(k, tile):
        out[:, k * LANES : (k + 1) * LANES] = tile

    condition_block(block_in[...], left_in[...], right_in[...], put, spread, stacked, placed)


def condition_layer(other, queries, left_factor, right_factor):
    _, _, count, width = queries.shape
    pairs = width // LANES
    far = pl.BlockSpec(memory_space=pltpu.HBM)
    return pl.pallas_call(
        functools.partial(condition_kernel, other),
        out_shape=jax.ShapeDtypeStruct((count, width), jnp.bfloat16),
        in_specs=[far] * 3,
        out_specs=pl.BlockSpec(memory_space=pltpu.VMEM),
        scratch_shapes=[
            pltpu.VMEM((count, width), jnp.bfloat16),
            pltpu.VMEM(left_factor.shape[1:], jnp.float32),
            pltpu.VMEM(right_factor.shape[1:], jnp.float32),
            pltpu.VMEM((2, pairs * count, LANES), jnp.float32),
            pltpu.VMEM((count // 2, 2 * pairs, LANES), jnp.float32),
            pltpu.VMEM((pairs * count, LANES), jnp.float32),
            pltpu.SemaphoreType.DMA((3,)),
        ],
        compiler_params=pltpu.CompilerParams(vmem_limit_bytes=8 * 2**20),
        cost_estimate=pl.CostEstimate(flops=2**27, bytes_accessed=2**19, transcendentals=0),
        name="condition_other" if other else "condition_mine",
    )(*(pltpu.with_memory_space_constraint(x, pltpu.HBM) for x in (queries, left_factor, right_factor)))


def along_columns(value, flip):
    return lax.ppermute(value, "train", [(k, k ^ (flip * PAIR)) for k in range(COLUMNS * PAIR)])


def other_core(value):
    return lax.ppermute(value, "train", [(k, k ^ 1) for k in range(COLUMNS * PAIR)])


def other_part(value, cross=False):
    train = COLUMNS * PAIR
    pairs = [(part * train + k, (1 - part) * train + (k ^ cross)) for part in range(2) for k in range(train)]
    return lax.ppermute(value, ("parts", "train"), pairs)


def copy_kernel(source, target, done):
    copy = pltpu.make_async_copy(source, target, done)
    copy.start()
    copy.wait()


def copy_near(value):
    return pl.pallas_call(
        copy_kernel,
        out_shape=jax.ShapeDtypeStruct(value.shape, value.dtype),
        in_specs=[pl.BlockSpec(memory_space=pltpu.HBM)],
        out_specs=pl.BlockSpec(memory_space=pltpu.VMEM),
        scratch_shapes=[pltpu.SemaphoreType.DMA],
        compiler_params=pltpu.CompilerParams(vmem_limit_bytes=6 * 2**20),
        cost_estimate=pl.CostEstimate(flops=0, bytes_accessed=2 * value.size * 2, transcendentals=0),
        name="near",
    )(pltpu.with_memory_space_constraint(value, pltpu.HBM))


def place():
    member = lax.axis_index("train")
    return member // PAIR, lax.rem(member, PAIR)


def row_scores(train, table, owner, terms, scores):
    share = scores.shape[0]
    rows, layer_count, width = train.shape
    queries = table.shape[1]
    first = pl.multiple_of(owner * share * layer_count, share * layer_count)
    both = lax.dot_general(
        train.reshape(rows * layer_count, width)[pl.ds(first, share * layer_count), :],
        table[...].reshape(layer_count * queries, width),
        LANES_LAST,
        preferred_element_type=jnp.float32,
    )
    for layer in range(layer_count):
        terms[layer] = both[:, layer * queries : (layer + 1) * queries]
    scores[...] = sum(terms[layer, pl.ds(layer, share, stride=layer_count), :] for layer in range(layer_count))


def sent_kernel(train, *refs):
    blocks, (scores, table, terms) = refs[:-3], refs[-3:]
    part = lax.axis_index("parts")
    column, core = place()
    count = blocks[0].shape[0]

    def put(layer, flip, other, block):
        member = (column ^ flip) * PAIR + (core ^ other)
        table[layer, pl.ds(pl.multiple_of(member * count, count), count), :] = block

    for twin in range(PAIR):
        for k, (layer, flip, cross) in enumerate(
            (
                (part, 0, 0),
                (1 - part, 0, 0),
                (part, 2, 0),
                (part, 1, 0),
                (part, 3, 0),
                (1 - part, 2, 0),
                (1 - part, 1, 1),
                (1 - part, 3, 0),
            )
        ):
            put(layer, flip, twin ^ cross, blocks[PAIR * k + twin][...])
    row_scores(train, table, 1 - lax.axis_index("layer"), terms, scores)


def kept_kernel(train, table, scores, terms):
    row_scores(train, table, lax.axis_index("layer"), terms, scores)


def local_call(kernel, name, out_shape, scratch_shapes, *operands):
    spec = pl.BlockSpec(memory_space=pltpu.VMEM)
    return pl.pallas_call(
        kernel,
        out_shape=out_shape,
        in_specs=[spec] * len(operands),
        out_specs=jax.tree.map(lambda _: spec, out_shape),
        scratch_shapes=scratch_shapes,
        compiler_params=pltpu.CompilerParams(vmem_limit_bytes=24 * 2**20),
        cost_estimate=pl.CostEstimate(flops=2**29, bytes_accessed=2**22, transcendentals=0),
        name=name,
    )(*operands)


def direct(train_grads, queries, left_factor, right_factor):
    rows, layer_count, width = train_grads.shape
    count = queries.shape[2]
    total = count * COLUMNS * PAIR
    share = rows // 2

    mine = condition_layer(False, queries, left_factor, right_factor)
    other = condition_layer(True, queries, left_factor, right_factor)
    near = copy_near(train_grads)
    s1 = along_columns(mine, 1)
    s3 = along_columns(mine, 3)
    s3, other = lax.optimization_barrier((s3, other))
    s2 = along_columns(s3, 1)
    y1 = other_part(s1, cross=True)
    y3 = other_part(s3)
    y2 = other_part(s2)
    y1, y3, near = lax.optimization_barrier((y1, y3, near))

    blocks = []
    for block in (mine, other, s2, s1, s3, y2, y1, y3):
        blocks += [block, other_core(block)]
    f32 = functools.partial(jax.ShapeDtypeStruct, dtype=jnp.float32)
    terms = [pltpu.VMEM((layer_count, share * layer_count, total), jnp.float32)]
    sent, table = local_call(
        sent_kernel,
        "scores_sent",
        [f32((share, total)), jax.ShapeDtypeStruct((layer_count, total, width), jnp.bfloat16)],
        terms,
        near,
        *blocks,
    )
    received = lax.ppermute(sent, "layer", [(0, 1), (1, 0)])
    kept = local_call(kept_kernel, "scores_kept", f32((share, total)), terms, near, table)
    return kept + received


def general(shape, train_grads, queries, left_factor, right_factor):
    layers = shape["layer"]
    own = condition(queries[:, 0], left_factor, right_factor)
    block = lax.all_gather(own, "train", axis=1, tiled=True)
    share = train_grads.shape[0] // layers
    here = lax.axis_index("layer")

    def terms(step):
        rows = lax.dynamic_slice_in_dim(train_grads, (here + step) % layers * share, share, 0)
        return jnp.einsum("fkm,krm->fr", rows, block, preferred_element_type=jnp.float32)

    scores = terms(0)
    for step in range(1, layers):
        scores += lax.ppermute(terms(step), "layer", [(k, (k + step) % layers) for k in range(layers)])
    return scores


def body(shape, train_grads, queries, left_factor, right_factor):
    fits = (
        shape["train"] == COLUMNS * PAIR
        and shape["parts"] == shape["layer"] == 2
        and shape["query"] == 1
        and train_grads.shape[0] == 2 * LANES
        and train_grads.shape[1:] == (2, 4096)
        and queries.shape[1:] == (1, 16, 4096)
        and left_factor.shape[1:] == right_factor.shape[1:] == (64, 64)
    )
    if fits:
        return direct(train_grads, queries, left_factor, right_factor)
    return general(shape, train_grads, queries, left_factor, right_factor)


def solution(mesh):
    return jax.shard_map(
        functools.partial(body, dict(mesh.shape)),
        mesh=mesh,
        in_specs=(
            P(("parts", "train"), "layer", None),
            P("layer", "query", "train", None),
            P("layer", None, None),
            P("layer", None, None),
        ),
        out_specs=P(("parts", "train", "layer"), "query"),
        check_vma=False,
    )
```

```python
import functools

import jax
import jax.numpy as jnp
from jax import lax
from jax.experimental import pallas as pl
from jax.experimental.pallas import tpu as pltpu
from jax.sharding import PartitionSpec as P

LANES = 128
PAIR = 2
COLUMNS = 4
LANES_LAST = (((1,), (1,)), ((), ()))


def split(value, parts):
    pieces = []
    for _ in range(parts):
        piece = value.astype(jnp.bfloat16)
        pieces.append(piece)
        value = value - piece.astype(jnp.float32)
    return pieces


def condition(own, left_factor, right_factor):
    layer_count, count, width = own.shape
    rows_out, rows_in = left_factor.shape[1], right_factor.shape[1]
    grid = own.astype(jnp.float32).reshape(layer_count, count, rows_out, rows_in)
    left_part = jnp.einsum("lab,lnbc->lnac", left_factor, grid, precision=lax.Precision.HIGHEST)
    both = jnp.einsum("lnac,lcd->lnad", left_part, right_factor, precision=lax.Precision.HIGHEST)
    return both.reshape(layer_count, count, width).astype(jnp.bfloat16)


def condition_block(block, left, right, put, spread, stacked, placed):
    count, width = block.shape
    inner = right.shape[0]
    pairs = width // LANES
    first_half = lax.broadcasted_iota(jnp.int32, (pairs, LANES), 1) < inner

    empty = jnp.zeros((inner, LANES), jnp.float32)
    twice = jnp.concatenate([right, right], axis=1)
    weight = jnp.concatenate(
        [jnp.concatenate([twice, empty], axis=1), jnp.concatenate([empty, twice], axis=1)], axis=0
    )
    high, middle, low = split(weight, 3)
    rows = jnp.concatenate([block[:, k * LANES : (k + 1) * LANES] for k in range(pairs)], axis=0)
    right_part = jnp.dot(
        jnp.concatenate([rows, rows], axis=1),
        jnp.concatenate([high, middle], axis=0),
        preferred_element_type=jnp.float32,
    ) + jnp.dot(rows, low, preferred_element_type=jnp.float32)
    spread[0] = right_part[:, :LANES]
    spread[1] = right_part[:, LANES:]

    for q in range(0, count, 2):
        for j in range(2):
            even = spread[j, pl.ds(q, pairs, stride=count), :]
            odd = spread[j, pl.ds(q + 1, pairs, stride=count), :]
            stacked[q // 2, pl.ds(j, pairs, stride=2), :] = jnp.where(first_half, even, odd)

    left_high, left_low = split(left, 2)
    moved = jnp.concatenate([stacked[k] for k in range(count // 2)], axis=1)
    moved_high, moved_low = split(moved, 2)
    done = jnp.dot(
        jnp.concatenate([left_high, left_high, left_low], axis=1),
        jnp.concatenate([moved_high, moved_low, moved_high], axis=0),
        preferred_element_type=jnp.float32,
    )
    for k in range(count // 2):
        stacked[k] = done[:, k * LANES : (k + 1) * LANES]

    for q in range(0, count, 2):
        upper = stacked[q // 2, pl.ds(0, pairs, stride=2), :]
        lower = stacked[q // 2, pl.ds(1, pairs, stride=2), :]
        placed[pl.ds(q, pairs, stride=count), :] = jnp.where(first_half, upper, pltpu.roll(lower, inner, 1))
        placed[pl.ds(q + 1, pairs, stride=count), :] = jnp.where(
            first_half, pltpu.roll(upper, inner, 1), lower
        )
    for k in range(pairs):
        put(k, placed[k * count : (k + 1) * count, :].astype(jnp.bfloat16))


def condition_kernel(other, queries, left, right, out, block_in, left_in, right_in, spread, stacked, placed, arrived):
    part = lax.axis_index("parts")
    layer = 1 - part if other else part
    copies = [
        pltpu.make_async_copy(source, target, arrived.at[k])
        for k, (source, target) in enumerate(
            ((queries.at[layer, 0], block_in), (right.at[layer], right_in), (left.at[layer], left_in))
        )
    ]
    for copy in copies:
        copy.start()
    for copy in copies:
        copy.wait()

    def put(k, tile):
        out[:, k * LANES : (k + 1) * LANES] = tile

    condition_block(block_in[...], left_in[...], right_in[...], put, spread, stacked, placed)


def condition_layer(other, queries, left_factor, right_factor):
    _, _, count, width = queries.shape
    pairs = width // LANES
    far = pl.BlockSpec(memory_space=pltpu.HBM)
    return pl.pallas_call(
        functools.partial(condition_kernel, other),
        out_shape=jax.ShapeDtypeStruct((count, width), jnp.bfloat16),
        in_specs=[far] * 3,
        out_specs=pl.BlockSpec(memory_space=pltpu.VMEM),
        scratch_shapes=[
            pltpu.VMEM((count, width), jnp.bfloat16),
            pltpu.VMEM(left_factor.shape[1:], jnp.float32),
            pltpu.VMEM(right_factor.shape[1:], jnp.float32),
            pltpu.VMEM((2, pairs * count, LANES), jnp.float32),
            pltpu.VMEM((count // 2, 2 * pairs, LANES), jnp.float32),
            pltpu.VMEM((pairs * count, LANES), jnp.float32),
            pltpu.SemaphoreType.DMA((3,)),
        ],
        compiler_params=pltpu.CompilerParams(vmem_limit_bytes=8 * 2**20),
        cost_estimate=pl.CostEstimate(flops=2**27, bytes_accessed=2**19, transcendentals=0),
        name="condition_other" if other else "condition_mine",
    )(*(pltpu.with_memory_space_constraint(x, pltpu.HBM) for x in (queries, left_factor, right_factor)))


def along_columns(value, flip):
    return lax.ppermute(value, "train", [(k, k ^ (flip * PAIR)) for k in range(COLUMNS * PAIR)])


def other_core(value):
    return lax.ppermute(value, "train", [(k, k ^ 1) for k in range(COLUMNS * PAIR)])


def other_part(value, cross=False):
    train = COLUMNS * PAIR
    pairs = [(part * train + k, (1 - part) * train + (k ^ cross)) for part in range(2) for k in range(train)]
    return lax.ppermute(value, ("parts", "train"), pairs)


def copy_kernel(source, target, done):
    copy = pltpu.make_async_copy(source, target, done)
    copy.start()
    copy.wait()


def copy_near(value):
    return pl.pallas_call(
        copy_kernel,
        out_shape=jax.ShapeDtypeStruct(value.shape, value.dtype),
        in_specs=[pl.BlockSpec(memory_space=pltpu.HBM)],
        out_specs=pl.BlockSpec(memory_space=pltpu.VMEM),
        scratch_shapes=[pltpu.SemaphoreType.DMA],
        compiler_params=pltpu.CompilerParams(vmem_limit_bytes=6 * 2**20),
        cost_estimate=pl.CostEstimate(flops=0, bytes_accessed=2 * value.size * 2, transcendentals=0),
        name="near",
    )(pltpu.with_memory_space_constraint(value, pltpu.HBM))


def place():
    member = lax.axis_index("train")
    return member // PAIR, lax.rem(member, PAIR)


def row_scores(train, table, owner, terms, scores):
    share = scores.shape[0]
    rows, layer_count, width = train.shape
    queries = table.shape[1]
    first = pl.multiple_of(owner * share * layer_count, share * layer_count)
    both = lax.dot_general(
        train.reshape(rows * layer_count, width)[pl.ds(first, share * layer_count), :],
        table[...].reshape(layer_count * queries, width),
        LANES_LAST,
        preferred_element_type=jnp.float32,
    )
    for layer in range(layer_count):
        terms[layer] = both[:, layer * queries : (layer + 1) * queries]
    scores[...] = sum(terms[layer, pl.ds(layer, share, stride=layer_count), :] for layer in range(layer_count))


def sent_kernel(train, *refs):
    blocks, (scores, table, terms) = refs[:-3], refs[-3:]
    part = lax.axis_index("parts")
    column, core = place()
    count = blocks[0].shape[0]

    def put(layer, flip, other, block):
        member = (column ^ flip) * PAIR + (core ^ other)
        table[layer, pl.ds(pl.multiple_of(member * count, count), count), :] = block

    for twin in range(PAIR):
        for k, (layer, flip, cross) in enumerate(
            (
                (part, 0, 0),
                (1 - part, 0, 0),
                (part, 2, 0),
                (part, 1, 0),
                (part, 3, 0),
                (1 - part, 2, 0),
                (1 - part, 1, 0),
                (1 - part, 3, 1),
            )
        ):
            put(layer, flip, twin ^ cross, blocks[PAIR * k + twin][...])
    row_scores(train, table, 1 - lax.axis_index("layer"), terms, scores)


def kept_kernel(train, table, scores, terms):
    row_scores(train, table, lax.axis_index("layer"), terms, scores)


def local_call(kernel, name, out_shape, scratch_shapes, *operands):
    spec = pl.BlockSpec(memory_space=pltpu.VMEM)
    return pl.pallas_call(
        kernel,
        out_shape=out_shape,
        in_specs=[spec] * len(operands),
        out_specs=jax.tree.map(lambda _: spec, out_shape),
        scratch_shapes=scratch_shapes,
        compiler_params=pltpu.CompilerParams(vmem_limit_bytes=24 * 2**20),
        cost_estimate=pl.CostEstimate(flops=2**29, bytes_accessed=2**22, transcendentals=0),
        name=name,
    )(*operands)


def direct(train_grads, queries, left_factor, right_factor):
    rows, layer_count, width = train_grads.shape
    count = queries.shape[2]
    total = count * COLUMNS * PAIR
    share = rows // 2

    mine = condition_layer(False, queries, left_factor, right_factor)
    other = condition_layer(True, queries, left_factor, right_factor)
    near = copy_near(train_grads)
    s2 = along_columns(mine, 2)
    s1 = along_columns(mine, 1)
    s3 = along_columns(mine, 3)
    t1 = along_columns(other, 1)
    y2 = other_part(s2)
    y3 = other_part(s3, cross=True)
    y3, near = lax.optimization_barrier((y3, near))

    blocks = []
    for block in (mine, other, s2, s1, s3, y2, t1, y3):
        blocks += [block, other_core(block)]
    f32 = functools.partial(jax.ShapeDtypeStruct, dtype=jnp.float32)
    terms = [pltpu.VMEM((layer_count, share * layer_count, total), jnp.float32)]
    sent, table = local_call(
        sent_kernel,
        "scores_sent",
        [f32((share, total)), jax.ShapeDtypeStruct((layer_count, total, width), jnp.bfloat16)],
        terms,
        near,
        *blocks,
    )
    received = lax.ppermute(sent, "layer", [(0, 1), (1, 0)])
    kept = local_call(kept_kernel, "scores_kept", f32((share, total)), terms, near, table)
    return kept + received


def general(shape, train_grads, queries, left_factor, right_factor):
    layers = shape["layer"]
    own = condition(queries[:, 0], left_factor, right_factor)
    block = lax.all_gather(own, "train", axis=1, tiled=True)
    share = train_grads.shape[0] // layers
    here = lax.axis_index("layer")

    def terms(step):
        rows = lax.dynamic_slice_in_dim(train_grads, (here + step) % layers * share, share, 0)
        return jnp.einsum("fkm,krm->fr", rows, block, preferred_element_type=jnp.float32)

    scores = terms(0)
    for step in range(1, layers):
        scores += lax.ppermute(terms(step), "layer", [(k, (k + step) % layers) for k in range(layers)])
    return scores


def body(shape, train_grads, queries, left_factor, right_factor):
    fits = (
        shape["train"] == COLUMNS * PAIR
        and shape["parts"] == shape["layer"] == 2
        and shape["query"] == 1
        and train_grads.shape[0] == 2 * LANES
        and train_grads.shape[1:] == (2, 4096)
        and queries.shape[1:] == (1, 16, 4096)
        and left_factor.shape[1:] == right_factor.shape[1:] == (64, 64)
    )
    if fits:
        return direct(train_grads, queries, left_factor, right_factor)
    return general(shape, train_grads, queries, left_factor, right_factor)


def solution(mesh):
    return jax.shard_map(
        functools.partial(body, dict(mesh.shape)),
        mesh=mesh,
        in_specs=(
            P(("parts", "train"), "layer", None),
            P("layer", "query", "train", None),
            P("layer", None, None),
            P("layer", None, None),
        ),
        out_specs=P(("parts", "train", "layer"), "query"),
        check_vma=False,
    )
```

```python
import functools

import jax
import jax.numpy as jnp
from jax import lax
from jax.experimental import pallas as pl
from jax.experimental.pallas import tpu as pltpu
from jax.sharding import PartitionSpec as P

LANES = 128
PAIR = 2
COLUMNS = 4
LANES_LAST = (((1,), (1,)), ((), ()))


def split(value, parts):
    pieces = []
    for _ in range(parts):
        piece = value.astype(jnp.bfloat16)
        pieces.append(piece)
        value = value - piece.astype(jnp.float32)
    return pieces


def condition(own, left_factor, right_factor):
    layer_count, count, width = own.shape
    rows_out, rows_in = left_factor.shape[1], right_factor.shape[1]
    grid = own.astype(jnp.float32).reshape(layer_count, count, rows_out, rows_in)
    left_part = jnp.einsum("lab,lnbc->lnac", left_factor, grid, precision=lax.Precision.HIGHEST)
    both = jnp.einsum("lnac,lcd->lnad", left_part, right_factor, precision=lax.Precision.HIGHEST)
    return both.reshape(layer_count, count, width).astype(jnp.bfloat16)


def condition_block(block, left, right, put, spread, stacked, placed):
    count, width = block.shape
    inner = right.shape[0]
    pairs = width // LANES
    first_half = lax.broadcasted_iota(jnp.int32, (pairs, LANES), 1) < inner

    empty = jnp.zeros((inner, LANES), jnp.float32)
    twice = jnp.concatenate([right, right], axis=1)
    weight = jnp.concatenate(
        [jnp.concatenate([twice, empty], axis=1), jnp.concatenate([empty, twice], axis=1)], axis=0
    )
    high, middle, low = split(weight, 3)
    rows = jnp.concatenate([block[:, k * LANES : (k + 1) * LANES] for k in range(pairs)], axis=0)
    right_part = jnp.dot(
        jnp.concatenate([rows, rows], axis=1),
        jnp.concatenate([high, middle], axis=0),
        preferred_element_type=jnp.float32,
    ) + jnp.dot(rows, low, preferred_element_type=jnp.float32)
    spread[0] = right_part[:, :LANES]
    spread[1] = right_part[:, LANES:]

    for q in range(0, count, 2):
        for j in range(2):
            even = spread[j, pl.ds(q, pairs, stride=count), :]
            odd = spread[j, pl.ds(q + 1, pairs, stride=count), :]
            stacked[q // 2, pl.ds(j, pairs, stride=2), :] = jnp.where(first_half, even, odd)

    left_high, left_low = split(left, 2)
    moved = jnp.concatenate([stacked[k] for k in range(count // 2)], axis=1)
    moved_high, moved_low = split(moved, 2)
    done = jnp.dot(
        jnp.concatenate([left_high, left_high, left_low], axis=1),
        jnp.concatenate([moved_high, moved_low, moved_high], axis=0),
        preferred_element_type=jnp.float32,
    )
    for k in range(count // 2):
        stacked[k] = done[:, k * LANES : (k + 1) * LANES]

    for q in range(0, count, 2):
        upper = stacked[q // 2, pl.ds(0, pairs, stride=2), :]
        lower = stacked[q // 2, pl.ds(1, pairs, stride=2), :]
        placed[pl.ds(q, pairs, stride=count), :] = jnp.where(first_half, upper, pltpu.roll(lower, inner, 1))
        placed[pl.ds(q + 1, pairs, stride=count), :] = jnp.where(
            first_half, pltpu.roll(upper, inner, 1), lower
        )
    for k in range(pairs):
        put(k, placed[k * count : (k + 1) * count, :].astype(jnp.bfloat16))


def condition_kernel(other, queries, left, right, out, block_in, left_in, right_in, spread, stacked, placed, arrived):
    part = lax.axis_index("parts")
    layer = 1 - part if other else part
    copies = [
        pltpu.make_async_copy(source, target, arrived.at[k])
        for k, (source, target) in enumerate(
            ((queries.at[layer, 0], block_in), (right.at[layer], right_in), (left.at[layer], left_in))
        )
    ]
    for copy in copies:
        copy.start()
    for copy in copies:
        copy.wait()

    def put(k, tile):
        out[:, k * LANES : (k + 1) * LANES] = tile

    condition_block(block_in[...], left_in[...], right_in[...], put, spread, stacked, placed)


def condition_layer(other, queries, left_factor, right_factor):
    _, _, count, width = queries.shape
    pairs = width // LANES
    far = pl.BlockSpec(memory_space=pltpu.HBM)
    return pl.pallas_call(
        functools.partial(condition_kernel, other),
        out_shape=jax.ShapeDtypeStruct((count, width), jnp.bfloat16),
        in_specs=[far] * 3,
        out_specs=pl.BlockSpec(memory_space=pltpu.VMEM),
        scratch_shapes=[
            pltpu.VMEM((count, width), jnp.bfloat16),
            pltpu.VMEM(left_factor.shape[1:], jnp.float32),
            pltpu.VMEM(right_factor.shape[1:], jnp.float32),
            pltpu.VMEM((2, pairs * count, LANES), jnp.float32),
            pltpu.VMEM((count // 2, 2 * pairs, LANES), jnp.float32),
            pltpu.VMEM((pairs * count, LANES), jnp.float32),
            pltpu.SemaphoreType.DMA((3,)),
        ],
        compiler_params=pltpu.CompilerParams(vmem_limit_bytes=8 * 2**20),
        cost_estimate=pl.CostEstimate(flops=2**27, bytes_accessed=2**19, transcendentals=0),
        name="condition_other" if other else "condition_mine",
    )(*(pltpu.with_memory_space_constraint(x, pltpu.HBM) for x in (queries, left_factor, right_factor)))


def along_columns(value, flip):
    return lax.ppermute(value, "train", [(k, k ^ (flip * PAIR)) for k in range(COLUMNS * PAIR)])


def other_core(value):
    return lax.ppermute(value, "train", [(k, k ^ 1) for k in range(COLUMNS * PAIR)])


def other_part(value, cross=False):
    train = COLUMNS * PAIR
    pairs = [(part * train + k, (1 - part) * train + (k ^ cross)) for part in range(2) for k in range(train)]
    return lax.ppermute(value, ("parts", "train"), pairs)


def copy_kernel(source, target, done):
    copy = pltpu.make_async_copy(source, target, done)
    copy.start()
    copy.wait()


def copy_near(value):
    return pl.pallas_call(
        copy_kernel,
        out_shape=jax.ShapeDtypeStruct(value.shape, value.dtype),
        in_specs=[pl.BlockSpec(memory_space=pltpu.HBM)],
        out_specs=pl.BlockSpec(memory_space=pltpu.VMEM),
        scratch_shapes=[pltpu.SemaphoreType.DMA],
        compiler_params=pltpu.CompilerParams(vmem_limit_bytes=6 * 2**20),
        cost_estimate=pl.CostEstimate(flops=0, bytes_accessed=2 * value.size * 2, transcendentals=0),
        name="near",
    )(pltpu.with_memory_space_constraint(value, pltpu.HBM))


def place():
    member = lax.axis_index("train")
    return member // PAIR, lax.rem(member, PAIR)


def row_scores(train, table, owner, terms, scores):
    share = scores.shape[0]
    rows, layer_count, width = train.shape
    queries = table.shape[1]
    first = pl.multiple_of(owner * share * layer_count, share * layer_count)
    both = lax.dot_general(
        train.reshape(rows * layer_count, width)[pl.ds(first, share * layer_count), :],
        table[...].reshape(layer_count * queries, width),
        LANES_LAST,
        preferred_element_type=jnp.float32,
    )
    for layer in range(layer_count):
        terms[layer] = both[:, layer * queries : (layer + 1) * queries]
    scores[...] = sum(terms[layer, pl.ds(layer, share, stride=layer_count), :] for layer in range(layer_count))


def sent_kernel(train, *refs):
    blocks, (scores, table, terms) = refs[:-3], refs[-3:]
    part = lax.axis_index("parts")
    column, core = place()
    count = blocks[0].shape[0]

    def put(layer, flip, other, block):
        member = (column ^ flip) * PAIR + (core ^ other)
        table[layer, pl.ds(pl.multiple_of(member * count, count), count), :] = block

    for twin in range(PAIR):
        for k, (layer, flip, cross) in enumerate(
            (
                (part, 0, 0),
                (1 - part, 0, 0),
                (part, 2, 0),
                (part, 1, 0),
                (part, 3, 0),
                (1 - part, 2, 0),
                (1 - part, 1, 1),
                (1 - part, 3, 0),
            )
        ):
            put(layer, flip, twin ^ cross, blocks[PAIR * k + twin][...])
    row_scores(train, table, 1 - lax.axis_index("layer"), terms, scores)


def kept_kernel(train, table, scores, terms):
    row_scores(train, table, lax.axis_index("layer"), terms, scores)


def local_call(kernel, name, out_shape, scratch_shapes, *operands):
    spec = pl.BlockSpec(memory_space=pltpu.VMEM)
    return pl.pallas_call(
        kernel,
        out_shape=out_shape,
        in_specs=[spec] * len(operands),
        out_specs=jax.tree.map(lambda _: spec, out_shape),
        scratch_shapes=scratch_shapes,
        compiler_params=pltpu.CompilerParams(vmem_limit_bytes=24 * 2**20),
        cost_estimate=pl.CostEstimate(flops=2**29, bytes_accessed=2**22, transcendentals=0),
        name=name,
    )(*operands)


def direct(train_grads, queries, left_factor, right_factor):
    rows, layer_count, width = train_grads.shape
    count = queries.shape[2]
    total = count * COLUMNS * PAIR
    share = rows // 2

    mine = condition_layer(False, queries, left_factor, right_factor)
    other = condition_layer(True, queries, left_factor, right_factor)
    near = copy_near(train_grads)
    s1 = along_columns(mine, 1)
    s3 = along_columns(mine, 3)
    s2 = along_columns(s3, 1)
    t2 = along_columns(other, 2)
    y1 = other_part(s1, cross=True)
    y3 = other_part(s3)
    s2, y1, y3, t2 = lax.optimization_barrier((s2, y1, y3, t2))
    other, near = lax.optimization_barrier((other, near))

    blocks = []
    for block in (mine, other, s2, s1, s3, t2, y1, y3):
        blocks += [block, other_core(block)]
    f32 = functools.partial(jax.ShapeDtypeStruct, dtype=jnp.float32)
    terms = [pltpu.VMEM((layer_count, share * layer_count, total), jnp.float32)]
    sent, table = local_call(
        sent_kernel,
        "scores_sent",
        [f32((share, total)), jax.ShapeDtypeStruct((layer_count, total, width), jnp.bfloat16)],
        terms,
        near,
        *blocks,
    )
    received = lax.ppermute(sent, "layer", [(0, 1), (1, 0)])
    kept = local_call(kept_kernel, "scores_kept", f32((share, total)), terms, near, table)
    return kept + received


def general(shape, train_grads, queries, left_factor, right_factor):
    layers = shape["layer"]
    own = condition(queries[:, 0], left_factor, right_factor)
    block = lax.all_gather(own, "train", axis=1, tiled=True)
    share = train_grads.shape[0] // layers
    here = lax.axis_index("layer")

    def terms(step):
        rows = lax.dynamic_slice_in_dim(train_grads, (here + step) % layers * share, share, 0)
        return jnp.einsum("fkm,krm->fr", rows, block, preferred_element_type=jnp.float32)

    scores = terms(0)
    for step in range(1, layers):
        scores += lax.ppermute(terms(step), "layer", [(k, (k + step) % layers) for k in range(layers)])
    return scores


def body(shape, train_grads, queries, left_factor, right_factor):
    fits = (
        shape["train"] == COLUMNS * PAIR
        and shape["parts"] == shape["layer"] == 2
        and shape["query"] == 1
        and train_grads.shape[0] == 2 * LANES
        and train_grads.shape[1:] == (2, 4096)
        and queries.shape[1:] == (1, 16, 4096)
        and left_factor.shape[1:] == right_factor.shape[1:] == (64, 64)
    )
    if fits:
        return direct(train_grads, queries, left_factor, right_factor)
    return general(shape, train_grads, queries, left_factor, right_factor)


def solution(mesh):
    return jax.shard_map(
        functools.partial(body, dict(mesh.shape)),
        mesh=mesh,
        in_specs=(
            P(("parts", "train"), "layer", None),
            P("layer", "query", "train", None),
            P("layer", None, None),
            P("layer", None, None),
        ),
        out_specs=P(("parts", "train", "layer"), "query"),
        check_vma=False,
    )
```

```python
import functools

import jax
import jax.numpy as jnp
from jax import lax
from jax.experimental import pallas as pl
from jax.experimental.pallas import tpu as pltpu
from jax.sharding import PartitionSpec as P

LANES = 128
PAIR = 2
COLUMNS = 4
LANES_LAST = (((1,), (1,)), ((), ()))


def split(value, parts):
    pieces = []
    for _ in range(parts):
        piece = value.astype(jnp.bfloat16)
        pieces.append(piece)
        value = value - piece.astype(jnp.float32)
    return pieces


def condition(own, left_factor, right_factor):
    layer_count, count, width = own.shape
    rows_out, rows_in = left_factor.shape[1], right_factor.shape[1]
    grid = own.astype(jnp.float32).reshape(layer_count, count, rows_out, rows_in)
    left_part = jnp.einsum("lab,lnbc->lnac", left_factor, grid, precision=lax.Precision.HIGHEST)
    both = jnp.einsum("lnac,lcd->lnad", left_part, right_factor, precision=lax.Precision.HIGHEST)
    return both.reshape(layer_count, count, width).astype(jnp.bfloat16)


def condition_block(block, left, right, put, spread, stacked, placed):
    count, width = block.shape
    inner = right.shape[0]
    pairs = width // LANES
    first_half = lax.broadcasted_iota(jnp.int32, (pairs, LANES), 1) < inner

    empty = jnp.zeros((inner, LANES), jnp.float32)
    twice = jnp.concatenate([right, right], axis=1)
    weight = jnp.concatenate(
        [jnp.concatenate([twice, empty], axis=1), jnp.concatenate([empty, twice], axis=1)], axis=0
    )
    high, middle, low = split(weight, 3)
    rows = jnp.concatenate([block[:, k * LANES : (k + 1) * LANES] for k in range(pairs)], axis=0)
    right_part = jnp.dot(
        jnp.concatenate([rows, rows], axis=1),
        jnp.concatenate([high, middle], axis=0),
        preferred_element_type=jnp.float32,
    ) + jnp.dot(rows, low, preferred_element_type=jnp.float32)
    spread[0] = right_part[:, :LANES]
    spread[1] = right_part[:, LANES:]

    for q in range(0, count, 2):
        for j in range(2):
            even = spread[j, pl.ds(q, pairs, stride=count), :]
            odd = spread[j, pl.ds(q + 1, pairs, stride=count), :]
            stacked[q // 2, pl.ds(j, pairs, stride=2), :] = jnp.where(first_half, even, odd)

    left_high, left_low = split(left, 2)
    moved = jnp.concatenate([stacked[k] for k in range(count // 2)], axis=1)
    moved_high, moved_low = split(moved, 2)
    done = jnp.dot(
        jnp.concatenate([left_high, left_high, left_low], axis=1),
        jnp.concatenate([moved_high, moved_low, moved_high], axis=0),
        preferred_element_type=jnp.float32,
    )
    for k in range(count // 2):
        stacked[k] = done[:, k * LANES : (k + 1) * LANES]

    for q in range(0, count, 2):
        upper = stacked[q // 2, pl.ds(0, pairs, stride=2), :]
        lower = stacked[q // 2, pl.ds(1, pairs, stride=2), :]
        placed[pl.ds(q, pairs, stride=count), :] = jnp.where(first_half, upper, pltpu.roll(lower, inner, 1))
        placed[pl.ds(q + 1, pairs, stride=count), :] = jnp.where(
            first_half, pltpu.roll(upper, inner, 1), lower
        )
    for k in range(pairs):
        put(k, placed[k * count : (k + 1) * count, :].astype(jnp.bfloat16))


def condition_kernel(other, queries, left, right, out, block_in, left_in, right_in, spread, stacked, placed, arrived):
    part = lax.axis_index("parts")
    layer = 1 - part if other else part
    copies = [
        pltpu.make_async_copy(source, target, arrived.at[k])
        for k, (source, target) in enumerate(
            ((queries.at[layer, 0], block_in), (right.at[layer], right_in), (left.at[layer], left_in))
        )
    ]
    for copy in copies:
        copy.start()
    for copy in copies:
        copy.wait()

    def put(k, tile):
        out[:, k * LANES : (k + 1) * LANES] = tile

    condition_block(block_in[...], left_in[...], right_in[...], put, spread, stacked, placed)


def condition_layer(other, queries, left_factor, right_factor):
    _, _, count, width = queries.shape
    pairs = width // LANES
    far = pl.BlockSpec(memory_space=pltpu.HBM)
    return pl.pallas_call(
        functools.partial(condition_kernel, other),
        out_shape=jax.ShapeDtypeStruct((count, width), jnp.bfloat16),
        in_specs=[far] * 3,
        out_specs=pl.BlockSpec(memory_space=pltpu.VMEM),
        scratch_shapes=[
            pltpu.VMEM((count, width), jnp.bfloat16),
            pltpu.VMEM(left_factor.shape[1:], jnp.float32),
            pltpu.VMEM(right_factor.shape[1:], jnp.float32),
            pltpu.VMEM((2, pairs * count, LANES), jnp.float32),
            pltpu.VMEM((count // 2, 2 * pairs, LANES), jnp.float32),
            pltpu.VMEM((pairs * count, LANES), jnp.float32),
            pltpu.SemaphoreType.DMA((3,)),
        ],
        compiler_params=pltpu.CompilerParams(vmem_limit_bytes=8 * 2**20),
        cost_estimate=pl.CostEstimate(flops=2**27, bytes_accessed=2**19, transcendentals=0),
        name="condition_other" if other else "condition_mine",
    )(*(pltpu.with_memory_space_constraint(x, pltpu.HBM) for x in (queries, left_factor, right_factor)))


def along_columns(value, flip):
    return lax.ppermute(value, "train", [(k, k ^ (flip * PAIR)) for k in range(COLUMNS * PAIR)])


def other_core(value):
    return lax.ppermute(value, "train", [(k, k ^ 1) for k in range(COLUMNS * PAIR)])


def other_part(value, cross=False):
    train = COLUMNS * PAIR
    pairs = [(part * train + k, (1 - part) * train + (k ^ cross)) for part in range(2) for k in range(train)]
    return lax.ppermute(value, ("parts", "train"), pairs)


def copy_kernel(source, target, done):
    copy = pltpu.make_async_copy(source, target, done)
    copy.start()
    copy.wait()


def copy_near(value):
    return pl.pallas_call(
        copy_kernel,
        out_shape=jax.ShapeDtypeStruct(value.shape, value.dtype),
        in_specs=[pl.BlockSpec(memory_space=pltpu.HBM)],
        out_specs=pl.BlockSpec(memory_space=pltpu.VMEM),
        scratch_shapes=[pltpu.SemaphoreType.DMA],
        compiler_params=pltpu.CompilerParams(vmem_limit_bytes=6 * 2**20),
        cost_estimate=pl.CostEstimate(flops=0, bytes_accessed=2 * value.size * 2, transcendentals=0),
        name="near",
    )(pltpu.with_memory_space_constraint(value, pltpu.HBM))


def place():
    member = lax.axis_index("train")
    return member // PAIR, lax.rem(member, PAIR)


def row_scores(train, table, owner, terms, scores):
    share = scores.shape[0]
    rows, layer_count, width = train.shape
    queries = table.shape[1]
    first = pl.multiple_of(owner * share * layer_count, share * layer_count)
    both = lax.dot_general(
        train.reshape(rows * layer_count, width)[pl.ds(first, share * layer_count), :],
        table[...].reshape(layer_count * queries, width),
        LANES_LAST,
        preferred_element_type=jnp.float32,
    )
    for layer in range(layer_count):
        terms[layer] = both[:, layer * queries : (layer + 1) * queries]
    scores[...] = sum(terms[layer, pl.ds(layer, share, stride=layer_count), :] for layer in range(layer_count))


def sent_kernel(train, *refs):
    blocks, (scores, table, terms) = refs[:-3], refs[-3:]
    part = lax.axis_index("parts")
    column, core = place()
    count = blocks[0].shape[0]

    def put(layer, flip, other, block):
        member = (column ^ flip) * PAIR + (core ^ other)
        table[layer, pl.ds(pl.multiple_of(member * count, count), count), :] = block

    for twin in range(PAIR):
        for k, (layer, flip, cross) in enumerate(
            (
                (part, 0, 0),
                (1 - part, 0, 0),
                (part, 2, 0),
                (part, 1, 0),
                (part, 3, 0),
                (1 - part, 2, 0),
                (1 - part, 1, 1),
                (1 - part, 3, 0),
            )
        ):
            put(layer, flip, twin ^ cross, blocks[PAIR * k + twin][...])
    row_scores(train, table, 1 - lax.axis_index("layer"), terms, scores)


def kept_kernel(train, table, scores, terms):
    row_scores(train, table, lax.axis_index("layer"), terms, scores)


def local_call(kernel, name, out_shape, scratch_shapes, *operands):
    spec = pl.BlockSpec(memory_space=pltpu.VMEM)
    return pl.pallas_call(
        kernel,
        out_shape=out_shape,
        in_specs=[spec] * len(operands),
        out_specs=jax.tree.map(lambda _: spec, out_shape),
        scratch_shapes=scratch_shapes,
        compiler_params=pltpu.CompilerParams(vmem_limit_bytes=24 * 2**20),
        cost_estimate=pl.CostEstimate(flops=2**29, bytes_accessed=2**22, transcendentals=0),
        name=name,
    )(*operands)


def direct(train_grads, queries, left_factor, right_factor):
    rows, layer_count, width = train_grads.shape
    count = queries.shape[2]
    total = count * COLUMNS * PAIR
    share = rows // 2

    mine = condition_layer(False, queries, left_factor, right_factor)
    other = condition_layer(True, queries, left_factor, right_factor)
    near = copy_near(train_grads)
    s1 = along_columns(mine, 1)
    s3 = along_columns(mine, 3)
    s3, near = lax.optimization_barrier((s3, near))
    s2 = along_columns(s3, 1)
    t2 = along_columns(other, 2)
    y1 = other_part(s1, cross=True)
    y3 = other_part(s3)
    s2, y1, y3, t2 = lax.optimization_barrier((s2, y1, y3, t2))

    blocks = []
    for block in (mine, other, s2, s1, s3, t2, y1, y3):
        blocks += [block, other_core(block)]
    f32 = functools.partial(jax.ShapeDtypeStruct, dtype=jnp.float32)
    terms = [pltpu.VMEM((layer_count, share * layer_count, total), jnp.float32)]
    sent, table = local_call(
        sent_kernel,
        "scores_sent",
        [f32((share, total)), jax.ShapeDtypeStruct((layer_count, total, width), jnp.bfloat16)],
        terms,
        near,
        *blocks,
    )
    received = lax.ppermute(sent, "layer", [(0, 1), (1, 0)])
    kept = local_call(kept_kernel, "scores_kept", f32((share, total)), terms, near, table)
    return kept + received


def general(shape, train_grads, queries, left_factor, right_factor):
    layers = shape["layer"]
    own = condition(queries[:, 0], left_factor, right_factor)
    block = lax.all_gather(own, "train", axis=1, tiled=True)
    share = train_grads.shape[0] // layers
    here = lax.axis_index("layer")

    def terms(step):
        rows = lax.dynamic_slice_in_dim(train_grads, (here + step) % layers * share, share, 0)
        return jnp.einsum("fkm,krm->fr", rows, block, preferred_element_type=jnp.float32)

    scores = terms(0)
    for step in range(1, layers):
        scores += lax.ppermute(terms(step), "layer", [(k, (k + step) % layers) for k in range(layers)])
    return scores


def body(shape, train_grads, queries, left_factor, right_factor):
    fits = (
        shape["train"] == COLUMNS * PAIR
        and shape["parts"] == shape["layer"] == 2
        and shape["query"] == 1
        and train_grads.shape[0] == 2 * LANES
        and train_grads.shape[1:] == (2, 4096)
        and queries.shape[1:] == (1, 16, 4096)
        and left_factor.shape[1:] == right_factor.shape[1:] == (64, 64)
    )
    if fits:
        return direct(train_grads, queries, left_factor, right_factor)
    return general(shape, train_grads, queries, left_factor, right_factor)


def solution(mesh):
    return jax.shard_map(
        functools.partial(body, dict(mesh.shape)),
        mesh=mesh,
        in_specs=(
            P(("parts", "train"), "layer", None),
            P("layer", "query", "train", None),
            P("layer", None, None),
            P("layer", None, None),
        ),
        out_specs=P(("parts", "train", "layer"), "query"),
        check_vma=False,
    )
```

```python
import functools

import jax
import jax.numpy as jnp
from jax import lax
from jax.experimental import pallas as pl
from jax.experimental.pallas import tpu as pltpu
from jax.sharding import PartitionSpec as P

LANES = 128
PAIR = 2
COLUMNS = 4
LANES_LAST = (((1,), (1,)), ((), ()))


def split(value, parts):
    pieces = []
    for _ in range(parts):
        piece = value.astype(jnp.bfloat16)
        pieces.append(piece)
        value = value - piece.astype(jnp.float32)
    return pieces


def condition(own, left_factor, right_factor):
    layer_count, count, width = own.shape
    rows_out, rows_in = left_factor.shape[1], right_factor.shape[1]
    grid = own.astype(jnp.float32).reshape(layer_count, count, rows_out, rows_in)
    left_part = jnp.einsum("lab,lnbc->lnac", left_factor, grid, precision=lax.Precision.HIGHEST)
    both = jnp.einsum("lnac,lcd->lnad", left_part, right_factor, precision=lax.Precision.HIGHEST)
    return both.reshape(layer_count, count, width).astype(jnp.bfloat16)


def condition_block(block, left, right, put, spread, stacked, placed):
    count, width = block.shape
    inner = right.shape[0]
    pairs = width // LANES
    first_half = lax.broadcasted_iota(jnp.int32, (pairs, LANES), 1) < inner

    empty = jnp.zeros((inner, LANES), jnp.float32)
    twice = jnp.concatenate([right, right], axis=1)
    weight = jnp.concatenate(
        [jnp.concatenate([twice, empty], axis=1), jnp.concatenate([empty, twice], axis=1)], axis=0
    )
    high, middle, low = split(weight, 3)
    rows = jnp.concatenate([block[:, k * LANES : (k + 1) * LANES] for k in range(pairs)], axis=0)
    right_part = jnp.dot(
        jnp.concatenate([rows, rows], axis=1),
        jnp.concatenate([high, middle], axis=0),
        preferred_element_type=jnp.float32,
    ) + jnp.dot(rows, low, preferred_element_type=jnp.float32)
    spread[0] = right_part[:, :LANES]
    spread[1] = right_part[:, LANES:]

    for q in range(0, count, 2):
        for j in range(2):
            even = spread[j, pl.ds(q, pairs, stride=count), :]
            odd = spread[j, pl.ds(q + 1, pairs, stride=count), :]
            stacked[q // 2, pl.ds(j, pairs, stride=2), :] = jnp.where(first_half, even, odd)

    left_high, left_low = split(left, 2)
    moved = jnp.concatenate([stacked[k] for k in range(count // 2)], axis=1)
    moved_high, moved_low = split(moved, 2)
    done = jnp.dot(
        jnp.concatenate([left_high, left_high, left_low], axis=1),
        jnp.concatenate([moved_high, moved_low, moved_high], axis=0),
        preferred_element_type=jnp.float32,
    )
    for k in range(count // 2):
        stacked[k] = done[:, k * LANES : (k + 1) * LANES]

    for q in range(0, count, 2):
        upper = stacked[q // 2, pl.ds(0, pairs, stride=2), :]
        lower = stacked[q // 2, pl.ds(1, pairs, stride=2), :]
        placed[pl.ds(q, pairs, stride=count), :] = jnp.where(first_half, upper, pltpu.roll(lower, inner, 1))
        placed[pl.ds(q + 1, pairs, stride=count), :] = jnp.where(
            first_half, pltpu.roll(upper, inner, 1), lower
        )
    for k in range(pairs):
        put(k, placed[k * count : (k + 1) * count, :].astype(jnp.bfloat16))


def condition_kernel(other, queries, left, right, out, block_in, left_in, right_in, spread, stacked, placed, arrived):
    part = lax.axis_index("parts")
    layer = 1 - part if other else part
    copies = [
        pltpu.make_async_copy(source, target, arrived.at[k])
        for k, (source, target) in enumerate(
            ((queries.at[layer, 0], block_in), (right.at[layer], right_in), (left.at[layer], left_in))
        )
    ]
    for copy in copies:
        copy.start()
    for copy in copies:
        copy.wait()

    def put(k, tile):
        out[:, k * LANES : (k + 1) * LANES] = tile

    condition_block(block_in[...], left_in[...], right_in[...], put, spread, stacked, placed)


def condition_layer(other, queries, left_factor, right_factor):
    _, _, count, width = queries.shape
    pairs = width // LANES
    far = pl.BlockSpec(memory_space=pltpu.HBM)
    return pl.pallas_call(
        functools.partial(condition_kernel, other),
        out_shape=jax.ShapeDtypeStruct((count, width), jnp.bfloat16),
        in_specs=[far] * 3,
        out_specs=pl.BlockSpec(memory_space=pltpu.VMEM),
        scratch_shapes=[
            pltpu.VMEM((count, width), jnp.bfloat16),
            pltpu.VMEM(left_factor.shape[1:], jnp.float32),
            pltpu.VMEM(right_factor.shape[1:], jnp.float32),
            pltpu.VMEM((2, pairs * count, LANES), jnp.float32),
            pltpu.VMEM((count // 2, 2 * pairs, LANES), jnp.float32),
            pltpu.VMEM((pairs * count, LANES), jnp.float32),
            pltpu.SemaphoreType.DMA((3,)),
        ],
        compiler_params=pltpu.CompilerParams(vmem_limit_bytes=8 * 2**20),
        cost_estimate=pl.CostEstimate(flops=2**27, bytes_accessed=2**19, transcendentals=0),
        name="condition_other" if other else "condition_mine",
    )(*(pltpu.with_memory_space_constraint(x, pltpu.HBM) for x in (queries, left_factor, right_factor)))


def along_columns(value, flip):
    return lax.ppermute(value, "train", [(k, k ^ (flip * PAIR)) for k in range(COLUMNS * PAIR)])


def other_core(value):
    return lax.ppermute(value, "train", [(k, k ^ 1) for k in range(COLUMNS * PAIR)])


def other_part(value, cross=False):
    train = COLUMNS * PAIR
    pairs = [(part * train + k, (1 - part) * train + (k ^ cross)) for part in range(2) for k in range(train)]
    return lax.ppermute(value, ("parts", "train"), pairs)


def copy_kernel(source, target, done):
    copy = pltpu.make_async_copy(source, target, done)
    copy.start()
    copy.wait()


def copy_near(value):
    return pl.pallas_call(
        copy_kernel,
        out_shape=jax.ShapeDtypeStruct(value.shape, value.dtype),
        in_specs=[pl.BlockSpec(memory_space=pltpu.HBM)],
        out_specs=pl.BlockSpec(memory_space=pltpu.VMEM),
        scratch_shapes=[pltpu.SemaphoreType.DMA],
        compiler_params=pltpu.CompilerParams(vmem_limit_bytes=6 * 2**20),
        cost_estimate=pl.CostEstimate(flops=0, bytes_accessed=2 * value.size * 2, transcendentals=0),
        name="near",
    )(pltpu.with_memory_space_constraint(value, pltpu.HBM))


def place():
    member = lax.axis_index("train")
    return member // PAIR, lax.rem(member, PAIR)


def row_scores(train, table, owner, terms, scores):
    share = scores.shape[0]
    rows, layer_count, width = train.shape
    queries = table.shape[1]
    first = pl.multiple_of(owner * share * layer_count, share * layer_count)
    both = lax.dot_general(
        train.reshape(rows * layer_count, width)[pl.ds(first, share * layer_count), :],
        table[...].reshape(layer_count * queries, width),
        LANES_LAST,
        preferred_element_type=jnp.float32,
    )
    for layer in range(layer_count):
        terms[layer] = both[:, layer * queries : (layer + 1) * queries]
    scores[...] = sum(terms[layer, pl.ds(layer, share, stride=layer_count), :] for layer in range(layer_count))


def sent_kernel(train, *refs):
    blocks, (scores, table, terms) = refs[:-3], refs[-3:]
    part = lax.axis_index("parts")
    column, core = place()
    count = blocks[0].shape[0]

    def put(layer, flip, other, block):
        member = (column ^ flip) * PAIR + (core ^ other)
        table[layer, pl.ds(pl.multiple_of(member * count, count), count), :] = block

    for twin in range(PAIR):
        for k, (layer, flip, cross) in enumerate(
            (
                (1 - part, 1, 1),
                (1 - part, 3, 0),
                (part, 0, 0),
                (1 - part, 0, 0),
                (part, 1, 0),
                (part, 3, 0),
                (part, 2, 0),
                (1 - part, 2, 0),
            )
        ):
            put(layer, flip, twin ^ cross, blocks[PAIR * k + twin][...])
    row_scores(train, table, 1 - lax.axis_index("layer"), terms, scores)


def kept_kernel(train, table, scores, terms):
    row_scores(train, table, lax.axis_index("layer"), terms, scores)


def local_call(kernel, name, out_shape, scratch_shapes, *operands):
    spec = pl.BlockSpec(memory_space=pltpu.VMEM)
    return pl.pallas_call(
        kernel,
        out_shape=out_shape,
        in_specs=[spec] * len(operands),
        out_specs=jax.tree.map(lambda _: spec, out_shape),
        scratch_shapes=scratch_shapes,
        compiler_params=pltpu.CompilerParams(vmem_limit_bytes=24 * 2**20),
        cost_estimate=pl.CostEstimate(flops=2**29, bytes_accessed=2**22, transcendentals=0),
        name=name,
    )(*operands)


def direct(train_grads, queries, left_factor, right_factor):
    rows, layer_count, width = train_grads.shape
    count = queries.shape[2]
    total = count * COLUMNS * PAIR
    share = rows // 2

    mine = condition_layer(False, queries, left_factor, right_factor)
    other = condition_layer(True, queries, left_factor, right_factor)
    near = copy_near(train_grads)
    s1 = along_columns(mine, 1)
    s3 = along_columns(mine, 3)
    s1, s3, other, near = lax.optimization_barrier((s1, s3, other, near))
    s2 = along_columns(s3, 1)
    t2 = along_columns(other, 2)
    y1 = other_part(s1, cross=True)
    y3 = other_part(s3)
    s2, t2 = lax.optimization_barrier((s2, t2))
    y1, y3 = lax.optimization_barrier((y1, y3))

    blocks = []
    for block in (y1, y3, mine, other, s1, s3, s2, t2):
        blocks += [block, other_core(block)]
    f32 = functools.partial(jax.ShapeDtypeStruct, dtype=jnp.float32)
    terms = [pltpu.VMEM((layer_count, share * layer_count, total), jnp.float32)]
    sent, table = local_call(
        sent_kernel,
        "scores_sent",
        [f32((share, total)), jax.ShapeDtypeStruct((layer_count, total, width), jnp.bfloat16)],
        terms,
        near,
        *blocks,
    )
    received = lax.ppermute(sent, "layer", [(0, 1), (1, 0)])
    kept = local_call(kept_kernel, "scores_kept", f32((share, total)), terms, near, table)
    return kept + received


def general(shape, train_grads, queries, left_factor, right_factor):
    layers = shape["layer"]
    own = condition(queries[:, 0], left_factor, right_factor)
    block = lax.all_gather(own, "train", axis=1, tiled=True)
    share = train_grads.shape[0] // layers
    here = lax.axis_index("layer")

    def terms(step):
        rows = lax.dynamic_slice_in_dim(train_grads, (here + step) % layers * share, share, 0)
        return jnp.einsum("fkm,krm->fr", rows, block, preferred_element_type=jnp.float32)

    scores = terms(0)
    for step in range(1, layers):
        scores += lax.ppermute(terms(step), "layer", [(k, (k + step) % layers) for k in range(layers)])
    return scores


def body(shape, train_grads, queries, left_factor, right_factor):
    fits = (
        shape["train"] == COLUMNS * PAIR
        and shape["parts"] == shape["layer"] == 2
        and shape["query"] == 1
        and train_grads.shape[0] == 2 * LANES
        and train_grads.shape[1:] == (2, 4096)
        and queries.shape[1:] == (1, 16, 4096)
        and left_factor.shape[1:] == right_factor.shape[1:] == (64, 64)
    )
    if fits:
        return direct(train_grads, queries, left_factor, right_factor)
    return general(shape, train_grads, queries, left_factor, right_factor)


def solution(mesh):
    return jax.shard_map(
        functools.partial(body, dict(mesh.shape)),
        mesh=mesh,
        in_specs=(
            P(("parts", "train"), "layer", None),
            P("layer", "query", "train", None),
            P("layer", None, None),
            P("layer", None, None),
        ),
        out_specs=P(("parts", "train", "layer"), "query"),
        check_vma=False,
    )
```

```python
import functools

import jax
import jax.numpy as jnp
from jax import lax
from jax.experimental import pallas as pl
from jax.experimental.pallas import tpu as pltpu
from jax.sharding import PartitionSpec as P

LANES = 128
PAIR = 2
COLUMNS = 4
LANES_LAST = (((1,), (1,)), ((), ()))


def split(value, parts):
    pieces = []
    for _ in range(parts):
        piece = value.astype(jnp.bfloat16)
        pieces.append(piece)
        value = value - piece.astype(jnp.float32)
    return pieces


def condition(own, left_factor, right_factor):
    layer_count, count, width = own.shape
    rows_out, rows_in = left_factor.shape[1], right_factor.shape[1]
    grid = own.astype(jnp.float32).reshape(layer_count, count, rows_out, rows_in)
    left_part = jnp.einsum("lab,lnbc->lnac", left_factor, grid, precision=lax.Precision.HIGHEST)
    both = jnp.einsum("lnac,lcd->lnad", left_part, right_factor, precision=lax.Precision.HIGHEST)
    return both.reshape(layer_count, count, width).astype(jnp.bfloat16)


def condition_block(block, left, right, put, spread, stacked, placed):
    count, width = block.shape
    inner = right.shape[0]
    pairs = width // LANES
    first_half = lax.broadcasted_iota(jnp.int32, (pairs, LANES), 1) < inner

    empty = jnp.zeros((inner, LANES), jnp.float32)
    twice = jnp.concatenate([right, right], axis=1)
    weight = jnp.concatenate(
        [jnp.concatenate([twice, empty], axis=1), jnp.concatenate([empty, twice], axis=1)], axis=0
    )
    high, middle, low = split(weight, 3)
    rows = jnp.concatenate([block[:, k * LANES : (k + 1) * LANES] for k in range(pairs)], axis=0)
    right_part = jnp.dot(
        jnp.concatenate([rows, rows], axis=1),
        jnp.concatenate([high, middle], axis=0),
        preferred_element_type=jnp.float32,
    ) + jnp.dot(rows, low, preferred_element_type=jnp.float32)
    spread[0] = right_part[:, :LANES]
    spread[1] = right_part[:, LANES:]

    for q in range(0, count, 2):
        for j in range(2):
            even = spread[j, pl.ds(q, pairs, stride=count), :]
            odd = spread[j, pl.ds(q + 1, pairs, stride=count), :]
            stacked[q // 2, pl.ds(j, pairs, stride=2), :] = jnp.where(first_half, even, odd)

    left_high, left_low = split(left, 2)
    moved = jnp.concatenate([stacked[k] for k in range(count // 2)], axis=1)
    moved_high, moved_low = split(moved, 2)
    done = jnp.dot(
        jnp.concatenate([left_high, left_high, left_low], axis=1),
        jnp.concatenate([moved_high, moved_low, moved_high], axis=0),
        preferred_element_type=jnp.float32,
    )
    for k in range(count // 2):
        stacked[k] = done[:, k * LANES : (k + 1) * LANES]

    for q in range(0, count, 2):
        upper = stacked[q // 2, pl.ds(0, pairs, stride=2), :]
        lower = stacked[q // 2, pl.ds(1, pairs, stride=2), :]
        placed[pl.ds(q, pairs, stride=count), :] = jnp.where(first_half, upper, pltpu.roll(lower, inner, 1))
        placed[pl.ds(q + 1, pairs, stride=count), :] = jnp.where(
            first_half, pltpu.roll(upper, inner, 1), lower
        )
    for k in range(pairs):
        put(k, placed[k * count : (k + 1) * count, :].astype(jnp.bfloat16))


def condition_kernel(other, queries, left, right, out, block_in, left_in, right_in, spread, stacked, placed, arrived):
    part = lax.axis_index("parts")
    layer = 1 - part if other else part
    copies = [
        pltpu.make_async_copy(source, target, arrived.at[k])
        for k, (source, target) in enumerate(
            ((queries.at[layer, 0], block_in), (right.at[layer], right_in), (left.at[layer], left_in))
        )
    ]
    for copy in copies:
        copy.start()
    for copy in copies:
        copy.wait()

    def put(k, tile):
        out[:, k * LANES : (k + 1) * LANES] = tile

    condition_block(block_in[...], left_in[...], right_in[...], put, spread, stacked, placed)


def condition_layer(other, queries, left_factor, right_factor):
    _, _, count, width = queries.shape
    pairs = width // LANES
    far = pl.BlockSpec(memory_space=pltpu.HBM)
    return pl.pallas_call(
        functools.partial(condition_kernel, other),
        out_shape=jax.ShapeDtypeStruct((count, width), jnp.bfloat16),
        in_specs=[far] * 3,
        out_specs=pl.BlockSpec(memory_space=pltpu.VMEM),
        scratch_shapes=[
            pltpu.VMEM((count, width), jnp.bfloat16),
            pltpu.VMEM(left_factor.shape[1:], jnp.float32),
            pltpu.VMEM(right_factor.shape[1:], jnp.float32),
            pltpu.VMEM((2, pairs * count, LANES), jnp.float32),
            pltpu.VMEM((count // 2, 2 * pairs, LANES), jnp.float32),
            pltpu.VMEM((pairs * count, LANES), jnp.float32),
            pltpu.SemaphoreType.DMA((3,)),
        ],
        compiler_params=pltpu.CompilerParams(vmem_limit_bytes=8 * 2**20),
        cost_estimate=pl.CostEstimate(flops=2**27, bytes_accessed=2**19, transcendentals=0),
        name="condition_other" if other else "condition_mine",
    )(*(pltpu.with_memory_space_constraint(x, pltpu.HBM) for x in (queries, left_factor, right_factor)))


def along_columns(value, flip):
    return lax.ppermute(value, "train", [(k, k ^ (flip * PAIR)) for k in range(COLUMNS * PAIR)])


def other_core(value):
    return lax.ppermute(value, "train", [(k, k ^ 1) for k in range(COLUMNS * PAIR)])


def other_part(value, cross=False):
    train = COLUMNS * PAIR
    pairs = [(part * train + k, (1 - part) * train + (k ^ cross)) for part in range(2) for k in range(train)]
    return lax.ppermute(value, ("parts", "train"), pairs)


def copy_kernel(source, target, done):
    copy = pltpu.make_async_copy(source, target, done)
    copy.start()
    copy.wait()


def copy_near(value):
    return pl.pallas_call(
        copy_kernel,
        out_shape=jax.ShapeDtypeStruct(value.shape, value.dtype),
        in_specs=[pl.BlockSpec(memory_space=pltpu.HBM)],
        out_specs=pl.BlockSpec(memory_space=pltpu.VMEM),
        scratch_shapes=[pltpu.SemaphoreType.DMA],
        compiler_params=pltpu.CompilerParams(vmem_limit_bytes=6 * 2**20),
        cost_estimate=pl.CostEstimate(flops=0, bytes_accessed=2 * value.size * 2, transcendentals=0),
        name="near",
    )(pltpu.with_memory_space_constraint(value, pltpu.HBM))


def scores_kernel(away, train, *refs):
    blocks, (scores, terms) = refs[:-2], refs[-2:]
    part, here = lax.axis_index("parts"), lax.axis_index("layer")
    count, width = blocks[0].shape
    rows, layer_count, _ = train.shape
    share, queries = scores.shape

    mine, other, s2, s1, s3, t2, y1, y3 = (blocks[k : k + PAIR] for k in range(0, len(blocks), PAIR))
    order = [*mine, *s1, *s2, *s3, *other, *y1[::-1], *t2, *y3]
    first = pl.multiple_of((1 - here if away else here) * share * layer_count, share * layer_count)
    both = lax.dot_general(
        train.reshape(rows * layer_count, width)[pl.ds(first, share * layer_count), :],
        jnp.concatenate([block[...] for block in order], axis=0),
        LANES_LAST,
        preferred_element_type=jnp.float32,
    )
    for k in range(layer_count):
        terms[k] = both[:, k * queries : (k + 1) * queries]
    total = (
        terms[0, pl.ds(part, share, stride=layer_count), :] + terms[1, pl.ds(1 - part, share, stride=layer_count), :]
    )

    place = lax.axis_index("train")
    lane = lax.broadcasted_iota(jnp.int32, (share, queries), 1)
    span = count
    while span < queries:
        swapped = jnp.where((lane & span) == 0, pltpu.roll(total, queries - span, 1), pltpu.roll(total, span, 1))
        odd = jnp.full((share, queries), place & (span // count), jnp.int32) != 0
        total = jnp.where(odd, swapped, total)
        span *= 2
    scores[...] = total


def local_call(kernel, name, out_shape, scratch_shapes, *operands):
    spec = pl.BlockSpec(memory_space=pltpu.VMEM)
    return pl.pallas_call(
        kernel,
        out_shape=out_shape,
        in_specs=[spec] * len(operands),
        out_specs=jax.tree.map(lambda _: spec, out_shape),
        scratch_shapes=scratch_shapes,
        compiler_params=pltpu.CompilerParams(vmem_limit_bytes=24 * 2**20),
        cost_estimate=pl.CostEstimate(flops=2**29, bytes_accessed=2**22, transcendentals=0),
        name=name,
    )(*operands)


def direct(train_grads, queries, left_factor, right_factor):
    rows, layer_count, width = train_grads.shape
    count = queries.shape[2]
    total = count * COLUMNS * PAIR
    share = rows // 2

    mine = condition_layer(False, queries, left_factor, right_factor)
    other = condition_layer(True, queries, left_factor, right_factor)
    near = copy_near(train_grads)
    s1 = along_columns(mine, 1)
    s3 = along_columns(mine, 3)
    s3, near = lax.optimization_barrier((s3, near))
    s2 = along_columns(s3, 1)
    t2 = along_columns(other, 2)
    y1 = other_part(s1, cross=True)
    y3 = other_part(s3)
    s2, y1, y3, t2 = lax.optimization_barrier((s2, y1, y3, t2))

    blocks = []
    for block in (mine, other, s2, s1, s3, t2, y1, y3):
        blocks += [block, other_core(block)]
    def scores(away):
        return local_call(
            functools.partial(scores_kernel, away),
            "scores_sent" if away else "scores_kept",
            jax.ShapeDtypeStruct((share, total), jnp.float32),
            [pltpu.VMEM((layer_count, share * layer_count, total), jnp.float32)],
            near,
            *blocks,
        )

    received = lax.ppermute(scores(True), "layer", [(0, 1), (1, 0)])
    return scores(False) + received


def general(shape, train_grads, queries, left_factor, right_factor):
    layers = shape["layer"]
    own = condition(queries[:, 0], left_factor, right_factor)
    block = lax.all_gather(own, "train", axis=1, tiled=True)
    share = train_grads.shape[0] // layers
    here = lax.axis_index("layer")

    def terms(step):
        rows = lax.dynamic_slice_in_dim(train_grads, (here + step) % layers * share, share, 0)
        return jnp.einsum("fkm,krm->fr", rows, block, preferred_element_type=jnp.float32)

    scores = terms(0)
    for step in range(1, layers):
        scores += lax.ppermute(terms(step), "layer", [(k, (k + step) % layers) for k in range(layers)])
    return scores


def body(shape, train_grads, queries, left_factor, right_factor):
    fits = (
        shape["train"] == COLUMNS * PAIR
        and shape["parts"] == shape["layer"] == 2
        and shape["query"] == 1
        and train_grads.shape[0] == 2 * LANES
        and train_grads.shape[1:] == (2, 4096)
        and queries.shape[1:] == (1, 16, 4096)
        and left_factor.shape[1:] == right_factor.shape[1:] == (64, 64)
    )
    if fits:
        return direct(train_grads, queries, left_factor, right_factor)
    return general(shape, train_grads, queries, left_factor, right_factor)


def solution(mesh):
    return jax.shard_map(
        functools.partial(body, dict(mesh.shape)),
        mesh=mesh,
        in_specs=(
            P(("parts", "train"), "layer", None),
            P("layer", "query", "train", None),
            P("layer", None, None),
            P("layer", None, None),
        ),
        out_specs=P(("parts", "train", "layer"), "query"),
        check_vma=False,
    )
```

```python
import functools

import jax
import jax.numpy as jnp
from jax import lax
from jax.experimental import pallas as pl
from jax.experimental.pallas import tpu as pltpu
from jax.sharding import PartitionSpec as P

LANES = 128
PAIR = 2
COLUMNS = 4
LANES_LAST = (((1,), (1,)), ((), ()))


def split(value, parts):
    pieces = []
    for _ in range(parts):
        piece = value.astype(jnp.bfloat16)
        pieces.append(piece)
        value = value - piece.astype(jnp.float32)
    return pieces


def condition(own, left_factor, right_factor):
    layer_count, count, width = own.shape
    rows_out, rows_in = left_factor.shape[1], right_factor.shape[1]
    grid = own.astype(jnp.float32).reshape(layer_count, count, rows_out, rows_in)
    left_part = jnp.einsum("lab,lnbc->lnac", left_factor, grid, precision=lax.Precision.HIGHEST)
    both = jnp.einsum("lnac,lcd->lnad", left_part, right_factor, precision=lax.Precision.HIGHEST)
    return both.reshape(layer_count, count, width).astype(jnp.bfloat16)


def condition_block(block, left, right, put, spread, stacked, placed):
    count, width = block.shape
    inner = right.shape[0]
    pairs = width // LANES
    first_half = lax.broadcasted_iota(jnp.int32, (pairs, LANES), 1) < inner

    empty = jnp.zeros((inner, LANES), jnp.float32)
    twice = jnp.concatenate([right, right], axis=1)
    weight = jnp.concatenate(
        [jnp.concatenate([twice, empty], axis=1), jnp.concatenate([empty, twice], axis=1)], axis=0
    )
    high, middle, low = split(weight, 3)
    rows = jnp.concatenate([block[:, k * LANES : (k + 1) * LANES] for k in range(pairs)], axis=0)
    right_part = jnp.dot(
        jnp.concatenate([rows, rows], axis=1),
        jnp.concatenate([high, middle], axis=0),
        preferred_element_type=jnp.float32,
    ) + jnp.dot(rows, low, preferred_element_type=jnp.float32)
    spread[0] = right_part[:, :LANES]
    spread[1] = right_part[:, LANES:]

    for q in range(0, count, 2):
        for j in range(2):
            even = spread[j, pl.ds(q, pairs, stride=count), :]
            odd = spread[j, pl.ds(q + 1, pairs, stride=count), :]
            stacked[q // 2, pl.ds(j, pairs, stride=2), :] = jnp.where(first_half, even, odd)

    left_high, left_low = split(left, 2)
    moved = jnp.concatenate([stacked[k] for k in range(count // 2)], axis=1)
    moved_high, moved_low = split(moved, 2)
    done = jnp.dot(
        jnp.concatenate([left_high, left_high, left_low], axis=1),
        jnp.concatenate([moved_high, moved_low, moved_high], axis=0),
        preferred_element_type=jnp.float32,
    )
    for k in range(count // 2):
        stacked[k] = done[:, k * LANES : (k + 1) * LANES]

    for q in range(0, count, 2):
        upper = stacked[q // 2, pl.ds(0, pairs, stride=2), :]
        lower = stacked[q // 2, pl.ds(1, pairs, stride=2), :]
        placed[pl.ds(q, pairs, stride=count), :] = jnp.where(first_half, upper, pltpu.roll(lower, inner, 1))
        placed[pl.ds(q + 1, pairs, stride=count), :] = jnp.where(
            first_half, pltpu.roll(upper, inner, 1), lower
        )
    for k in range(pairs):
        put(k, placed[k * count : (k + 1) * count, :].astype(jnp.bfloat16))


def condition_kernel(other, queries, left, right, out, block_in, left_in, right_in, spread, stacked, placed, arrived):
    part = lax.axis_index("parts")
    layer = 1 - part if other else part
    copies = [
        pltpu.make_async_copy(source, target, arrived.at[k])
        for k, (source, target) in enumerate(
            ((queries.at[layer, 0], block_in), (right.at[layer], right_in), (left.at[layer], left_in))
        )
    ]
    for copy in copies:
        copy.start()
    for copy in copies:
        copy.wait()

    def put(k, tile):
        out[:, k * LANES : (k + 1) * LANES] = tile

    condition_block(block_in[...], left_in[...], right_in[...], put, spread, stacked, placed)


def condition_layer(other, queries, left_factor, right_factor):
    _, _, count, width = queries.shape
    pairs = width // LANES
    far = pl.BlockSpec(memory_space=pltpu.HBM)
    return pl.pallas_call(
        functools.partial(condition_kernel, other),
        out_shape=jax.ShapeDtypeStruct((count, width), jnp.bfloat16),
        in_specs=[far] * 3,
        out_specs=pl.BlockSpec(memory_space=pltpu.VMEM),
        scratch_shapes=[
            pltpu.VMEM((count, width), jnp.bfloat16),
            pltpu.VMEM(left_factor.shape[1:], jnp.float32),
            pltpu.VMEM(right_factor.shape[1:], jnp.float32),
            pltpu.VMEM((2, pairs * count, LANES), jnp.float32),
            pltpu.VMEM((count // 2, 2 * pairs, LANES), jnp.float32),
            pltpu.VMEM((pairs * count, LANES), jnp.float32),
            pltpu.SemaphoreType.DMA((3,)),
        ],
        compiler_params=pltpu.CompilerParams(vmem_limit_bytes=8 * 2**20),
        cost_estimate=pl.CostEstimate(flops=2**27, bytes_accessed=2**19, transcendentals=0),
        name="condition_other" if other else "condition_mine",
    )(*(pltpu.with_memory_space_constraint(x, pltpu.HBM) for x in (queries, left_factor, right_factor)))


def along_columns(value, flip):
    return lax.ppermute(value, "train", [(k, k ^ (flip * PAIR)) for k in range(COLUMNS * PAIR)])


def other_core(value):
    return lax.ppermute(value, "train", [(k, k ^ 1) for k in range(COLUMNS * PAIR)])


def other_part(value, cross=False):
    train = COLUMNS * PAIR
    pairs = [(part * train + k, (1 - part) * train + (k ^ cross)) for part in range(2) for k in range(train)]
    return lax.ppermute(value, ("parts", "train"), pairs)


def copy_kernel(source, target, done):
    copy = pltpu.make_async_copy(source, target, done)
    copy.start()
    copy.wait()


def copy_near(value):
    return pl.pallas_call(
        copy_kernel,
        out_shape=jax.ShapeDtypeStruct(value.shape, value.dtype),
        in_specs=[pl.BlockSpec(memory_space=pltpu.HBM)],
        out_specs=pl.BlockSpec(memory_space=pltpu.VMEM),
        scratch_shapes=[pltpu.SemaphoreType.DMA],
        compiler_params=pltpu.CompilerParams(vmem_limit_bytes=6 * 2**20),
        cost_estimate=pl.CostEstimate(flops=0, bytes_accessed=2 * value.size * 2, transcendentals=0),
        name="near",
    )(pltpu.with_memory_space_constraint(value, pltpu.HBM))


def place():
    member = lax.axis_index("train")
    return member // PAIR, lax.rem(member, PAIR)


def row_scores(train, table, owner, terms, scores):
    share = scores.shape[0]
    rows, layer_count, width = train.shape
    queries = table.shape[1]
    first = pl.multiple_of(owner * share * layer_count, share * layer_count)
    both = lax.dot_general(
        train.reshape(rows * layer_count, width)[pl.ds(first, share * layer_count), :],
        table[...].reshape(layer_count * queries, width),
        LANES_LAST,
        preferred_element_type=jnp.float32,
    )
    for layer in range(layer_count):
        terms[layer] = both[:, layer * queries : (layer + 1) * queries]
    scores[...] = sum(terms[layer, pl.ds(layer, share, stride=layer_count), :] for layer in range(layer_count))


def sent_kernel(train, *refs):
    blocks, (scores, table, terms) = refs[:-3], refs[-3:]
    part = lax.axis_index("parts")
    column, core = place()
    count = blocks[0].shape[0]

    def put(layer, flip, other, block):
        member = (column ^ flip) * PAIR + (core ^ other)
        table[layer, pl.ds(pl.multiple_of(member * count, count), count), :] = block

    for twin in range(PAIR):
        for k, (layer, flip, cross) in enumerate(
            (
                (part, 0, 0),
                (1 - part, 0, 0),
                (part, 2, 0),
                (part, 1, 0),
                (part, 3, 0),
                (1 - part, 2, 0),
                (1 - part, 1, 1),
                (1 - part, 3, 0),
            )
        ):
            put(layer, flip, twin ^ cross, blocks[PAIR * k + twin][...])
    row_scores(train, table, 1 - lax.axis_index("layer"), terms, scores)


def kept_kernel(train, table, scores, terms):
    row_scores(train, table, lax.axis_index("layer"), terms, scores)


def local_call(kernel, name, out_shape, scratch_shapes, *operands):
    spec = pl.BlockSpec(memory_space=pltpu.VMEM)
    return pl.pallas_call(
        kernel,
        out_shape=out_shape,
        in_specs=[spec] * len(operands),
        out_specs=jax.tree.map(lambda _: spec, out_shape),
        scratch_shapes=scratch_shapes,
        compiler_params=pltpu.CompilerParams(vmem_limit_bytes=24 * 2**20),
        cost_estimate=pl.CostEstimate(flops=2**29, bytes_accessed=2**22, transcendentals=0),
        name=name,
    )(*operands)


def direct(train_grads, queries, left_factor, right_factor):
    rows, layer_count, width = train_grads.shape
    count = queries.shape[2]
    total = count * COLUMNS * PAIR
    share = rows // 2

    mine = condition_layer(False, queries, left_factor, right_factor)
    other = condition_layer(True, queries, left_factor, right_factor)
    near = copy_near(train_grads)
    s1 = along_columns(mine, 1)
    s3 = along_columns(mine, 3)
    s3, near = lax.optimization_barrier((s3, near))
    s2 = along_columns(s3, 1)
    t2 = along_columns(other, 2)
    y1 = other_part(s1, cross=True)
    y3 = other_part(s3)
    y1_c = other_core(y1)
    s2, y3, y1_c = lax.optimization_barrier((s2, y3, y1_c))

    blocks = [
        mine, other_core(mine),
        other, other_core(other),
        s2, other_core(s2),
        s1, other_core(s1),
        s3, other_core(s3),
        t2, other_core(t2),
        y1, y1_c,
        y3, other_core(y3),
    ]
    f32 = functools.partial(jax.ShapeDtypeStruct, dtype=jnp.float32)
    terms = [pltpu.VMEM((layer_count, share * layer_count, total), jnp.float32)]
    sent, table = local_call(
        sent_kernel,
        "scores_sent",
        [f32((share, total)), jax.ShapeDtypeStruct((layer_count, total, width), jnp.bfloat16)],
        terms,
        near,
        *blocks,
    )
    received = lax.ppermute(sent, "layer", [(0, 1), (1, 0)])
    kept = local_call(kept_kernel, "scores_kept", f32((share, total)), terms, near, table)
    return kept + received


def general(shape, train_grads, queries, left_factor, right_factor):
    layers = shape["layer"]
    own = condition(queries[:, 0], left_factor, right_factor)
    block = lax.all_gather(own, "train", axis=1, tiled=True)
    share = train_grads.shape[0] // layers
    here = lax.axis_index("layer")

    def terms(step):
        rows = lax.dynamic_slice_in_dim(train_grads, (here + step) % layers * share, share, 0)
        return jnp.einsum("fkm,krm->fr", rows, block, preferred_element_type=jnp.float32)

    scores = terms(0)
    for step in range(1, layers):
        scores += lax.ppermute(terms(step), "layer", [(k, (k + step) % layers) for k in range(layers)])
    return scores


def body(shape, train_grads, queries, left_factor, right_factor):
    fits = (
        shape["train"] == COLUMNS * PAIR
        and shape["parts"] == shape["layer"] == 2
        and shape["query"] == 1
        and train_grads.shape[0] == 2 * LANES
        and train_grads.shape[1:] == (2, 4096)
        and queries.shape[1:] == (1, 16, 4096)
        and left_factor.shape[1:] == right_factor.shape[1:] == (64, 64)
    )
    if fits:
        return direct(train_grads, queries, left_factor, right_factor)
    return general(shape, train_grads, queries, left_factor, right_factor)


def solution(mesh):
    return jax.shard_map(
        functools.partial(body, dict(mesh.shape)),
        mesh=mesh,
        in_specs=(
            P(("parts", "train"), "layer", None),
            P("layer", "query", "train", None),
            P("layer", None, None),
            P("layer", None, None),
        ),
        out_specs=P(("parts", "train", "layer"), "query"),
        check_vma=False,
    )
```

```python
import functools

import jax
import jax.numpy as jnp
from jax import lax
from jax.experimental import pallas as pl
from jax.experimental.pallas import tpu as pltpu
from jax.sharding import PartitionSpec as P

LANES = 128
PAIR = 2
COLUMNS = 4
LANES_LAST = (((1,), (1,)), ((), ()))


def split(value, parts):
    pieces = []
    for _ in range(parts):
        piece = value.astype(jnp.bfloat16)
        pieces.append(piece)
        value = value - piece.astype(jnp.float32)
    return pieces


def condition(own, left_factor, right_factor):
    layer_count, count, width = own.shape
    rows_out, rows_in = left_factor.shape[1], right_factor.shape[1]
    grid = own.astype(jnp.float32).reshape(layer_count, count, rows_out, rows_in)
    left_part = jnp.einsum("lab,lnbc->lnac", left_factor, grid, precision=lax.Precision.HIGHEST)
    both = jnp.einsum("lnac,lcd->lnad", left_part, right_factor, precision=lax.Precision.HIGHEST)
    return both.reshape(layer_count, count, width).astype(jnp.bfloat16)


def condition_block(block, left, right, put, spread, stacked, placed):
    count, width = block.shape
    inner = right.shape[0]
    pairs = width // LANES
    first_half = lax.broadcasted_iota(jnp.int32, (pairs, LANES), 1) < inner

    empty = jnp.zeros((inner, LANES), jnp.float32)
    twice = jnp.concatenate([right, right], axis=1)
    weight = jnp.concatenate(
        [jnp.concatenate([twice, empty], axis=1), jnp.concatenate([empty, twice], axis=1)], axis=0
    )
    high, middle, low = split(weight, 3)
    rows = jnp.concatenate([block[:, k * LANES : (k + 1) * LANES] for k in range(pairs)], axis=0)
    right_part = jnp.dot(
        jnp.concatenate([rows, rows], axis=1),
        jnp.concatenate([high, middle], axis=0),
        preferred_element_type=jnp.float32,
    ) + jnp.dot(rows, low, preferred_element_type=jnp.float32)
    spread[0] = right_part[:, :LANES]
    spread[1] = right_part[:, LANES:]

    for q in range(0, count, 2):
        for j in range(2):
            even = spread[j, pl.ds(q, pairs, stride=count), :]
            odd = spread[j, pl.ds(q + 1, pairs, stride=count), :]
            stacked[q // 2, pl.ds(j, pairs, stride=2), :] = jnp.where(first_half, even, odd)

    left_high, left_low = split(left, 2)
    moved = jnp.concatenate([stacked[k] for k in range(count // 2)], axis=1)
    moved_high, moved_low = split(moved, 2)
    done = jnp.dot(
        jnp.concatenate([left_high, left_high, left_low], axis=1),
        jnp.concatenate([moved_high, moved_low, moved_high], axis=0),
        preferred_element_type=jnp.float32,
    )
    for k in range(count // 2):
        stacked[k] = done[:, k * LANES : (k + 1) * LANES]

    for q in range(0, count, 2):
        upper = stacked[q // 2, pl.ds(0, pairs, stride=2), :]
        lower = stacked[q // 2, pl.ds(1, pairs, stride=2), :]
        placed[pl.ds(q, pairs, stride=count), :] = jnp.where(first_half, upper, pltpu.roll(lower, inner, 1))
        placed[pl.ds(q + 1, pairs, stride=count), :] = jnp.where(
            first_half, pltpu.roll(upper, inner, 1), lower
        )
    for k in range(pairs):
        put(k, placed[k * count : (k + 1) * count, :].astype(jnp.bfloat16))


def condition_kernel(other, queries, left, right, out, block_in, left_in, right_in, spread, stacked, placed, arrived):
    part = lax.axis_index("parts")
    layer = 1 - part if other else part
    copies = [
        pltpu.make_async_copy(source, target, arrived.at[k])
        for k, (source, target) in enumerate(
            ((queries.at[layer, 0], block_in), (right.at[layer], right_in), (left.at[layer], left_in))
        )
    ]
    for copy in copies:
        copy.start()
    for copy in copies:
        copy.wait()

    def put(k, tile):
        out[:, k * LANES : (k + 1) * LANES] = tile

    condition_block(block_in[...], left_in[...], right_in[...], put, spread, stacked, placed)


def condition_layer(other, queries, left_factor, right_factor):
    _, _, count, width = queries.shape
    pairs = width // LANES
    far = pl.BlockSpec(memory_space=pltpu.HBM)
    return pl.pallas_call(
        functools.partial(condition_kernel, other),
        out_shape=jax.ShapeDtypeStruct((count, width), jnp.bfloat16),
        in_specs=[far] * 3,
        out_specs=pl.BlockSpec(memory_space=pltpu.VMEM),
        scratch_shapes=[
            pltpu.VMEM((count, width), jnp.bfloat16),
            pltpu.VMEM(left_factor.shape[1:], jnp.float32),
            pltpu.VMEM(right_factor.shape[1:], jnp.float32),
            pltpu.VMEM((2, pairs * count, LANES), jnp.float32),
            pltpu.VMEM((count // 2, 2 * pairs, LANES), jnp.float32),
            pltpu.VMEM((pairs * count, LANES), jnp.float32),
            pltpu.SemaphoreType.DMA((3,)),
        ],
        compiler_params=pltpu.CompilerParams(vmem_limit_bytes=8 * 2**20),
        cost_estimate=pl.CostEstimate(flops=2**27, bytes_accessed=2**19, transcendentals=0),
        name="condition_other" if other else "condition_mine",
    )(*(pltpu.with_memory_space_constraint(x, pltpu.HBM) for x in (queries, left_factor, right_factor)))


def along_columns(value, flip):
    return lax.ppermute(value, "train", [(k, k ^ (flip * PAIR)) for k in range(COLUMNS * PAIR)])


def other_core(value):
    return lax.ppermute(value, "train", [(k, k ^ 1) for k in range(COLUMNS * PAIR)])


def other_part(value, cross=False):
    train = COLUMNS * PAIR
    pairs = [(part * train + k, (1 - part) * train + (k ^ cross)) for part in range(2) for k in range(train)]
    return lax.ppermute(value, ("parts", "train"), pairs)


def copy_kernel(source, target, done):
    copy = pltpu.make_async_copy(source, target, done)
    copy.start()
    copy.wait()


def copy_near(value):
    return pl.pallas_call(
        copy_kernel,
        out_shape=jax.ShapeDtypeStruct(value.shape, value.dtype),
        in_specs=[pl.BlockSpec(memory_space=pltpu.HBM)],
        out_specs=pl.BlockSpec(memory_space=pltpu.VMEM),
        scratch_shapes=[pltpu.SemaphoreType.DMA],
        compiler_params=pltpu.CompilerParams(vmem_limit_bytes=6 * 2**20),
        cost_estimate=pl.CostEstimate(flops=0, bytes_accessed=2 * value.size * 2, transcendentals=0),
        name="near",
    )(pltpu.with_memory_space_constraint(value, pltpu.HBM))


def place():
    member = lax.axis_index("train")
    return member // PAIR, lax.rem(member, PAIR)


def row_scores(train, table, owner, terms, scores):
    share = scores.shape[0]
    rows, layer_count, width = train.shape
    queries = table.shape[1]
    first = pl.multiple_of(owner * share * layer_count, share * layer_count)
    both = lax.dot_general(
        train.reshape(rows * layer_count, width)[pl.ds(first, share * layer_count), :],
        table[...].reshape(layer_count * queries, width),
        LANES_LAST,
        preferred_element_type=jnp.float32,
    )
    for layer in range(layer_count):
        terms[layer] = both[:, layer * queries : (layer + 1) * queries]
    scores[...] = sum(terms[layer, pl.ds(layer, share, stride=layer_count), :] for layer in range(layer_count))


def sent_kernel(train, *refs):
    blocks, (scores, table, terms) = refs[:-3], refs[-3:]
    part = lax.axis_index("parts")
    column, core = place()
    count = blocks[0].shape[0]

    def put(layer, flip, other, block):
        member = (column ^ flip) * PAIR + (core ^ other)
        table[layer, pl.ds(pl.multiple_of(member * count, count), count), :] = block

    for twin in range(PAIR):
        for k, (layer, flip, cross) in enumerate(
            (
                (part, 0, 0),
                (1 - part, 0, 0),
                (part, 2, 0),
                (part, 1, 0),
                (part, 3, 0),
                (1 - part, 2, 0),
                (1 - part, 1, 1),
                (1 - part, 3, 0),
            )
        ):
            put(layer, flip, twin ^ cross, blocks[PAIR * k + twin][...])
    row_scores(train, table, 1 - lax.axis_index("layer"), terms, scores)


def kept_kernel(train, table, scores, terms):
    row_scores(train, table, lax.axis_index("layer"), terms, scores)


def local_call(kernel, name, out_shape, scratch_shapes, *operands):
    spec = pl.BlockSpec(memory_space=pltpu.VMEM)
    return pl.pallas_call(
        kernel,
        out_shape=out_shape,
        in_specs=[spec] * len(operands),
        out_specs=jax.tree.map(lambda _: spec, out_shape),
        scratch_shapes=scratch_shapes,
        compiler_params=pltpu.CompilerParams(vmem_limit_bytes=24 * 2**20),
        cost_estimate=pl.CostEstimate(flops=2**29, bytes_accessed=2**22, transcendentals=0),
        name=name,
    )(*operands)


def direct(train_grads, queries, left_factor, right_factor):
    rows, layer_count, width = train_grads.shape
    count = queries.shape[2]
    total = count * COLUMNS * PAIR
    share = rows // 2

    mine = condition_layer(False, queries, left_factor, right_factor)
    other = condition_layer(True, queries, left_factor, right_factor)
    near = copy_near(train_grads)
    s1 = along_columns(mine, 1)
    s3 = along_columns(mine, 3)
    s1, s3, near = lax.optimization_barrier((s1, s3, near))
    s2 = along_columns(s3, 1)
    t2 = along_columns(other, 2)
    y1 = other_part(s1, cross=True)
    y3 = other_part(s3)
    s2, y1, y3, t2 = lax.optimization_barrier((s2, y1, y3, t2))

    blocks = []
    for block in (mine, other, s2, s1, s3, t2, y1, y3):
        blocks += [block, other_core(block)]
    f32 = functools.partial(jax.ShapeDtypeStruct, dtype=jnp.float32)
    terms = [pltpu.VMEM((layer_count, share * layer_count, total), jnp.float32)]
    sent, table = local_call(
        sent_kernel,
        "scores_sent",
        [f32((share, total)), jax.ShapeDtypeStruct((layer_count, total, width), jnp.bfloat16)],
        terms,
        near,
        *blocks,
    )
    received = lax.ppermute(sent, "layer", [(0, 1), (1, 0)])
    kept = local_call(kept_kernel, "scores_kept", f32((share, total)), terms, near, table)
    return kept + received


def general(shape, train_grads, queries, left_factor, right_factor):
    layers = shape["layer"]
    own = condition(queries[:, 0], left_factor, right_factor)
    block = lax.all_gather(own, "train", axis=1, tiled=True)
    share = train_grads.shape[0] // layers
    here = lax.axis_index("layer")

    def terms(step):
        rows = lax.dynamic_slice_in_dim(train_grads, (here + step) % layers * share, share, 0)
        return jnp.einsum("fkm,krm->fr", rows, block, preferred_element_type=jnp.float32)

    scores = terms(0)
    for step in range(1, layers):
        scores += lax.ppermute(terms(step), "layer", [(k, (k + step) % layers) for k in range(layers)])
    return scores


def body(shape, train_grads, queries, left_factor, right_factor):
    fits = (
        shape["train"] == COLUMNS * PAIR
        and shape["parts"] == shape["layer"] == 2
        and shape["query"] == 1
        and train_grads.shape[0] == 2 * LANES
        and train_grads.shape[1:] == (2, 4096)
        and queries.shape[1:] == (1, 16, 4096)
        and left_factor.shape[1:] == right_factor.shape[1:] == (64, 64)
    )
    if fits:
        return direct(train_grads, queries, left_factor, right_factor)
    return general(shape, train_grads, queries, left_factor, right_factor)


def solution(mesh):
    return jax.shard_map(
        functools.partial(body, dict(mesh.shape)),
        mesh=mesh,
        in_specs=(
            P(("parts", "train"), "layer", None),
            P("layer", "query", "train", None),
            P("layer", None, None),
            P("layer", None, None),
        ),
        out_specs=P(("parts", "train", "layer"), "query"),
        check_vma=False,
    )
```

```python
import functools

import jax
import jax.numpy as jnp
from jax import lax
from jax.experimental import pallas as pl
from jax.experimental.pallas import tpu as pltpu
from jax.sharding import PartitionSpec as P

LANES = 128
PAIR = 2
COLUMNS = 4
LANES_LAST = (((1,), (1,)), ((), ()))


def split(value, parts):
    pieces = []
    for _ in range(parts):
        piece = value.astype(jnp.bfloat16)
        pieces.append(piece)
        value = value - piece.astype(jnp.float32)
    return pieces


def condition(own, left_factor, right_factor):
    layer_count, count, width = own.shape
    rows_out, rows_in = left_factor.shape[1], right_factor.shape[1]
    grid = own.astype(jnp.float32).reshape(layer_count, count, rows_out, rows_in)
    left_part = jnp.einsum("lab,lnbc->lnac", left_factor, grid, precision=lax.Precision.HIGHEST)
    both = jnp.einsum("lnac,lcd->lnad", left_part, right_factor, precision=lax.Precision.HIGHEST)
    return both.reshape(layer_count, count, width).astype(jnp.bfloat16)


def condition_block(block, left, right, put, spread, stacked, placed):
    count, width = block.shape
    inner = right.shape[0]
    pairs = width // LANES
    first_half = lax.broadcasted_iota(jnp.int32, (pairs, LANES), 1) < inner

    empty = jnp.zeros((inner, LANES), jnp.float32)
    twice = jnp.concatenate([right, right], axis=1)
    weight = jnp.concatenate(
        [jnp.concatenate([twice, empty], axis=1), jnp.concatenate([empty, twice], axis=1)], axis=0
    )
    high, middle, low = split(weight, 3)
    rows = jnp.concatenate([block[:, k * LANES : (k + 1) * LANES] for k in range(pairs)], axis=0)
    right_part = jnp.dot(
        jnp.concatenate([rows, rows], axis=1),
        jnp.concatenate([high, middle], axis=0),
        preferred_element_type=jnp.float32,
    ) + jnp.dot(rows, low, preferred_element_type=jnp.float32)
    spread[0] = right_part[:, :LANES]
    spread[1] = right_part[:, LANES:]

    for q in range(0, count, 2):
        for j in range(2):
            even = spread[j, pl.ds(q, pairs, stride=count), :]
            odd = spread[j, pl.ds(q + 1, pairs, stride=count), :]
            stacked[q // 2, pl.ds(j, pairs, stride=2), :] = jnp.where(first_half, even, odd)

    left_high, left_low = split(left, 2)
    moved = jnp.concatenate([stacked[k] for k in range(count // 2)], axis=1)
    moved_high, moved_low = split(moved, 2)
    done = jnp.dot(
        jnp.concatenate([left_high, left_high, left_low], axis=1),
        jnp.concatenate([moved_high, moved_low, moved_high], axis=0),
        preferred_element_type=jnp.float32,
    )
    for k in range(count // 2):
        stacked[k] = done[:, k * LANES : (k + 1) * LANES]

    for q in range(0, count, 2):
        upper = stacked[q // 2, pl.ds(0, pairs, stride=2), :]
        lower = stacked[q // 2, pl.ds(1, pairs, stride=2), :]
        placed[pl.ds(q, pairs, stride=count), :] = jnp.where(first_half, upper, pltpu.roll(lower, inner, 1))
        placed[pl.ds(q + 1, pairs, stride=count), :] = jnp.where(
            first_half, pltpu.roll(upper, inner, 1), lower
        )
    for k in range(pairs):
        put(k, placed[k * count : (k + 1) * count, :].astype(jnp.bfloat16))


def condition_kernel(other, queries, left, right, out, block_in, left_in, right_in, spread, stacked, placed, arrived):
    part = lax.axis_index("parts")
    layer = 1 - part if other else part
    copies = [
        pltpu.make_async_copy(source, target, arrived.at[k])
        for k, (source, target) in enumerate(
            ((queries.at[layer, 0], block_in), (right.at[layer], right_in), (left.at[layer], left_in))
        )
    ]
    for copy in copies:
        copy.start()
    for copy in copies:
        copy.wait()

    def put(k, tile):
        out[:, k * LANES : (k + 1) * LANES] = tile

    condition_block(block_in[...], left_in[...], right_in[...], put, spread, stacked, placed)


def condition_layer(other, queries, left_factor, right_factor):
    _, _, count, width = queries.shape
    pairs = width // LANES
    far = pl.BlockSpec(memory_space=pltpu.HBM)
    return pl.pallas_call(
        functools.partial(condition_kernel, other),
        out_shape=jax.ShapeDtypeStruct((count, width), jnp.bfloat16),
        in_specs=[far] * 3,
        out_specs=pl.BlockSpec(memory_space=pltpu.VMEM),
        scratch_shapes=[
            pltpu.VMEM((count, width), jnp.bfloat16),
            pltpu.VMEM(left_factor.shape[1:], jnp.float32),
            pltpu.VMEM(right_factor.shape[1:], jnp.float32),
            pltpu.VMEM((2, pairs * count, LANES), jnp.float32),
            pltpu.VMEM((count // 2, 2 * pairs, LANES), jnp.float32),
            pltpu.VMEM((pairs * count, LANES), jnp.float32),
            pltpu.SemaphoreType.DMA((3,)),
        ],
        compiler_params=pltpu.CompilerParams(vmem_limit_bytes=8 * 2**20),
        cost_estimate=pl.CostEstimate(flops=2**27, bytes_accessed=2**19, transcendentals=0),
        name="condition_other" if other else "condition_mine",
    )(*(pltpu.with_memory_space_constraint(x, pltpu.HBM) for x in (queries, left_factor, right_factor)))


def along_columns(value, flip):
    return lax.ppermute(value, "train", [(k, k ^ (flip * PAIR)) for k in range(COLUMNS * PAIR)])


def other_core(value):
    return lax.ppermute(value, "train", [(k, k ^ 1) for k in range(COLUMNS * PAIR)])


def other_part(value, cross=False):
    train = COLUMNS * PAIR
    pairs = [(part * train + k, (1 - part) * train + (k ^ cross)) for part in range(2) for k in range(train)]
    return lax.ppermute(value, ("parts", "train"), pairs)


def copy_kernel(source, target, done):
    copy = pltpu.make_async_copy(source, target, done)
    copy.start()
    copy.wait()


def copy_near(value):
    return pl.pallas_call(
        copy_kernel,
        out_shape=jax.ShapeDtypeStruct(value.shape, value.dtype),
        in_specs=[pl.BlockSpec(memory_space=pltpu.HBM)],
        out_specs=pl.BlockSpec(memory_space=pltpu.VMEM),
        scratch_shapes=[pltpu.SemaphoreType.DMA],
        compiler_params=pltpu.CompilerParams(vmem_limit_bytes=6 * 2**20),
        cost_estimate=pl.CostEstimate(flops=0, bytes_accessed=2 * value.size * 2, transcendentals=0),
        name="near",
    )(pltpu.with_memory_space_constraint(value, pltpu.HBM))


def place():
    member = lax.axis_index("train")
    return member // PAIR, lax.rem(member, PAIR)


def row_scores(train, table, owner, terms, scores):
    share = scores.shape[0]
    rows, layer_count, width = train.shape
    queries = table.shape[1]
    first = pl.multiple_of(owner * share * layer_count, share * layer_count)
    both = lax.dot_general(
        train.reshape(rows * layer_count, width)[pl.ds(first, share * layer_count), :],
        table[...].reshape(layer_count * queries, width),
        LANES_LAST,
        preferred_element_type=jnp.float32,
    )
    for layer in range(layer_count):
        terms[layer] = both[:, layer * queries : (layer + 1) * queries]
    scores[...] = sum(terms[layer, pl.ds(layer, share, stride=layer_count), :] for layer in range(layer_count))


def sent_kernel(train, *refs):
    other, other_c, mine, s1, s3, first_c, s2, y3, last_c, t2, y1, middle_c, scores, table, terms = refs
    blocks = [other, other_c]
    for group, swapped in (((mine, s1, s3), first_c), ((s2, y3), last_c), ((t2, y1), middle_c)):
        for k, block in enumerate(group):
            blocks += [block, swapped.at[k]]
    part = lax.axis_index("parts")
    column, core = place()
    count = blocks[0].shape[0]

    def put(layer, flip, other, block):
        member = (column ^ flip) * PAIR + (core ^ other)
        table[layer, pl.ds(pl.multiple_of(member * count, count), count), :] = block

    for twin in range(PAIR):
        for k, (layer, flip, cross) in enumerate(
            (
                (1 - part, 0, 0),
                (part, 0, 0),
                (part, 1, 0),
                (part, 3, 0),
                (part, 2, 0),
                (1 - part, 3, 0),
                (1 - part, 2, 0),
                (1 - part, 1, 1),
            )
        ):
            put(layer, flip, twin ^ cross, blocks[PAIR * k + twin][...])
    row_scores(train, table, 1 - lax.axis_index("layer"), terms, scores)


def kept_kernel(train, table, scores, terms):
    row_scores(train, table, lax.axis_index("layer"), terms, scores)


def local_call(kernel, name, out_shape, scratch_shapes, *operands):
    spec = pl.BlockSpec(memory_space=pltpu.VMEM)
    return pl.pallas_call(
        kernel,
        out_shape=out_shape,
        in_specs=[spec] * len(operands),
        out_specs=jax.tree.map(lambda _: spec, out_shape),
        scratch_shapes=scratch_shapes,
        compiler_params=pltpu.CompilerParams(vmem_limit_bytes=24 * 2**20),
        cost_estimate=pl.CostEstimate(flops=2**29, bytes_accessed=2**22, transcendentals=0),
        name=name,
    )(*operands)


def direct(train_grads, queries, left_factor, right_factor):
    rows, layer_count, width = train_grads.shape
    count = queries.shape[2]
    total = count * COLUMNS * PAIR
    share = rows // 2

    mine = condition_layer(False, queries, left_factor, right_factor)
    other = condition_layer(True, queries, left_factor, right_factor)
    near = copy_near(train_grads)
    s1 = along_columns(mine, 1)
    s3 = along_columns(mine, 3)
    s3, near = lax.optimization_barrier((s3, near))
    s2 = along_columns(s3, 1)
    t2 = along_columns(other, 2)
    y1 = other_part(s1, cross=True)
    y3 = other_part(s3)

    blocks = [other, other_core(other)]
    for group in ((mine, s1, s3), (s2, y3), (t2, y1)):
        blocks += [*group, other_core(jnp.stack(group))]
    f32 = functools.partial(jax.ShapeDtypeStruct, dtype=jnp.float32)
    terms = [pltpu.VMEM((layer_count, share * layer_count, total), jnp.float32)]
    sent, table = local_call(
        sent_kernel,
        "scores_sent",
        [f32((share, total)), jax.ShapeDtypeStruct((layer_count, total, width), jnp.bfloat16)],
        terms,
        near,
        *blocks,
    )
    received = lax.ppermute(sent, "layer", [(0, 1), (1, 0)])
    kept = local_call(kept_kernel, "scores_kept", f32((share, total)), terms, near, table)
    return kept + received


def general(shape, train_grads, queries, left_factor, right_factor):
    layers = shape["layer"]
    own = condition(queries[:, 0], left_factor, right_factor)
    block = lax.all_gather(own, "train", axis=1, tiled=True)
    share = train_grads.shape[0] // layers
    here = lax.axis_index("layer")

    def terms(step):
        rows = lax.dynamic_slice_in_dim(train_grads, (here + step) % layers * share, share, 0)
        return jnp.einsum("fkm,krm->fr", rows, block, preferred_element_type=jnp.float32)

    scores = terms(0)
    for step in range(1, layers):
        scores += lax.ppermute(terms(step), "layer", [(k, (k + step) % layers) for k in range(layers)])
    return scores


def body(shape, train_grads, queries, left_factor, right_factor):
    fits = (
        shape["train"] == COLUMNS * PAIR
        and shape["parts"] == shape["layer"] == 2
        and shape["query"] == 1
        and train_grads.shape[0] == 2 * LANES
        and train_grads.shape[1:] == (2, 4096)
        and queries.shape[1:] == (1, 16, 4096)
        and left_factor.shape[1:] == right_factor.shape[1:] == (64, 64)
    )
    if fits:
        return direct(train_grads, queries, left_factor, right_factor)
    return general(shape, train_grads, queries, left_factor, right_factor)


def solution(mesh):
    return jax.shard_map(
        functools.partial(body, dict(mesh.shape)),
        mesh=mesh,
        in_specs=(
            P(("parts", "train"), "layer", None),
            P("layer", "query", "train", None),
            P("layer", None, None),
            P("layer", None, None),
        ),
        out_specs=P(("parts", "train", "layer"), "query"),
        check_vma=False,
    )
```

```python
import functools

import jax
import jax.numpy as jnp
from jax import lax
from jax.experimental import pallas as pl
from jax.experimental.pallas import tpu as pltpu
from jax.sharding import PartitionSpec as P

LANES = 128
PAIR = 2
COLUMNS = 4
LANES_LAST = (((1,), (1,)), ((), ()))


def split(value, parts):
    pieces = []
    for _ in range(parts):
        piece = value.astype(jnp.bfloat16)
        pieces.append(piece)
        value = value - piece.astype(jnp.float32)
    return pieces


def condition(own, left_factor, right_factor):
    layer_count, count, width = own.shape
    rows_out, rows_in = left_factor.shape[1], right_factor.shape[1]
    grid = own.astype(jnp.float32).reshape(layer_count, count, rows_out, rows_in)
    left_part = jnp.einsum("lab,lnbc->lnac", left_factor, grid, precision=lax.Precision.HIGHEST)
    both = jnp.einsum("lnac,lcd->lnad", left_part, right_factor, precision=lax.Precision.HIGHEST)
    return both.reshape(layer_count, count, width).astype(jnp.bfloat16)


def condition_block(block, left, right, put, spread, stacked, placed):
    count, width = block.shape
    inner = right.shape[0]
    pairs = width // LANES
    first_half = lax.broadcasted_iota(jnp.int32, (pairs, LANES), 1) < inner

    empty = jnp.zeros((inner, LANES), jnp.float32)
    twice = jnp.concatenate([right, right], axis=1)
    weight = jnp.concatenate(
        [jnp.concatenate([twice, empty], axis=1), jnp.concatenate([empty, twice], axis=1)], axis=0
    )
    high, middle, low = split(weight, 3)
    rows = jnp.concatenate([block[:, k * LANES : (k + 1) * LANES] for k in range(pairs)], axis=0)
    right_part = jnp.dot(
        jnp.concatenate([rows, rows], axis=1),
        jnp.concatenate([high, middle], axis=0),
        preferred_element_type=jnp.float32,
    ) + jnp.dot(rows, low, preferred_element_type=jnp.float32)
    spread[0] = right_part[:, :LANES]
    spread[1] = right_part[:, LANES:]

    for q in range(0, count, 2):
        for j in range(2):
            even = spread[j, pl.ds(q, pairs, stride=count), :]
            odd = spread[j, pl.ds(q + 1, pairs, stride=count), :]
            stacked[q // 2, pl.ds(j, pairs, stride=2), :] = jnp.where(first_half, even, odd)

    left_high, left_low = split(left, 2)
    moved = jnp.concatenate([stacked[k] for k in range(count // 2)], axis=1)
    moved_high, moved_low = split(moved, 2)
    done = jnp.dot(
        jnp.concatenate([left_high, left_high, left_low], axis=1),
        jnp.concatenate([moved_high, moved_low, moved_high], axis=0),
        preferred_element_type=jnp.float32,
    )
    for k in range(count // 2):
        stacked[k] = done[:, k * LANES : (k + 1) * LANES]

    for q in range(0, count, 2):
        upper = stacked[q // 2, pl.ds(0, pairs, stride=2), :]
        lower = stacked[q // 2, pl.ds(1, pairs, stride=2), :]
        placed[pl.ds(q, pairs, stride=count), :] = jnp.where(first_half, upper, pltpu.roll(lower, inner, 1))
        placed[pl.ds(q + 1, pairs, stride=count), :] = jnp.where(
            first_half, pltpu.roll(upper, inner, 1), lower
        )
    for k in range(pairs):
        put(k, placed[k * count : (k + 1) * count, :].astype(jnp.bfloat16))


def condition_kernel(other, queries, left, right, out, block_in, left_in, right_in, spread, stacked, placed, arrived):
    part = lax.axis_index("parts")
    layer = 1 - part if other else part
    copies = [
        pltpu.make_async_copy(source, target, arrived.at[k])
        for k, (source, target) in enumerate(
            ((queries.at[layer, 0], block_in), (right.at[layer], right_in), (left.at[layer], left_in))
        )
    ]
    for copy in copies:
        copy.start()
    for copy in copies:
        copy.wait()

    def put(k, tile):
        out[:, k * LANES : (k + 1) * LANES] = tile

    condition_block(block_in[...], left_in[...], right_in[...], put, spread, stacked, placed)


def condition_layer(other, queries, left_factor, right_factor):
    _, _, count, width = queries.shape
    pairs = width // LANES
    far = pl.BlockSpec(memory_space=pltpu.HBM)
    return pl.pallas_call(
        functools.partial(condition_kernel, other),
        out_shape=jax.ShapeDtypeStruct((count, width), jnp.bfloat16),
        in_specs=[far] * 3,
        out_specs=pl.BlockSpec(memory_space=pltpu.VMEM),
        scratch_shapes=[
            pltpu.VMEM((count, width), jnp.bfloat16),
            pltpu.VMEM(left_factor.shape[1:], jnp.float32),
            pltpu.VMEM(right_factor.shape[1:], jnp.float32),
            pltpu.VMEM((2, pairs * count, LANES), jnp.float32),
            pltpu.VMEM((count // 2, 2 * pairs, LANES), jnp.float32),
            pltpu.VMEM((pairs * count, LANES), jnp.float32),
            pltpu.SemaphoreType.DMA((3,)),
        ],
        compiler_params=pltpu.CompilerParams(vmem_limit_bytes=8 * 2**20),
        cost_estimate=pl.CostEstimate(flops=2**27, bytes_accessed=2**19, transcendentals=0),
        name="condition_other" if other else "condition_mine",
    )(*(pltpu.with_memory_space_constraint(x, pltpu.HBM) for x in (queries, left_factor, right_factor)))


def along_columns(value, flip):
    return lax.ppermute(value, "train", [(k, k ^ (flip * PAIR)) for k in range(COLUMNS * PAIR)])


def other_core(value):
    return lax.ppermute(value, "train", [(k, k ^ 1) for k in range(COLUMNS * PAIR)])


def other_part(value, cross=False):
    train = COLUMNS * PAIR
    pairs = [(part * train + k, (1 - part) * train + (k ^ cross)) for part in range(2) for k in range(train)]
    return lax.ppermute(value, ("parts", "train"), pairs)


def copy_kernel(source, target, done):
    copy = pltpu.make_async_copy(source, target, done)
    copy.start()
    copy.wait()


def copy_near(value):
    return pl.pallas_call(
        copy_kernel,
        out_shape=jax.ShapeDtypeStruct(value.shape, value.dtype),
        in_specs=[pl.BlockSpec(memory_space=pltpu.HBM)],
        out_specs=pl.BlockSpec(memory_space=pltpu.VMEM),
        scratch_shapes=[pltpu.SemaphoreType.DMA],
        compiler_params=pltpu.CompilerParams(vmem_limit_bytes=6 * 2**20),
        cost_estimate=pl.CostEstimate(flops=0, bytes_accessed=2 * value.size * 2, transcendentals=0),
        name="near",
    )(pltpu.with_memory_space_constraint(value, pltpu.HBM))


def place():
    member = lax.axis_index("train")
    return member // PAIR, lax.rem(member, PAIR)


def row_scores(train, table, owner, terms, scores):
    share = scores.shape[0]
    rows, layer_count, width = train.shape
    queries = table.shape[1]
    first = pl.multiple_of(owner * share * layer_count, share * layer_count)
    both = lax.dot_general(
        train.reshape(rows * layer_count, width)[pl.ds(first, share * layer_count), :],
        table[...].reshape(layer_count * queries, width),
        LANES_LAST,
        preferred_element_type=jnp.float32,
    )
    for layer in range(layer_count):
        terms[layer] = both[:, layer * queries : (layer + 1) * queries]
    scores[...] = sum(terms[layer, pl.ds(layer, share, stride=layer_count), :] for layer in range(layer_count))


def sent_kernel(train, *refs):
    mine, other, s1, s3, first_c, s2, y3, last_c, t2, y1, middle_c, scores, table, terms = refs
    blocks = []
    for group, swapped in (((mine, other, s1, s3), first_c), ((s2, y3), last_c), ((t2, y1), middle_c)):
        for k, block in enumerate(group):
            blocks += [block, swapped.at[k]]
    part = lax.axis_index("parts")
    column, core = place()
    count = blocks[0].shape[0]

    def put(layer, flip, other, block):
        member = (column ^ flip) * PAIR + (core ^ other)
        table[layer, pl.ds(pl.multiple_of(member * count, count), count), :] = block

    for twin in range(PAIR):
        for k, (layer, flip, cross) in enumerate(
            (
                (part, 0, 0),
                (1 - part, 0, 0),
                (part, 1, 0),
                (part, 3, 0),
                (part, 2, 0),
                (1 - part, 3, 0),
                (1 - part, 2, 0),
                (1 - part, 1, 1),
            )
        ):
            put(layer, flip, twin ^ cross, blocks[PAIR * k + twin][...])
    row_scores(train, table, 1 - lax.axis_index("layer"), terms, scores)


def kept_kernel(train, table, scores, terms):
    row_scores(train, table, lax.axis_index("layer"), terms, scores)


def local_call(kernel, name, out_shape, scratch_shapes, *operands):
    spec = pl.BlockSpec(memory_space=pltpu.VMEM)
    return pl.pallas_call(
        kernel,
        out_shape=out_shape,
        in_specs=[spec] * len(operands),
        out_specs=jax.tree.map(lambda _: spec, out_shape),
        scratch_shapes=scratch_shapes,
        compiler_params=pltpu.CompilerParams(vmem_limit_bytes=24 * 2**20),
        cost_estimate=pl.CostEstimate(flops=2**29, bytes_accessed=2**22, transcendentals=0),
        name=name,
    )(*operands)


def direct(train_grads, queries, left_factor, right_factor):
    rows, layer_count, width = train_grads.shape
    count = queries.shape[2]
    total = count * COLUMNS * PAIR
    share = rows // 2

    mine = condition_layer(False, queries, left_factor, right_factor)
    other = condition_layer(True, queries, left_factor, right_factor)
    near = copy_near(train_grads)
    s1 = along_columns(mine, 1)
    s3 = along_columns(mine, 3)
    s3, near = lax.optimization_barrier((s3, near))
    s2 = along_columns(s3, 1)
    t2 = along_columns(other, 2)
    y1 = other_part(s1, cross=True)
    y3 = other_part(s3)

    blocks = []
    for group in ((mine, other, s1, s3), (s2, y3), (t2, y1)):
        blocks += [*group, other_core(jnp.stack(group))]
    f32 = functools.partial(jax.ShapeDtypeStruct, dtype=jnp.float32)
    terms = [pltpu.VMEM((layer_count, share * layer_count, total), jnp.float32)]
    sent, table = local_call(
        sent_kernel,
        "scores_sent",
        [f32((share, total)), jax.ShapeDtypeStruct((layer_count, total, width), jnp.bfloat16)],
        terms,
        near,
        *blocks,
    )
    received = lax.ppermute(sent, "layer", [(0, 1), (1, 0)])
    kept = local_call(kept_kernel, "scores_kept", f32((share, total)), terms, near, table)
    return kept + received


def general(shape, train_grads, queries, left_factor, right_factor):
    layers = shape["layer"]
    own = condition(queries[:, 0], left_factor, right_factor)
    block = lax.all_gather(own, "train", axis=1, tiled=True)
    share = train_grads.shape[0] // layers
    here = lax.axis_index("layer")

    def terms(step):
        rows = lax.dynamic_slice_in_dim(train_grads, (here + step) % layers * share, share, 0)
        return jnp.einsum("fkm,krm->fr", rows, block, preferred_element_type=jnp.float32)

    scores = terms(0)
    for step in range(1, layers):
        scores += lax.ppermute(terms(step), "layer", [(k, (k + step) % layers) for k in range(layers)])
    return scores


def body(shape, train_grads, queries, left_factor, right_factor):
    fits = (
        shape["train"] == COLUMNS * PAIR
        and shape["parts"] == shape["layer"] == 2
        and shape["query"] == 1
        and train_grads.shape[0] == 2 * LANES
        and train_grads.shape[1:] == (2, 4096)
        and queries.shape[1:] == (1, 16, 4096)
        and left_factor.shape[1:] == right_factor.shape[1:] == (64, 64)
    )
    if fits:
        return direct(train_grads, queries, left_factor, right_factor)
    return general(shape, train_grads, queries, left_factor, right_factor)


def solution(mesh):
    return jax.shard_map(
        functools.partial(body, dict(mesh.shape)),
        mesh=mesh,
        in_specs=(
            P(("parts", "train"), "layer", None),
            P("layer", "query", "train", None),
            P("layer", None, None),
            P("layer", None, None),
        ),
        out_specs=P(("parts", "train", "layer"), "query"),
        check_vma=False,
    )
```

```python
import functools

import jax
import jax.numpy as jnp
from jax import lax
from jax.experimental import pallas as pl
from jax.experimental.pallas import tpu as pltpu
from jax.sharding import PartitionSpec as P

LANES = 128
PAIR = 2
COLUMNS = 4
LANES_LAST = (((1,), (1,)), ((), ()))


def split(value, parts):
    pieces = []
    for _ in range(parts):
        piece = value.astype(jnp.bfloat16)
        pieces.append(piece)
        value = value - piece.astype(jnp.float32)
    return pieces


def condition(own, left_factor, right_factor):
    layer_count, count, width = own.shape
    rows_out, rows_in = left_factor.shape[1], right_factor.shape[1]
    grid = own.astype(jnp.float32).reshape(layer_count, count, rows_out, rows_in)
    left_part = jnp.einsum("lab,lnbc->lnac", left_factor, grid, precision=lax.Precision.HIGHEST)
    both = jnp.einsum("lnac,lcd->lnad", left_part, right_factor, precision=lax.Precision.HIGHEST)
    return both.reshape(layer_count, count, width).astype(jnp.bfloat16)


def condition_block(block, left, right, put, spread, stacked, placed):
    count, width = block.shape
    inner = right.shape[0]
    pairs = width // LANES
    first_half = lax.broadcasted_iota(jnp.int32, (pairs, LANES), 1) < inner

    empty = jnp.zeros((inner, LANES), jnp.float32)
    twice = jnp.concatenate([right, right], axis=1)
    weight = jnp.concatenate(
        [jnp.concatenate([twice, empty], axis=1), jnp.concatenate([empty, twice], axis=1)], axis=0
    )
    high, middle, low = split(weight, 3)
    rows = jnp.concatenate([block[:, k * LANES : (k + 1) * LANES] for k in range(pairs)], axis=0)
    right_part = jnp.dot(
        jnp.concatenate([rows, rows], axis=1),
        jnp.concatenate([high, middle], axis=0),
        preferred_element_type=jnp.float32,
    ) + jnp.dot(rows, low, preferred_element_type=jnp.float32)
    spread[0] = right_part[:, :LANES]
    spread[1] = right_part[:, LANES:]

    for q in range(0, count, 2):
        for j in range(2):
            even = spread[j, pl.ds(q, pairs, stride=count), :]
            odd = spread[j, pl.ds(q + 1, pairs, stride=count), :]
            stacked[q // 2, pl.ds(j, pairs, stride=2), :] = jnp.where(first_half, even, odd)

    left_high, left_low = split(left, 2)
    moved = jnp.concatenate([stacked[k] for k in range(count // 2)], axis=1)
    moved_high, moved_low = split(moved, 2)
    done = jnp.dot(
        jnp.concatenate([left_high, left_high, left_low], axis=1),
        jnp.concatenate([moved_high, moved_low, moved_high], axis=0),
        preferred_element_type=jnp.float32,
    )
    for k in range(count // 2):
        stacked[k] = done[:, k * LANES : (k + 1) * LANES]

    for q in range(0, count, 2):
        upper = stacked[q // 2, pl.ds(0, pairs, stride=2), :]
        lower = stacked[q // 2, pl.ds(1, pairs, stride=2), :]
        placed[pl.ds(q, pairs, stride=count), :] = jnp.where(first_half, upper, pltpu.roll(lower, inner, 1))
        placed[pl.ds(q + 1, pairs, stride=count), :] = jnp.where(
            first_half, pltpu.roll(upper, inner, 1), lower
        )
    for k in range(pairs):
        put(k, placed[k * count : (k + 1) * count, :].astype(jnp.bfloat16))


def condition_kernel(other, queries, left, right, out, block_in, left_in, right_in, spread, stacked, placed, arrived):
    part = lax.axis_index("parts")
    layer = 1 - part if other else part
    copies = [
        pltpu.make_async_copy(source, target, arrived.at[k])
        for k, (source, target) in enumerate(
            ((queries.at[layer, 0], block_in), (right.at[layer], right_in), (left.at[layer], left_in))
        )
    ]
    for copy in copies:
        copy.start()
    for copy in copies:
        copy.wait()

    def put(k, tile):
        out[:, k * LANES : (k + 1) * LANES] = tile

    condition_block(block_in[...], left_in[...], right_in[...], put, spread, stacked, placed)


def condition_layer(other, queries, left_factor, right_factor):
    _, _, count, width = queries.shape
    pairs = width // LANES
    far = pl.BlockSpec(memory_space=pltpu.HBM)
    return pl.pallas_call(
        functools.partial(condition_kernel, other),
        out_shape=jax.ShapeDtypeStruct((count, width), jnp.bfloat16),
        in_specs=[far] * 3,
        out_specs=pl.BlockSpec(memory_space=pltpu.VMEM),
        scratch_shapes=[
            pltpu.VMEM((count, width), jnp.bfloat16),
            pltpu.VMEM(left_factor.shape[1:], jnp.float32),
            pltpu.VMEM(right_factor.shape[1:], jnp.float32),
            pltpu.VMEM((2, pairs * count, LANES), jnp.float32),
            pltpu.VMEM((count // 2, 2 * pairs, LANES), jnp.float32),
            pltpu.VMEM((pairs * count, LANES), jnp.float32),
            pltpu.SemaphoreType.DMA((3,)),
        ],
        compiler_params=pltpu.CompilerParams(vmem_limit_bytes=8 * 2**20),
        cost_estimate=pl.CostEstimate(flops=2**27, bytes_accessed=2**19, transcendentals=0),
        name="condition_other" if other else "condition_mine",
    )(*(pltpu.with_memory_space_constraint(x, pltpu.HBM) for x in (queries, left_factor, right_factor)))


def along_columns(value, flip):
    return lax.ppermute(value, "train", [(k, k ^ (flip * PAIR)) for k in range(COLUMNS * PAIR)])


def other_core(value):
    return lax.ppermute(value, "train", [(k, k ^ 1) for k in range(COLUMNS * PAIR)])


def other_part(value, cross=False):
    train = COLUMNS * PAIR
    pairs = [(part * train + k, (1 - part) * train + (k ^ cross)) for part in range(2) for k in range(train)]
    return lax.ppermute(value, ("parts", "train"), pairs)


def copy_kernel(source, target, done):
    copy = pltpu.make_async_copy(source, target, done)
    copy.start()
    copy.wait()


def copy_near(value):
    return pl.pallas_call(
        copy_kernel,
        out_shape=jax.ShapeDtypeStruct(value.shape, value.dtype),
        in_specs=[pl.BlockSpec(memory_space=pltpu.HBM)],
        out_specs=pl.BlockSpec(memory_space=pltpu.VMEM),
        scratch_shapes=[pltpu.SemaphoreType.DMA],
        compiler_params=pltpu.CompilerParams(vmem_limit_bytes=6 * 2**20),
        cost_estimate=pl.CostEstimate(flops=0, bytes_accessed=2 * value.size * 2, transcendentals=0),
        name="near",
    )(pltpu.with_memory_space_constraint(value, pltpu.HBM))


def place():
    member = lax.axis_index("train")
    return member // PAIR, lax.rem(member, PAIR)


def row_scores(train, table, owner, terms, scores):
    share = scores.shape[0]
    rows, layer_count, width = train.shape
    queries = table.shape[1]
    first = pl.multiple_of(owner * share * layer_count, share * layer_count)
    both = lax.dot_general(
        train.reshape(rows * layer_count, width)[pl.ds(first, share * layer_count), :],
        table[...].reshape(layer_count * queries, width),
        LANES_LAST,
        preferred_element_type=jnp.float32,
    )
    for layer in range(layer_count):
        terms[layer] = both[:, layer * queries : (layer + 1) * queries]
    scores[...] = sum(terms[layer, pl.ds(layer, share, stride=layer_count), :] for layer in range(layer_count))


def sent_kernel(train, *refs):
    mine, other, s1, s3, first_c, s2, y1, last_c, t2, y3, middle_c, scores, table, terms = refs
    blocks = []
    for group, swapped in (((mine, other, s1, s3), first_c), ((s2, y1), last_c), ((t2, y3), middle_c)):
        for k, block in enumerate(group):
            blocks += [block, swapped.at[k]]
    part = lax.axis_index("parts")
    column, core = place()
    count = blocks[0].shape[0]

    def put(layer, flip, other, block):
        member = (column ^ flip) * PAIR + (core ^ other)
        table[layer, pl.ds(pl.multiple_of(member * count, count), count), :] = block

    for twin in range(PAIR):
        for k, (layer, flip, cross) in enumerate(
            (
                (part, 0, 0),
                (1 - part, 0, 0),
                (part, 1, 0),
                (part, 3, 0),
                (part, 2, 0),
                (1 - part, 1, 1),
                (1 - part, 2, 0),
                (1 - part, 3, 0),
            )
        ):
            put(layer, flip, twin ^ cross, blocks[PAIR * k + twin][...])
    row_scores(train, table, 1 - lax.axis_index("layer"), terms, scores)


def kept_kernel(train, table, scores, terms):
    row_scores(train, table, lax.axis_index("layer"), terms, scores)


def local_call(kernel, name, out_shape, scratch_shapes, *operands):
    spec = pl.BlockSpec(memory_space=pltpu.VMEM)
    return pl.pallas_call(
        kernel,
        out_shape=out_shape,
        in_specs=[spec] * len(operands),
        out_specs=jax.tree.map(lambda _: spec, out_shape),
        scratch_shapes=scratch_shapes,
        compiler_params=pltpu.CompilerParams(vmem_limit_bytes=24 * 2**20),
        cost_estimate=pl.CostEstimate(flops=2**29, bytes_accessed=2**22, transcendentals=0),
        name=name,
    )(*operands)


def direct(train_grads, queries, left_factor, right_factor):
    rows, layer_count, width = train_grads.shape
    count = queries.shape[2]
    total = count * COLUMNS * PAIR
    share = rows // 2

    mine = condition_layer(False, queries, left_factor, right_factor)
    other = condition_layer(True, queries, left_factor, right_factor)
    near = copy_near(train_grads)
    s1 = along_columns(mine, 1)
    s3 = along_columns(mine, 3)
    s3, near = lax.optimization_barrier((s3, near))
    s2 = along_columns(s3, 1)
    t2 = along_columns(other, 2)
    y1 = other_part(s1, cross=True)
    y3 = other_part(s3)

    blocks = []
    for group in ((mine, other, s1, s3), (s2, y1), (t2, y3)):
        blocks += [*group, other_core(jnp.stack(group))]
    f32 = functools.partial(jax.ShapeDtypeStruct, dtype=jnp.float32)
    terms = [pltpu.VMEM((layer_count, share * layer_count, total), jnp.float32)]
    sent, table = local_call(
        sent_kernel,
        "scores_sent",
        [f32((share, total)), jax.ShapeDtypeStruct((layer_count, total, width), jnp.bfloat16)],
        terms,
        near,
        *blocks,
    )
    received = lax.ppermute(sent, "layer", [(0, 1), (1, 0)])
    kept = local_call(kept_kernel, "scores_kept", f32((share, total)), terms, near, table)
    return kept + received


def general(shape, train_grads, queries, left_factor, right_factor):
    layers = shape["layer"]
    own = condition(queries[:, 0], left_factor, right_factor)
    block = lax.all_gather(own, "train", axis=1, tiled=True)
    share = train_grads.shape[0] // layers
    here = lax.axis_index("layer")

    def terms(step):
        rows = lax.dynamic_slice_in_dim(train_grads, (here + step) % layers * share, share, 0)
        return jnp.einsum("fkm,krm->fr", rows, block, preferred_element_type=jnp.float32)

    scores = terms(0)
    for step in range(1, layers):
        scores += lax.ppermute(terms(step), "layer", [(k, (k + step) % layers) for k in range(layers)])
    return scores


def body(shape, train_grads, queries, left_factor, right_factor):
    fits = (
        shape["train"] == COLUMNS * PAIR
        and shape["parts"] == shape["layer"] == 2
        and shape["query"] == 1
        and train_grads.shape[0] == 2 * LANES
        and train_grads.shape[1:] == (2, 4096)
        and queries.shape[1:] == (1, 16, 4096)
        and left_factor.shape[1:] == right_factor.shape[1:] == (64, 64)
    )
    if fits:
        return direct(train_grads, queries, left_factor, right_factor)
    return general(shape, train_grads, queries, left_factor, right_factor)


def solution(mesh):
    return jax.shard_map(
        functools.partial(body, dict(mesh.shape)),
        mesh=mesh,
        in_specs=(
            P(("parts", "train"), "layer", None),
            P("layer", "query", "train", None),
            P("layer", None, None),
            P("layer", None, None),
        ),
        out_specs=P(("parts", "train", "layer"), "query"),
        check_vma=False,
    )
```
